32 devices in a mesh: space: 16 (over z, y, x), mp: 2 (over core).
Axes of the slice: x: 2, y: 2, z: 4, core: 2. Of those that a mesh axis runs over, the one named last changes fastest.
Arguments:
- points: bfloat16 [32768, 512], P('space'), may hold values from -40 to 40
- curve_rank: int32 [32768], P('space'), may hold values from 0 to 32767, as said below
- patch_counts: int32 [16, 4], P('space'), may hold values from 1 to 1024, 2048 in all within a row
- norm_gain_attn: float32 [512], replicated, may hold values from 0.1 to 1.9
- w_qkv: bfloat16 [3, 512, 512], P(None, None, 'mp'), may hold values from -1.5 to 1.5
- w_out: bfloat16 [512, 512], P('mp'), may hold values from -0.75 to 0.75
- norm_gain_mlp: float32 [512], replicated, may hold values from 0.1 to 1.9
- w_fc1: bfloat16 [512, 2048], P(None, 'mp'), may hold values from -0.25 to 0.25
- w_fc2: bfloat16 [2048, 512], P('mp'), may hold values from -0.1875 to 0.1875
Outputs:
- layer_out: bfloat16 [32768, 512], P('space')
The draws below stay inside these ranges and needn't reach their ends.
Inputs may be any that keep to these rules, and one draw needn't show every extreme that they name: curve_rank is a permutation; the points of shard a take exactly the positions b * 2048 + a * 128 + m for every owner b and every m below 128. `patch_counts`: each row sums to 2048.
All inputs are finite; a program needn't handle non-finite values.
Results may differ from the reference program's by a relative error of at most 0.0075.
Values may be sent and summed in bfloat16 or wider, within the bound.
No kernel may reach another device: no remote copies, remote signals or barrier semaphores. Data moves between devices by JAX's collectives and lax.ppermute only.
A program may use at most 128 MiB of HBM per device.

```python
import math
import jax
import jax.numpy as jnp
import numpy as np
from jax import lax

D = 512
FF = 2048
PATCH = 1024
P_DEV = 2048
HDIM = 64
TILES = 4
SHARDS = 16
CELL = 128
NPTS = 32768


def draw_points(key, part):
    subkeys = jax.random.split(jax.random.fold_in(key, 11), 4)
    normal_part = jax.random.normal(subkeys[0], (NPTS, D), jnp.float32)
    row_scale = jnp.exp(jax.random.uniform(subkeys[1], (NPTS, 1), jnp.float32, math.log(0.5), math.log(2.0)))
    column_scale = jnp.exp(jax.random.uniform(subkeys[2], (1, D), jnp.float32, math.log(0.4), math.log(4.0)))
    offset = 0.5 * jax.random.normal(subkeys[3], (NPTS, 1), jnp.float32)
    values = (normal_part * column_scale + offset) * row_scale
    return jnp.clip(values, -40.0, 40.0).astype(jnp.bfloat16)


def draw_w_qkv(key, part):
    subkeys = jax.random.split(jax.random.fold_in(key, 23), 1)
    normal_part = jax.random.normal(subkeys[0], (3, D, D), jnp.float32) / math.sqrt(D)
    factor = jnp.array([1.4142, 1.4142, 1.0], jnp.float32)[:, None, None]
    weights = normal_part * factor
    return jnp.clip(weights, -1.5, 1.5).astype(jnp.bfloat16)


def draw_curve_rank(key, part):
    subkeys = jax.random.split(jax.random.fold_in(key, 5), SHARDS)

    def per_shard(shard_key):
        return jax.random.permutation(shard_key, P_DEV)
    local_slot = jax.vmap(per_shard)(subkeys).astype(jnp.int32)
    device = jnp.arange(SHARDS, dtype=jnp.int32)[:, None]
    positions = local_slot // CELL * P_DEV + device * CELL + local_slot % CELL
    return positions.reshape(NPTS).astype(jnp.int32)


def level_of(rng, dims, cuts, low, largest):
    level, own = 1.0, jax.random.fold_in(rng, 6)
    for axis_at, blocks in cuts:
        heights = jnp.exp(jax.random.uniform(jax.random.fold_in(own, axis_at), (blocks,), jnp.float32, low / len(cuts), largest / len(cuts)))
        level = level * jnp.repeat(heights, dims[axis_at] // blocks).reshape([-1 if axis == axis_at else 1 for axis in range(len(dims))])
    return level


def length_profile(amount, total, limit, lean):
    weights = [(1 << 20) // math.isqrt(rank ** lean) + 1 for rank in range(2, amount + 1)]
    spare, holding = total - limit - (amount - 1), [1] * (amount - 1)
    while spare > 0:
        free = [i for i in range(amount - 1) if holding[i] < limit]
        pool, budget = sum([weights[i] for i in free]), spare
        for i in free:
            more = min(limit - holding[i], max(1, budget * weights[i] // pool), spare)
            holding[i] = holding[i] + more
            spare = spare - more
    return np.array([limit] + holding)


def uneven(stream_key, amount, total, reach, skew):
    if amount == 2:
        one = jax.random.randint(stream_key, (), max(1, total - reach), min(reach, total - 1) + 1)
        return jnp.stack([one, total - one])
    lengths = jnp.asarray(length_profile(amount, total, reach, skew), jnp.int32)
    couples = (amount - 1) // 2
    donor, taker = lengths[1:1 + 2 * couples:2], lengths[2:2 + 2 * couples:2]
    slack = jnp.minimum(donor - 1, reach - taker)
    moved = jax.random.randint(jax.random.fold_in(stream_key, 1), (couples,), 0, 1 << 20) % (slack + 1)
    lengths = lengths.at[1:1 + 2 * couples:2].set(donor - moved).at[2:2 + 2 * couples:2].set(taker + moved)
    return lengths[jax.random.permutation(jax.random.fold_in(stream_key, 2), amount)]


def bell_draw(key, shape, deviation, most, cuts=(), kind=jnp.bfloat16):
    level = level_of(key, shape, cuts, -0.22, 0.18) if cuts else 1.0
    values = jax.random.normal(key, shape, jnp.float32) * deviation * level
    return jnp.minimum(jnp.maximum(values, -most), most).astype(kind)


def setup_inputs(seed: int = 0) -> dict:
    keys = jax.random.split(jax.random.key(seed), 10)
    return {
        "points": draw_points(jax.random.fold_in(keys[9], 71), 0),
        "curve_rank": draw_curve_rank(jax.random.fold_in(keys[9], 71), 0),
        "patch_counts": jax.vmap(lambda own: uneven(own, TILES, P_DEV, PATCH, 2))(jax.random.split(keys[2], SHARDS)).reshape((SHARDS, TILES)).astype(jnp.int32),
        "norm_gain_attn": jnp.clip(1.0 + 0.18 * jax.random.normal(keys[3], (D,), jnp.float32), 0.1, 1.9),
        "w_qkv": draw_w_qkv(jax.random.fold_in(keys[9], 71), 0),
        "w_out": bell_draw(keys[5], (D, D), (D // 8) ** -0.5, 0.75, ((0, 2),)),
        "norm_gain_mlp": jnp.clip(1.0 + 0.18 * jax.random.normal(keys[6], (D,), jnp.float32), 0.1, 1.9),
        "w_fc1": bell_draw(keys[7], (D, FF), D ** -0.5, 0.25, ((1, 2),)),
        "w_fc2": bell_draw(keys[8], (FF, D), (FF // 2) ** -0.5, 0.1875, ((0, 2),)),
    }


epsilon = 1e-06

def layer_norm(inputs, gain_row):
    values = inputs.astype(jnp.float32)
    average = lax.optimization_barrier(jnp.mean(values, axis=-1, keepdims=True))
    centred = values - average
    second = lax.optimization_barrier(jnp.mean(centred * centred, axis=-1, keepdims=True))
    return (centred * lax.rsqrt(second + epsilon) * gain_row).astype(jnp.bfloat16)

def tile_layout(counts, tile_width):
    starts = (jnp.cumsum(counts) - counts).astype(jnp.int32)
    offsets = jnp.arange(tile_width, dtype=jnp.int32)
    usable = offsets[None, :] < counts[:, None]
    source = jnp.where(usable, starts[:, None] + offsets[None, :], 0).astype(jnp.int32)
    return (starts, source, usable)

def back_index(starts, length, tile_width):
    places = jnp.arange(length, dtype=jnp.int32)
    covered = starts[None, :] <= places[:, None]
    owning = lax.optimization_barrier(jnp.sum(covered.astype(jnp.int32), axis=1)) - 1
    start_of = lax.optimization_barrier(jnp.max(jnp.where(covered, starts[None, :], 0), axis=1))
    return (owning * tile_width + places - start_of).astype(jnp.int32)

def attend(queries, key_rows, value_rows, counts):
    length, columns = queries.shape
    head_count = columns // HDIM
    score_scale = 1.0 / math.sqrt(HDIM)
    starts, source, usable = tile_layout(counts, PATCH)

    def one_tile(packed):
        picked, allowed = packed
        tile_q = queries[picked].reshape(PATCH, head_count, HDIM).astype(jnp.float32)
        tile_k = key_rows[picked].reshape(PATCH, head_count, HDIM).astype(jnp.float32)
        tile_v = value_rows[picked].reshape(PATCH, head_count, HDIM).astype(jnp.float32)
        scores = jnp.einsum('qhd,khd->hqk', tile_q, tile_k) * score_scale
        scores = jnp.where(allowed[None, None, :], scores, -jnp.inf)
        highest = lax.optimization_barrier(jnp.max(scores, axis=2, keepdims=True))
        raised = jnp.exp(scores - highest)
        weights = (raised / lax.optimization_barrier(jnp.sum(raised, axis=2, keepdims=True))).astype(jnp.bfloat16)
        context = jnp.einsum('hqk,khd->qhd', weights.astype(jnp.float32), tile_v)
        return context.astype(jnp.bfloat16).reshape(PATCH, columns)
    tile_out = lax.map(one_tile, (source, usable))
    places = back_index(starts, length, PATCH)
    return tile_out.reshape(-1, columns)[places]

def reference(points, curve_rank, patch_counts, norm_gain_attn, w_qkv, w_out, norm_gain_mlp, w_fc1, w_fc2):
    normed = layer_norm(points, norm_gain_attn)
    ordered = jnp.zeros_like(normed).at[curve_rank].set(normed)
    owner_blocks = ordered.reshape(SHARDS, P_DEV, D)

    def owner_step(packed):
        owner_rows, counts = packed
        queries = jnp.dot(owner_rows, w_qkv[0], preferred_element_type=jnp.float32).astype(jnp.bfloat16)
        key_rows = jnp.dot(owner_rows, w_qkv[1], preferred_element_type=jnp.float32).astype(jnp.bfloat16)
        value_rows = jnp.dot(owner_rows, w_qkv[2], preferred_element_type=jnp.float32).astype(jnp.bfloat16)
        return attend(queries, key_rows, value_rows, counts)
    context = lax.map(owner_step, (owner_blocks, patch_counts)).reshape(NPTS, D)
    gathered = context[curve_rank]

    def finish(packed):
        rows_ctx, rows_in = packed
        attn_out = jnp.dot(rows_ctx, w_out, preferred_element_type=jnp.float32).astype(jnp.bfloat16)
        middle = (rows_in.astype(jnp.float32) + attn_out.astype(jnp.float32)).astype(jnp.bfloat16)
        normed_mlp = layer_norm(middle, norm_gain_mlp)
        hidden = jax.nn.gelu(jnp.dot(normed_mlp, w_fc1, preferred_element_type=jnp.float32), approximate=True).astype(jnp.bfloat16)
        return (middle.astype(jnp.float32) + jnp.dot(hidden, w_fc2, preferred_element_type=jnp.float32)).astype(jnp.bfloat16)
    finished = lax.map(finish, (gathered.reshape(SHARDS, P_DEV, D), points.reshape(SHARDS, P_DEV, D)))
    return finished.reshape(NPTS, D)
```

```python
import functools
import math

import jax
import jax.numpy as jnp
from jax import lax
from jax.experimental import pallas as pl
from jax.experimental.pallas import tpu as pltpu
from jax.sharding import PartitionSpec as P

HDIM = 64
LANES = 128
ROWS = 256
EPSILON = 1e-06
FAR = 1e30
VMEM_BYTES = 50 * 1024 * 1024

f32 = jnp.float32
bf16 = jnp.bfloat16


def normalise(values, gain_row):
    average = jnp.mean(values, axis=-1, keepdims=True)
    centred = values - average
    second = jnp.mean(centred * centred, axis=-1, keepdims=True)
    return (centred * lax.rsqrt(second + EPSILON) * gain_row).astype(bf16)


def dot(left, right):
    return jnp.dot(left, right, preferred_element_type=f32)


def split_rank(rank, length):
    if length & (length - 1) == 0:
        return rank >> (length.bit_length() - 1), rank & (length - 1)
    return rank // length, rank % length


def slots(rank, length, shards):
    cell = length // shards
    owner, within = split_rank(rank, length)
    return owner * cell + within - lax.axis_index("space") * cell


def send_kernel(shards, rank_ref, gain_ref, points_ref, out_ref, half_ref):
    length, features = points_ref.shape
    half = features // 2
    core = lax.axis_index("mp")

    def norm_block(i, carry):
        rows = pl.ds(pl.multiple_of(i * ROWS, ROWS), ROWS)
        normed = normalise(points_ref[rows, :].astype(f32), gain_ref[...])
        half_ref[rows, :] = jnp.where(core == 0, normed[:, :half], normed[:, half:])
        return carry

    lax.fori_loop(0, length // ROWS, norm_block, 0)
    slot = slots(rank_ref[...], length, shards)

    def order_block(i, carry):
        start = pl.multiple_of(i * ROWS, ROWS)
        place = lax.broadcasted_iota(jnp.int32, (ROWS, length), 0) + start
        pick = (place == slot).astype(f32).astype(bf16)
        out_ref[pl.ds(start, ROWS), :] = dot(pick, half_ref[...]).astype(bf16)
        return carry

    lax.fori_loop(0, length // ROWS, order_block, 0)


def order_for_owners(points, rank_row, gain_row, shards):
    length, features = points.shape
    return pl.pallas_call(
        functools.partial(send_kernel, shards),
        out_shape=jax.ShapeDtypeStruct((length, features // 2), bf16),
        scratch_shapes=[pltpu.VMEM((length, features // 2), bf16)],
        compiler_params=pltpu.CompilerParams(vmem_limit_bytes=VMEM_BYTES),
        cost_estimate=pl.CostEstimate(
            flops=length * length * features, bytes_accessed=4 * length * features, transcendentals=0
        ),
    )(rank_row, gain_row, points)


def attend_kernel(counts_ref, own_ref, other_ref, weight_ref, out_ref, q_ref, k_ref, v_ref):
    length, half = own_ref.shape
    tiles = counts_ref.shape[1]
    heads = q_ref.shape[0]
    core = lax.axis_index("mp")
    own_rows = pl.ds(pl.multiple_of(core * half, half), half)
    other_rows = pl.ds(pl.multiple_of((1 - core) * half, half), half)
    scale = math.log2(math.e) / math.sqrt(HDIM)

    starts = [jnp.int32(0)]
    for t in range(tiles):
        starts.append(starts[-1] + counts_ref[0, t])
    lane = lax.broadcasted_iota(jnp.int32, (1, LANES), 1)
    first = jnp.full((1, LANES), length, jnp.int32)
    last = jnp.zeros((1, LANES), jnp.int32)
    for t in range(tiles):
        first = jnp.where(lane == HDIM + t, starts[t], first)
        last = jnp.where(lane == HDIM + t, starts[t + 1], last)
    flags = jnp.logical_and(lane >= HDIM, lane < HDIM + tiles)

    def project(i, carry):
        rows = pl.ds(pl.multiple_of(i * ROWS, ROWS), ROWS)
        mine, theirs = own_ref[rows, :], other_ref[rows, :]
        place = lax.broadcasted_iota(jnp.int32, (ROWS, LANES), 0) + i * ROWS
        inside = jnp.logical_and(place >= first, place < last)
        q_flag = jnp.where(inside, 1.0, 0.0)
        k_flag = jnp.where(jnp.logical_and(flags, jnp.logical_not(inside)), -FAR, 0.0)
        spread = [
            dot(mine, weight_ref[j, own_rows, :]) + dot(theirs, weight_ref[j, other_rows, :])
            for j in range(3)
        ]
        for h in range(heads):
            cols = slice(h * LANES, (h + 1) * LANES)
            q_ref[h, rows, :] = (spread[0][:, cols] * scale + q_flag).astype(bf16)
            k_ref[h, rows, :] = (spread[1][:, cols] + k_flag).astype(bf16)
            ones = (lane >= HDIM) if h % 2 == 0 else (lane < HDIM)
            v_ref[h, rows, :] = (spread[2][:, cols] + jnp.where(ones, 1.0, 0.0)).astype(bf16)
        return carry

    lax.fori_loop(0, length // ROWS, project, 0)

    def one_head(h, rows, keys):
        scores = lax.dot_general(
            q_ref[h, rows, :], k_ref[h, keys, :], (((1,), (1,)), ((), ())), preferred_element_type=f32
        )
        raised = jnp.exp2(scores - jnp.max(scores, axis=1, keepdims=True)).astype(bf16)
        return dot(raised, v_ref[h, keys, :])

    def query_block(i, carry):
        begin = i * ROWS
        rows = pl.ds(pl.multiple_of(begin, ROWS), ROWS)
        low, high = jnp.int32(0), jnp.int32(length)
        for t in range(tiles):
            low = jnp.where(starts[t] <= begin, starts[t], low)
            end = starts[tiles - t]
            high = jnp.where(end >= begin + ROWS, end, high)
        low = (low // 16) * 16
        blocks = (high - low + ROWS - 1) // ROWS
        for n in range(1, length // ROWS + 1):

            @pl.when(blocks == n)
            def _(n=n):
                start = jnp.minimum(low, length - n * ROWS)
                keys = pl.ds(pl.multiple_of(start, 16), n * ROWS)
                for pair in range(heads // 2):
                    even = one_head(2 * pair, rows, keys)
                    odd = one_head(2 * pair + 1, rows, keys)
                    total = pltpu.roll(jnp.where(lane < HDIM, odd, even), HDIM, 1)
                    value = jnp.where(lane < HDIM, even, odd) / total
                    out_ref[rows, pair * LANES : (pair + 1) * LANES] = value.astype(bf16)

        return carry

    lax.fori_loop(0, length // ROWS, query_block, 0)


def attend(counts, own, other, weights):
    length, half = own.shape
    heads = weights.shape[2] // LANES
    whole = pl.BlockSpec(memory_space=pltpu.VMEM)
    return pl.pallas_call(
        attend_kernel,
        out_shape=jax.ShapeDtypeStruct((length, heads * HDIM), bf16),
        in_specs=[pl.BlockSpec(memory_space=pltpu.SMEM), whole, whole, whole],
        out_specs=whole,
        scratch_shapes=[pltpu.VMEM((heads, length, LANES), bf16)] * 3,
        compiler_params=pltpu.CompilerParams(vmem_limit_bytes=VMEM_BYTES),
        cost_estimate=pl.CostEstimate(
            flops=16 * length * length * HDIM * heads,
            bytes_accessed=8 * length * half,
            transcendentals=length * length * heads,
        ),
    )(counts, own, other, weights)


def finish_kernel(
    shards,
    rank_ref,
    gain_ref,
    points_ref,
    ret_own_ref,
    ret_other_ref,
    out_own_ref,
    out_other_ref,
    fc1_own_ref,
    fc1_other_ref,
    fc2_own_ref,
    fc2_other_ref,
    done_ref,
):
    length = points_ref.shape[0]
    half_rows = done_ref.shape[0]
    base = lax.axis_index("mp") * half_rows

    def block(i, carry):
        start = pl.multiple_of(base + i * ROWS, ROWS)
        rank = rank_ref[:, pl.ds(start, ROWS)]
        slot = slots(rank, length, shards)
        slot = jnp.transpose(jnp.broadcast_to(slot, (LANES, ROWS)))
        place = lax.broadcasted_iota(jnp.int32, (ROWS, LANES), 1)
        pick = jnp.concatenate(
            [
                (slot == place + k * LANES).astype(f32).astype(bf16)
                for k in range(length // LANES)
            ],
            axis=1,
        )
        mine = dot(pick, ret_own_ref[...]).astype(bf16)
        theirs = dot(pick, ret_other_ref[...]).astype(bf16)
        attn_out = (dot(mine, out_own_ref[...]) + dot(theirs, out_other_ref[...])).astype(bf16)
        middle = points_ref[pl.ds(start, ROWS), :].astype(f32) + attn_out.astype(f32)
        middle = middle.astype(bf16).astype(f32)
        normed = normalise(middle, gain_ref[...])
        total = middle
        for fc1_ref, fc2_ref in ((fc1_own_ref, fc2_own_ref), (fc1_other_ref, fc2_other_ref)):
            hidden = jax.nn.gelu(dot(normed, fc1_ref[...]), approximate=True).astype(bf16)
            total = total + dot(hidden, fc2_ref[...])
        done_ref[pl.ds(pl.multiple_of(i * ROWS, ROWS), ROWS), :] = total.astype(bf16)
        return carry

    lax.fori_loop(0, half_rows // ROWS, block, 0)


def finish(shards, rank_row, gain_row, points, *arrays):
    length, features = points.shape
    half_rows = length // 2
    return pl.pallas_call(
        functools.partial(finish_kernel, shards),
        out_shape=jax.ShapeDtypeStruct((half_rows, features), bf16),
        compiler_params=pltpu.CompilerParams(vmem_limit_bytes=VMEM_BYTES),
        cost_estimate=pl.CostEstimate(
            flops=2 * half_rows * features * (length + 9 * features),
            bytes_accessed=16 * length * features,
            transcendentals=half_rows * 4 * features,
        ),
    )(rank_row, gain_row, points, *arrays)


def join_kernel(own_ref, other_ref, out_ref, sems):
    half_rows = own_ref.shape[0]
    core = lax.axis_index("mp")
    copies = [
        pltpu.make_async_copy(ref, out_ref.at[pl.ds(pl.multiple_of(at * half_rows, half_rows), half_rows)], sems.at[k])
        for k, (ref, at) in enumerate(((own_ref, core), (other_ref, 1 - core)))
    ]
    for copy in copies:
        copy.start()
    for copy in copies:
        copy.wait()


def join(own, other):
    half_rows, features = own.shape
    anywhere = pl.BlockSpec(memory_space=pl.ANY)
    return pl.pallas_call(
        join_kernel,
        out_shape=jax.ShapeDtypeStruct((2 * half_rows, features), own.dtype),
        in_specs=[anywhere, anywhere],
        out_specs=anywhere,
        scratch_shapes=[pltpu.SemaphoreType.DMA((2,))],
    )(own, other)


def across(values):
    return lax.ppermute(values, "mp", [(0, 1), (1, 0)])


def exchange(rows, shards):
    length, columns = rows.shape
    cells = rows.reshape(shards, length // shards, columns)
    return lax.all_to_all(cells, "space", split_axis=0, concat_axis=0, tiled=True).reshape(length, columns)


def spread_heads(w_qkv):
    three, features, columns = w_qkv.shape
    heads = columns // HDIM
    split = w_qkv.reshape(three, features, heads // 2, 2, HDIM)
    empty = jnp.zeros_like(split[:, :, :, 0])
    low = jnp.concatenate([split[:, :, :, 0], empty, split[:, :, :, 1], empty], axis=-1)
    mixed = jnp.concatenate([split[:, :, :, 0], empty, empty, split[:, :, :, 1]], axis=-1)
    spread = jnp.concatenate([low[:2], mixed[2:]], axis=0)
    return spread.reshape(three, features, heads * LANES)


def body(points, curve_rank, patch_counts, norm_gain_attn, w_qkv, w_out, norm_gain_mlp, w_fc1, w_fc2):
    shards = lax.axis_size("space")
    length, features = points.shape
    rank_row = curve_rank.reshape(1, length)
    send = order_for_owners(points, rank_row, norm_gain_attn.reshape(1, features), shards)
    own = exchange(send, shards)
    weights = spread_heads(w_qkv)
    other_fc1, other_fc2, other_out = across(w_fc1), across(w_fc2), across(w_out)
    other = across(own)
    context = attend(patch_counts, own, other, weights)
    ret_own = exchange(context, shards)
    ret_other = across(ret_own)
    done = finish(
        shards,
        rank_row,
        norm_gain_mlp.reshape(1, features),
        points,
        ret_own,
        ret_other,
        w_out,
        other_out,
        w_fc1,
        other_fc1,
        w_fc2,
        other_fc2,
    )
    return join(done, across(done))


def solution(mesh):
    placed = (
        P("space", None),
        P("space"),
        P("space", None),
        P(),
        P(None, None, "mp"),
        P("mp", None),
        P(),
        P(None, "mp"),
        P("mp", None),
    )
    return jax.shard_map(
        body, mesh=mesh, in_specs=placed, out_specs=P("space", None), check_vma=False
    )
```

```python
import functools
import math

import jax
import jax.numpy as jnp
from jax import lax
from jax.experimental import pallas as pl
from jax.experimental.pallas import tpu as pltpu
from jax.sharding import PartitionSpec as P

HDIM = 64
LANES = 128
ROWS = 256
EPSILON = 1e-06
FAR = 1e30
SEND_BYTES = 58 * 1024 * 1024
VMEM_BYTES = 30 * 1024 * 1024

f32 = jnp.float32
bf16 = jnp.bfloat16


def normalise(values, gain_row):
    average = jnp.mean(values, axis=-1, keepdims=True)
    centred = values - average
    second = jnp.mean(centred * centred, axis=-1, keepdims=True)
    return (centred * lax.rsqrt(second + EPSILON) * gain_row).astype(bf16)


def dot(left, right):
    return jnp.dot(left, right, preferred_element_type=f32)


def split_rank(rank, length):
    if length & (length - 1) == 0:
        return rank >> (length.bit_length() - 1), rank & (length - 1)
    return rank // length, rank % length


def slots(rank, length, shards):
    cell = length // shards
    owner, within = split_rank(rank, length)
    return owner * cell + within - lax.axis_index("space") * cell


def send_kernel(shards, rank_hbm, gain_hbm, points_hbm, out_ref, rank_ref, gain_ref, points_ref, half_ref, small, large):
    length, features = points_ref.shape
    half = features // 2
    core = lax.axis_index("mp")
    blocks = length // ROWS
    rows_of = [slice(i * ROWS, (i + 1) * ROWS) for i in range(blocks)]
    gain_copy = pltpu.make_async_copy(gain_hbm, gain_ref, small.at[0])
    rank_copy = pltpu.make_async_copy(rank_hbm, rank_ref, small.at[1])
    copies = [
        pltpu.make_async_copy(points_hbm.at[rows], points_ref.at[rows], large.at[i])
        for i, rows in enumerate(rows_of)
    ]
    gain_copy.start()
    for copy in copies:
        copy.start()
    rank_copy.start()
    gain_copy.wait()
    for copy, rows in zip(copies, rows_of):
        copy.wait()
        normed = normalise(points_ref[rows, :].astype(f32), gain_ref[...])
        half_ref[rows, :] = jnp.where(core == 0, normed[:, :half], normed[:, half:])
    rank_copy.wait()
    slot = slots(rank_ref[...], length, shards)

    def order_block(i, carry):
        start = pl.multiple_of(i * ROWS, ROWS)
        place = lax.broadcasted_iota(jnp.int32, (ROWS, length), 0) + start
        pick = (place == slot).astype(f32).astype(bf16)
        out_ref[pl.ds(start, ROWS), :] = dot(pick, half_ref[...]).astype(bf16)
        return carry

    lax.fori_loop(0, blocks, order_block, 0)


def order_for_owners(points, rank_row, gain_row, shards):
    length, features = points.shape
    anywhere = pl.BlockSpec(memory_space=pl.ANY)
    return pl.pallas_call(
        functools.partial(send_kernel, shards),
        out_shape=jax.ShapeDtypeStruct((length, features // 2), bf16),
        in_specs=[anywhere] * 3,
        out_specs=pl.BlockSpec(memory_space=pltpu.VMEM),
        scratch_shapes=[
            pltpu.VMEM((1, length), jnp.int32),
            pltpu.VMEM((1, features), f32),
            pltpu.VMEM((length, features), bf16),
            pltpu.VMEM((length, features // 2), bf16),
            pltpu.SemaphoreType.DMA((2,)),
            pltpu.SemaphoreType.DMA((length // ROWS,)),
        ],
        compiler_params=pltpu.CompilerParams(vmem_limit_bytes=SEND_BYTES),
        cost_estimate=pl.CostEstimate(
            flops=length * length * features, bytes_accessed=4 * length * features, transcendentals=0
        ),
    )(rank_row, gain_row, points)


def attend_kernel(pair, counts_ref, own_ref, other_ref, weight_ref, out_ref, w_ref, q_ref, k_ref, v_ref):
    length, half = own_ref.shape
    tiles = counts_ref.shape[1]
    core = lax.axis_index("mp")
    own_rows = pl.ds(pl.multiple_of(core * half, half), half)
    other_rows = pl.ds(pl.multiple_of((1 - core) * half, half), half)
    scale = math.log2(math.e) / math.sqrt(HDIM)

    starts = [jnp.int32(0)]
    for t in range(tiles):
        starts.append(starts[-1] + counts_ref[0, t])
    lane = lax.broadcasted_iota(jnp.int32, (1, LANES), 1)
    first = jnp.full((1, LANES), length, jnp.int32)
    last = jnp.zeros((1, LANES), jnp.int32)
    for t in range(tiles):
        first = jnp.where(lane == HDIM + t, starts[t], first)
        last = jnp.where(lane == HDIM + t, starts[t + 1], last)
    flags = jnp.logical_and(lane >= HDIM, lane < HDIM + tiles)
    low_lanes = lane < HDIM

    for j in range(3):
        both = weight_ref[j, :, pair * LANES : (pair + 1) * LANES].astype(f32)
        w_ref[j, :, :LANES] = jnp.where(low_lanes, both, 0.0).astype(bf16)
        odd = jnp.where(low_lanes, pltpu.roll(both, HDIM, 1), 0.0) if j < 2 else jnp.where(low_lanes, 0.0, both)
        w_ref[j, :, LANES:] = odd.astype(bf16)

    def project(i, carry):
        rows = pl.ds(pl.multiple_of(i * ROWS, ROWS), ROWS)
        mine, theirs = own_ref[rows, :], other_ref[rows, :]
        place = lax.broadcasted_iota(jnp.int32, (ROWS, LANES), 0) + i * ROWS
        inside = jnp.logical_and(place >= first, place < last)
        q_flag = jnp.where(inside, 1.0, 0.0)
        k_flag = jnp.where(jnp.logical_and(flags, jnp.logical_not(inside)), -FAR, 0.0)
        spread = [
            dot(mine, w_ref[j, own_rows, :]) + dot(theirs, w_ref[j, other_rows, :]) for j in range(3)
        ]
        for h in range(2):
            cols = slice(h * LANES, (h + 1) * LANES)
            q_ref[h, rows, :] = (spread[0][:, cols] * scale + q_flag).astype(bf16)
            k_ref[h, rows, :] = (spread[1][:, cols] + k_flag).astype(bf16)
            ones = jnp.logical_not(low_lanes) if h == 0 else low_lanes
            v_ref[h, rows, :] = (spread[2][:, cols] + jnp.where(ones, 1.0, 0.0)).astype(bf16)
        return carry

    lax.fori_loop(0, length // ROWS, project, 0)

    def raise_scores(scores):
        return jnp.exp2(scores - jnp.max(scores, axis=1, keepdims=True)).astype(bf16)

    def query_block(i, carry):
        begin = i * ROWS
        rows = pl.ds(pl.multiple_of(begin, ROWS), ROWS)
        low, high = jnp.int32(0), jnp.int32(length)
        for t in range(tiles):
            low = jnp.where(starts[t] <= begin, starts[t], low)
            end = starts[tiles - t]
            high = jnp.where(end >= begin + ROWS, end, high)
        low = (low // 16) * 16
        blocks = (high - low + ROWS - 1) // ROWS
        for n in range(1, length // ROWS + 1):

            @pl.when(blocks == n)
            def _(n=n):
                start = jnp.minimum(low, length - n * ROWS)
                keys = pl.ds(pl.multiple_of(start, 16), n * ROWS)
                scores = [
                    lax.dot_general(
                        q_ref[h, rows, :],
                        k_ref[h, keys, :],
                        (((1,), (1,)), ((), ())),
                        preferred_element_type=f32,
                    )
                    for h in range(2)
                ]
                even = dot(raise_scores(scores[0]), v_ref[0, keys, :])
                odd = dot(raise_scores(scores[1]), v_ref[1, keys, :])
                total = pltpu.roll(jnp.where(low_lanes, odd, even), HDIM, 1)
                out_ref[rows, :] = (jnp.where(low_lanes, even, odd) / total).astype(bf16)

        return carry

    lax.fori_loop(0, length // ROWS, query_block, 0)


def attend(pair, counts, own, other, w_qkv):
    length, half = own.shape
    features = w_qkv.shape[1]
    whole = pl.BlockSpec(memory_space=pltpu.VMEM)
    return pl.pallas_call(
        functools.partial(attend_kernel, pair),
        out_shape=jax.ShapeDtypeStruct((length, LANES), bf16),
        in_specs=[pl.BlockSpec(memory_space=pltpu.SMEM), whole, whole, whole],
        out_specs=whole,
        scratch_shapes=[pltpu.VMEM((3, features, 2 * LANES), bf16)] + [pltpu.VMEM((2, length, LANES), bf16)] * 3,
        compiler_params=pltpu.CompilerParams(vmem_limit_bytes=VMEM_BYTES),
        cost_estimate=pl.CostEstimate(
            flops=32 * length * length * HDIM, bytes_accessed=8 * length * half, transcendentals=2 * length * length
        ),
    )(counts, own, other, w_qkv)


def finish_kernel(
    shards,
    rank_ref,
    gain_ref,
    points_ref,
    own_a_ref,
    own_b_ref,
    other_a_ref,
    other_b_ref,
    out_own_ref,
    out_other_ref,
    fc1_own_ref,
    fc1_other_ref,
    fc2_own_ref,
    fc2_other_ref,
    done_ref,
    whole_ref,
    context_ref,
    sems,
):
    length = points_ref.shape[0]
    half_rows = done_ref.shape[0]
    base = lax.axis_index("mp") * half_rows
    half = out_own_ref.shape[0]
    for k, ref in enumerate((own_a_ref, own_b_ref, other_a_ref, other_b_ref)):
        context_ref[:, k * LANES : (k + 1) * LANES] = ref[...]

    def away(i):
        here = pl.multiple_of(i * ROWS, ROWS)
        there = pl.multiple_of(base + i * ROWS, ROWS)
        return pltpu.make_async_copy(
            done_ref.at[pl.ds(here, ROWS)], whole_ref.at[pl.ds(there, ROWS)], sems.at[i]
        )

    def block(i, carry):
        start = pl.multiple_of(base + i * ROWS, ROWS)
        rank = rank_ref[:, pl.ds(start, ROWS)]
        slot = slots(rank, length, shards)
        slot = jnp.transpose(jnp.broadcast_to(slot, (LANES, ROWS)))
        place = lax.broadcasted_iota(jnp.int32, (ROWS, LANES), 1)
        pick = jnp.concatenate(
            [
                (slot == place + k * LANES).astype(f32).astype(bf16)
                for k in range(length // LANES)
            ],
            axis=1,
        )
        context = dot(pick, context_ref[...]).astype(bf16)
        attn_out = dot(context[:, :half], out_own_ref[...]) + dot(context[:, half:], out_other_ref[...])
        middle = points_ref[pl.ds(start, ROWS), :].astype(f32) + attn_out.astype(bf16).astype(f32)
        middle = middle.astype(bf16).astype(f32)
        normed = normalise(middle, gain_ref[...])
        total = middle
        for fc1_ref, fc2_ref in ((fc1_own_ref, fc2_own_ref), (fc1_other_ref, fc2_other_ref)):
            hidden = jax.nn.gelu(dot(normed, fc1_ref[...]), approximate=True).astype(bf16)
            total = total + dot(hidden, fc2_ref[...])
        done_ref[pl.ds(pl.multiple_of(i * ROWS, ROWS), ROWS), :] = total.astype(bf16)
        away(i).start()
        return carry

    lax.fori_loop(0, half_rows // ROWS, block, 0)
    for i in range(half_rows // ROWS):
        away(i).wait()


def finish(shards, rank_row, gain_row, points, *arrays):
    length, features = points.shape
    half_rows = length // 2
    return pl.pallas_call(
        functools.partial(finish_kernel, shards),
        out_shape=(
            jax.ShapeDtypeStruct((half_rows, features), bf16),
            jax.ShapeDtypeStruct((length, features), bf16),
        ),
        out_specs=(pl.BlockSpec(memory_space=pltpu.VMEM), pl.BlockSpec(memory_space=pl.ANY)),
        scratch_shapes=[
            pltpu.VMEM((length, features), bf16),
            pltpu.SemaphoreType.DMA((half_rows // ROWS,)),
        ],
        compiler_params=pltpu.CompilerParams(vmem_limit_bytes=VMEM_BYTES),
        cost_estimate=pl.CostEstimate(
            flops=2 * half_rows * features * (length + 9 * features),
            bytes_accessed=16 * length * features,
            transcendentals=half_rows * 4 * features,
        ),
    )(rank_row, gain_row, points, *arrays)


def join_kernel(whole_in_ref, other_ref, whole_ref, sem):
    del whole_in_ref
    half_rows = other_ref.shape[0]
    start = pl.multiple_of((1 - lax.axis_index("mp")) * half_rows, half_rows)
    copy = pltpu.make_async_copy(other_ref, whole_ref.at[pl.ds(start, half_rows)], sem)
    copy.start()
    copy.wait()


def join(whole, other):
    anywhere = pl.BlockSpec(memory_space=pl.ANY)
    return pl.pallas_call(
        join_kernel,
        out_shape=jax.ShapeDtypeStruct(whole.shape, whole.dtype),
        in_specs=[anywhere, pl.BlockSpec(memory_space=pltpu.VMEM)],
        out_specs=anywhere,
        scratch_shapes=[pltpu.SemaphoreType.DMA],
        input_output_aliases={0: 0},
    )(whole, other)


def across(values):
    return lax.ppermute(values, "mp", [(0, 1), (1, 0)])


def exchange(rows, shards):
    length, columns = rows.shape
    cells = rows.reshape(shards, length // shards, columns)
    return lax.all_to_all(cells, "space", split_axis=0, concat_axis=0, tiled=True).reshape(length, columns)


def body(points, curve_rank, patch_counts, norm_gain_attn, w_qkv, w_out, norm_gain_mlp, w_fc1, w_fc2):
    shards = lax.axis_size("space")
    length, features = points.shape
    rank_row = curve_rank.reshape(1, length)
    send = order_for_owners(points, rank_row, norm_gain_attn.reshape(1, features), shards)
    own = exchange(send, shards)
    other_fc1, other_fc2, other_out = across(w_fc1), across(w_fc2), across(w_out)
    other = across(own)
    returned = [exchange(attend(pair, patch_counts, own, other, w_qkv), shards) for pair in range(w_qkv.shape[2] // LANES)]
    crossed = [across(rows) for rows in returned]
    done, whole = finish(
        shards,
        rank_row,
        norm_gain_mlp.reshape(1, features),
        points,
        *returned,
        *crossed,
        w_out,
        other_out,
        w_fc1,
        other_fc1,
        w_fc2,
        other_fc2,
    )
    return join(whole, across(done))


def solution(mesh):
    placed = (
        P("space", None),
        P("space"),
        P("space", None),
        P(),
        P(None, None, "mp"),
        P("mp", None),
        P(),
        P(None, "mp"),
        P("mp", None),
    )
    return jax.shard_map(
        body, mesh=mesh, in_specs=placed, out_specs=P("space", None), check_vma=False
    )
```

```python
import functools
import math

import jax
import jax.numpy as jnp
from jax import lax
from jax.experimental import pallas as pl
from jax.experimental.pallas import tpu as pltpu
from jax.sharding import PartitionSpec as P

HDIM = 64
LANES = 128
ROWS = 256
EPSILON = 1e-06
FAR = 1e30
VMEM_BYTES = 58 * 1024 * 1024

f32 = jnp.float32
bf16 = jnp.bfloat16

ANYWHERE = pl.BlockSpec(memory_space=pl.ANY)
SCALARS = pl.BlockSpec(memory_space=pltpu.SMEM)


def normalise(values, gain_row):
    average = jnp.mean(values, axis=-1, keepdims=True)
    centred = values - average
    second = jnp.mean(centred * centred, axis=-1, keepdims=True)
    return (centred * lax.rsqrt(second + EPSILON) * gain_row).astype(bf16)


def dot(left, right):
    return jnp.dot(left, right, preferred_element_type=f32)


def split(number, size):
    if size & (size - 1) == 0:
        return number >> (size.bit_length() - 1), number & (size - 1)
    return number // size, number % size


def owner_slots(rank, length, shards):
    owner, within = split(rank, length)
    return owner, within - lax.axis_index("space") * (length // shards)


def equal(left, right):
    return (left == right).astype(f32).astype(bf16)


def blocks_of(length, rows=ROWS):
    return [slice(i * rows, (i + 1) * rows) for i in range(length // rows)]


def params():
    return pltpu.CompilerParams(vmem_limit_bytes=VMEM_BYTES)


def part_slots(rank, length, shards, parts):
    owner, within = owner_slots(rank, length, shards)
    part_cell = length // shards // parts
    part, row = split(within, part_cell)
    return part * (length // parts) + owner * part_cell + row


def pick_rows(first_row, slot, source_ref, out_ref):
    def order_block(i, carry):
        start = pl.multiple_of(i * ROWS, ROWS)
        place = lax.broadcasted_iota(jnp.int32, (ROWS, slot.shape[1]), 0) + (start + first_row)
        out_ref[pl.ds(start, ROWS), :] = dot(equal(place, slot), source_ref[...]).astype(bf16)
        return carry

    lax.fori_loop(0, out_ref.shape[0] // ROWS, order_block, 0)


def first_send_kernel(
    shards, parts, rank_hbm, gain_hbm, points_hbm, out_ref, normed_hbm, rank_ref, gain_ref, points_ref, half_ref, small, large, away
):
    length, features = points_ref.shape
    half = features // 2
    core = lax.axis_index("mp")
    gain_copy = pltpu.make_async_copy(gain_hbm, gain_ref, small.at[0])
    rank_copy = pltpu.make_async_copy(rank_hbm, rank_ref, small.at[1])
    rows_of = blocks_of(length)
    copies = [
        pltpu.make_async_copy(points_hbm.at[rows], points_ref.at[rows], large.at[i])
        for i, rows in enumerate(rows_of)
    ]
    gain_copy.start()
    for copy in copies:
        copy.start()
    rank_copy.start()
    gain_copy.wait()
    for copy, rows in zip(copies, rows_of):
        copy.wait()
        normed = normalise(points_ref[rows, :].astype(f32), gain_ref[...])
        half_ref[rows, :] = jnp.where(core == 0, normed[:, :half], normed[:, half:])
    keep = pltpu.make_async_copy(half_ref, normed_hbm, away)
    keep.start()
    rank_copy.wait()
    pick_rows(0, part_slots(rank_ref[...], length, shards, parts), half_ref, out_ref)
    keep.wait()


def first_send(shards, parts, rank_row, gain_row, points):
    length, features = points.shape
    return pl.pallas_call(
        functools.partial(first_send_kernel, shards, parts),
        out_shape=(
            jax.ShapeDtypeStruct((length // parts, features // 2), bf16),
            jax.ShapeDtypeStruct((length, features // 2), bf16),
        ),
        in_specs=[ANYWHERE] * 3,
        out_specs=(pl.BlockSpec(memory_space=pltpu.VMEM), ANYWHERE),
        scratch_shapes=[
            pltpu.VMEM((1, length), jnp.int32),
            pltpu.VMEM((1, features), f32),
            pltpu.VMEM((length, features), bf16),
            pltpu.VMEM((length, features // 2), bf16),
            pltpu.SemaphoreType.DMA((2,)),
            pltpu.SemaphoreType.DMA((length // ROWS,)),
            pltpu.SemaphoreType.DMA,
        ],
        compiler_params=params(),
        cost_estimate=pl.CostEstimate(
            flops=length * length * features // parts, bytes_accessed=4 * length * features, transcendentals=0
        ),
    )(rank_row, gain_row, points)


def next_send_kernel(shards, parts, part, rank_hbm, normed_hbm, out_ref, rank_ref, half_ref, sems):
    length = half_ref.shape[0]
    copies = [
        pltpu.make_async_copy(rank_hbm, rank_ref, sems.at[0]),
        pltpu.make_async_copy(normed_hbm, half_ref, sems.at[1]),
    ]
    for copy in copies:
        copy.start()
    for copy in copies:
        copy.wait()
    pick_rows(part * out_ref.shape[0], part_slots(rank_ref[...], length, shards, parts), half_ref, out_ref)


def next_send(shards, parts, part, rank_row, normed):
    length, half = normed.shape
    return pl.pallas_call(
        functools.partial(next_send_kernel, shards, parts, part),
        out_shape=jax.ShapeDtypeStruct((length // parts, half), bf16),
        in_specs=[ANYWHERE] * 2,
        out_specs=pl.BlockSpec(memory_space=pltpu.VMEM),
        scratch_shapes=[
            pltpu.VMEM((1, length), jnp.int32),
            pltpu.VMEM((length, half), bf16),
            pltpu.SemaphoreType.DMA((2,)),
        ],
        compiler_params=params(),
        cost_estimate=pl.CostEstimate(
            flops=2 * length * length * half // parts, bytes_accessed=4 * length * half, transcendentals=0
        ),
    )(rank_row, normed)


def attend_kernel(pair, parts, counts_ref, *refs):
    arrived = refs[: 2 * parts]
    weight_hbm, out_hbm, x_ref, raw_ref, w_ref, q_ref, k_ref, v_ref, out_ref, x_sems, w_sems, out_sems = refs[2 * parts :]
    length, features = q_ref.shape[1], w_ref.shape[0]
    half = features // 2
    tiles = counts_ref.shape[1]
    core = lax.axis_index("mp")
    scale = math.log2(math.e) / math.sqrt(HDIM)
    pair_columns = slice(pair * LANES, (pair + 1) * LANES)

    w_copies = [
        pltpu.make_async_copy(
            weight_hbm.at[:, pl.ds(pl.multiple_of(at * half, half), half), pair_columns],
            raw_ref.at[:, k * half : (k + 1) * half],
            w_sems.at[k],
        )
        for k, at in enumerate((core, 1 - core))
    ]
    part_cell = arrived[0].shape[1]
    x_copies = [
        pltpu.make_async_copy(
            arrived[k * parts + part],
            x_ref.at[:, part * part_cell : (part + 1) * part_cell, k * half : (k + 1) * half],
            x_sems.at[k * parts + part],
        )
        for k in range(2)
        for part in range(parts)
    ]
    for copy in w_copies + x_copies:
        copy.start()

    starts = [jnp.int32(0)]
    for t in range(tiles):
        starts.append(starts[-1] + counts_ref[0, t])
    lane = lax.broadcasted_iota(jnp.int32, (1, LANES), 1)
    first = jnp.full((1, LANES), length, jnp.int32)
    last = jnp.zeros((1, LANES), jnp.int32)
    for t in range(tiles):
        first = jnp.where(lane == HDIM + t, starts[t], first)
        last = jnp.where(lane == HDIM + t, starts[t + 1], last)
    flags = jnp.logical_and(lane >= HDIM, lane < HDIM + tiles)
    low_lanes = lane < HDIM

    for copy in w_copies:
        copy.wait()
    for j in range(3):
        both = raw_ref[j].astype(f32)
        at = 2 * j * LANES
        w_ref[:, at : at + LANES] = jnp.where(low_lanes, both, 0.0).astype(bf16)
        odd = jnp.where(low_lanes, pltpu.roll(both, HDIM, 1), 0.0) if j < 2 else jnp.where(low_lanes, 0.0, both)
        w_ref[:, at + LANES : at + 2 * LANES] = odd.astype(bf16)
    for copy in x_copies:
        copy.wait()

    cell = x_ref.shape[1]
    cells = ROWS // cell

    def project(i, carry):
        rows = pl.ds(pl.multiple_of(i * ROWS, ROWS), ROWS)
        block = x_ref[pl.ds(i * cells, cells)].reshape(ROWS, features)
        place = lax.broadcasted_iota(jnp.int32, (ROWS, LANES), 0) + i * ROWS
        inside = jnp.logical_and(place >= first, place < last)
        q_flag = jnp.where(inside, 1.0, 0.0)
        k_flag = jnp.where(jnp.logical_and(flags, jnp.logical_not(inside)), -FAR, 0.0)
        spread = dot(block, w_ref[...])
        for h in range(2):
            q, k, v = (spread[:, (2 * j + h) * LANES : (2 * j + h + 1) * LANES] for j in range(3))
            q_ref[h, rows, :] = (q * scale + q_flag).astype(bf16)
            k_ref[h, rows, :] = (k + k_flag).astype(bf16)
            ones = jnp.logical_not(low_lanes) if h == 0 else low_lanes
            v_ref[h, rows, :] = (v + jnp.where(ones, 1.0, 0.0)).astype(bf16)
        return carry

    lax.fori_loop(0, length // ROWS, project, 0)

    def raise_scores(scores):
        return jnp.exp2(scores - jnp.max(scores, axis=1, keepdims=True)).astype(bf16)

    def send_out(i):
        rows = pl.ds(pl.multiple_of(i * ROWS, ROWS), ROWS)
        return pltpu.make_async_copy(out_ref.at[rows], out_hbm.at[rows], out_sems.at[i])

    def query_block(i, carry):
        begin = i * ROWS
        rows = pl.ds(pl.multiple_of(begin, ROWS), ROWS)
        low, high = jnp.int32(0), jnp.int32(length)
        for t in range(tiles):
            low = jnp.where(starts[t] <= begin, starts[t], low)
            end = starts[tiles - t]
            high = jnp.where(end >= begin + ROWS, end, high)
        low = (low // 16) * 16
        blocks = (high - low + ROWS - 1) // ROWS
        for n in range(1, length // ROWS + 1):

            @pl.when(blocks == n)
            def _(n=n):
                start = jnp.minimum(low, length - n * ROWS)
                keys = pl.ds(pl.multiple_of(start, 16), n * ROWS)
                scores = [
                    lax.dot_general(
                        q_ref[h, rows, :],
                        k_ref[h, keys, :],
                        (((1,), (1,)), ((), ())),
                        preferred_element_type=f32,
                    )
                    for h in range(2)
                ]
                even = dot(raise_scores(scores[0]), v_ref[0, keys, :])
                odd = dot(raise_scores(scores[1]), v_ref[1, keys, :])
                total = pltpu.roll(jnp.where(low_lanes, odd, even), HDIM, 1)
                out_ref[rows, :] = (jnp.where(low_lanes, even, odd) / total).astype(bf16)

        send_out(i).start()
        return carry

    lax.fori_loop(0, length // ROWS, query_block, 0)
    for i in range(length // ROWS):
        send_out(i).wait()


def attend(pair, counts, arrived, w_qkv):
    parts = len(arrived) // 2
    shards, part_cell, half = arrived[0].shape
    cell = part_cell * parts
    length = shards * cell
    features = 2 * half
    return pl.pallas_call(
        functools.partial(attend_kernel, pair, parts),
        out_shape=jax.ShapeDtypeStruct((length, LANES), bf16),
        in_specs=[SCALARS] + [ANYWHERE] * (2 * parts + 1),
        out_specs=ANYWHERE,
        scratch_shapes=[
            pltpu.VMEM((shards, cell, features), bf16),
            pltpu.VMEM((3, features, LANES), bf16),
            pltpu.VMEM((features, 6 * LANES), bf16),
            pltpu.VMEM((2, length, LANES), bf16),
            pltpu.VMEM((2, length, LANES), bf16),
            pltpu.VMEM((2, length, LANES), bf16),
            pltpu.VMEM((length, LANES), bf16),
            pltpu.SemaphoreType.DMA((2 * parts,)),
            pltpu.SemaphoreType.DMA((2,)),
            pltpu.SemaphoreType.DMA((length // ROWS,)),
        ],
        compiler_params=params(),
        cost_estimate=pl.CostEstimate(
            flops=32 * length * length * HDIM, bytes_accessed=8 * length * half, transcendentals=2 * length * length
        ),
    )(counts, *arrived, w_qkv)


def unorder(rank_ref, start, length, shards, context_ref):
    owner, within = owner_slots(rank_ref[:, pl.ds(start, ROWS)], length, shards)
    slot = owner * (length // shards) + within
    slot = jnp.transpose(jnp.broadcast_to(slot, (LANES, ROWS)))
    place = lax.broadcasted_iota(jnp.int32, (ROWS, LANES), 1)
    pick = jnp.concatenate([equal(slot, place + k * LANES) for k in range(length // LANES)], axis=1)
    return dot(pick, context_ref[...]).astype(bf16)


def unorder_kernel(shards, rank_hbm, own_hbm, other_hbm, out_ref, rank_ref, context_ref, sems):
    length = context_ref.shape[0]
    half_rows = out_ref.shape[0]
    base = lax.axis_index("mp") * half_rows
    copies = [
        pltpu.make_async_copy(rank_hbm, rank_ref, sems.at[0]),
        pltpu.make_async_copy(own_hbm, context_ref.at[:, :LANES], sems.at[1]),
        pltpu.make_async_copy(other_hbm, context_ref.at[:, LANES:], sems.at[2]),
    ]
    for copy in copies:
        copy.start()
    for copy in copies:
        copy.wait()

    def block(i, carry):
        start = pl.multiple_of(base + i * ROWS, ROWS)
        out_ref[pl.ds(pl.multiple_of(i * ROWS, ROWS), ROWS), :] = unorder(
            rank_ref, start, length, shards, context_ref
        )
        return carry

    lax.fori_loop(0, half_rows // ROWS, block, 0)


def unorder_pair(shards, rank_row, own, other):
    length = own.shape[0]
    half_rows = length // 2
    return pl.pallas_call(
        functools.partial(unorder_kernel, shards),
        out_shape=jax.ShapeDtypeStruct((half_rows, 2 * LANES), bf16),
        in_specs=[ANYWHERE] * 3,
        out_specs=pl.BlockSpec(memory_space=pltpu.VMEM),
        scratch_shapes=[
            pltpu.VMEM((1, length), jnp.int32),
            pltpu.VMEM((length, 2 * LANES), bf16),
            pltpu.SemaphoreType.DMA((3,)),
        ],
        compiler_params=params(),
        cost_estimate=pl.CostEstimate(
            flops=4 * half_rows * length * LANES, bytes_accessed=8 * length * LANES, transcendentals=0
        ),
    )(rank_row, own, other)


def finish_kernel(
    shards,
    rank_hbm,
    gain_hbm,
    points_hbm,
    first_hbm,
    own_hbm,
    other_hbm,
    out_own_hbm,
    out_other_hbm,
    fc1_own_hbm,
    fc1_other_hbm,
    fc2_own_hbm,
    fc2_other_hbm,
    done_ref,
    whole_hbm,
    rank_ref,
    gain_ref,
    points_ref,
    first_ref,
    context_ref,
    out_ref,
    fc1_ref,
    fc2_ref,
    in_sems,
    sems,
):
    length = context_ref.shape[0]
    half_rows = done_ref.shape[0]
    base = pl.multiple_of(lax.axis_index("mp") * half_rows, half_rows)
    half = out_own_hbm.shape[0]
    hidden_half = fc2_own_hbm.shape[0]
    pairs = [
        (rank_hbm, rank_ref),
        (own_hbm, context_ref.at[:, :LANES]),
        (other_hbm, context_ref.at[:, LANES:]),
        (gain_hbm, gain_ref),
        (first_hbm, first_ref),
        (out_own_hbm, out_ref.at[:half]),
        (out_other_hbm, out_ref.at[half:]),
        (points_hbm.at[pl.ds(base, half_rows)], points_ref),
        (fc1_own_hbm, fc1_ref.at[0]),
        (fc2_own_hbm, fc2_ref.at[0]),
        (fc1_other_hbm, fc1_ref.at[1]),
        (fc2_other_hbm, fc2_ref.at[1]),
    ]
    copies = [pltpu.make_async_copy(*pair, in_sems.at[k]) for k, pair in enumerate(pairs)]
    for copy in copies:
        copy.start()

    def away(i):
        here = pl.multiple_of(i * ROWS, ROWS)
        there = pl.multiple_of(base + i * ROWS, ROWS)
        return pltpu.make_async_copy(
            done_ref.at[pl.ds(here, ROWS)], whole_hbm.at[pl.ds(there, ROWS)], sems.at[i]
        )

    def block(i, late):
        here = pl.ds(pl.multiple_of(i * ROWS, ROWS), ROWS)
        start = pl.multiple_of(base + i * ROWS, ROWS)
        second = unorder(rank_ref, start, length, shards, context_ref)
        for copy in late[:5]:
            copy.wait()
        pick = first_ref[here, :]
        context = jnp.concatenate([pick[:, :LANES], second[:, :LANES], pick[:, LANES:], second[:, LANES:]], axis=1)
        attn_out = dot(context, out_ref[...]).astype(bf16).astype(f32)
        middle = (points_ref[here, :].astype(f32) + attn_out).astype(bf16).astype(f32)
        normed = normalise(middle, gain_ref[...])
        for copy in late[5:]:
            copy.wait()
        total = middle
        for k in range(2):
            hidden = jax.nn.gelu(dot(normed, fc1_ref[k]), approximate=True).astype(bf16)
            total = total + dot(hidden, fc2_ref[k])
        done_ref[here, :] = total.astype(bf16)
        away(i).start()

    for copy in copies[:3]:
        copy.wait()
    block(0, copies[3:])

    def rest(i, carry):
        block(i, ())
        return carry

    lax.fori_loop(1, half_rows // ROWS, rest, 0)
    for i in range(half_rows // ROWS):
        away(i).wait()


def finish(shards, rank_row, gain_row, points, first, own, other, w_out, other_out, *mlp):
    length, features = points.shape
    half_rows = length // 2
    hidden_half = mlp[2].shape[0]
    return pl.pallas_call(
        functools.partial(finish_kernel, shards),
        out_shape=(
            jax.ShapeDtypeStruct((half_rows, features), bf16),
            jax.ShapeDtypeStruct((length, features), bf16),
        ),
        in_specs=[ANYWHERE] * 12,
        out_specs=(pl.BlockSpec(memory_space=pltpu.VMEM), ANYWHERE),
        scratch_shapes=[
            pltpu.VMEM((1, length), jnp.int32),
            pltpu.VMEM((1, features), f32),
            pltpu.VMEM((half_rows, features), bf16),
            pltpu.VMEM((half_rows, 2 * LANES), bf16),
            pltpu.VMEM((length, 2 * LANES), bf16),
            pltpu.VMEM((features, features), bf16),
            pltpu.VMEM((2, features, hidden_half), bf16),
            pltpu.VMEM((2, hidden_half, features), bf16),
            pltpu.SemaphoreType.DMA((12,)),
            pltpu.SemaphoreType.DMA((half_rows // ROWS,)),
        ],
        compiler_params=params(),
        cost_estimate=pl.CostEstimate(
            flops=2 * half_rows * features * (length + 9 * features),
            bytes_accessed=16 * length * features,
            transcendentals=half_rows * 4 * features,
        ),
    )(rank_row, gain_row, points, first, own, other, w_out, other_out, *mlp)


def across(values):
    return lax.ppermute(values, "mp", [(0, 1), (1, 0)])


def exchange(rows, shards):
    length, columns = rows.shape
    cells = rows.reshape(shards, length // shards, columns)
    return lax.all_to_all(cells, "space", split_axis=0, concat_axis=0, tiled=True)


def body(points, curve_rank, patch_counts, norm_gain_attn, w_qkv, w_out, norm_gain_mlp, w_fc1, w_fc2):
    shards = lax.axis_size("space")
    length, features = points.shape
    parts = 2 if (length // shards) % 32 == 0 else 1
    rank_row = curve_rank.reshape(1, length)
    send, normed = first_send(shards, parts, rank_row, norm_gain_attn.reshape(1, features), points)
    own = [exchange(send, shards)]
    for part in range(1, parts):
        own.append(exchange(next_send(shards, parts, part, rank_row, normed), shards))
    mlp = w_fc1, across(w_fc1), w_fc2, across(w_fc2)
    other_out = across(w_out)
    other = [across(rows) for rows in own]
    returned = [
        exchange(attend(pair, patch_counts, own + other, w_qkv), shards).reshape(length, LANES) for pair in range(2)
    ]
    crossed = [across(rows) for rows in returned]
    first = unorder_pair(shards, rank_row, returned[0], crossed[0])
    done, whole = finish(
        shards,
        rank_row,
        norm_gain_mlp.reshape(1, features),
        points,
        first,
        returned[1],
        crossed[1],
        w_out,
        other_out,
        *mlp,
    )
    start = (1 - lax.axis_index("mp")) * (length // 2)
    return lax.dynamic_update_slice(whole, across(done), (start, 0))


def solution(mesh):
    placed = (
        P("space", None),
        P("space"),
        P("space", None),
        P(),
        P(None, None, "mp"),
        P("mp", None),
        P(),
        P(None, "mp"),
        P("mp", None),
    )
    return jax.shard_map(
        body, mesh=mesh, in_specs=placed, out_specs=P("space", None), check_vma=False
    )
```

```python
import functools
import math

import jax
import jax.numpy as jnp
from jax import lax
from jax.experimental import pallas as pl
from jax.experimental.pallas import tpu as pltpu
from jax.sharding import PartitionSpec as P

HDIM = 64
LANES = 128
ROWS = 256
EPSILON = 1e-06
FAR = 1e30
VMEM_BYTES = 58 * 1024 * 1024

f32 = jnp.float32
bf16 = jnp.bfloat16

ANYWHERE = pl.BlockSpec(memory_space=pl.ANY)
SCALARS = pl.BlockSpec(memory_space=pltpu.SMEM)


def normalise(values, gain_row):
    average = jnp.mean(values, axis=-1, keepdims=True)
    centred = values - average
    second = jnp.mean(centred * centred, axis=-1, keepdims=True)
    return (centred * lax.rsqrt(second + EPSILON) * gain_row).astype(bf16)


def dot(left, right):
    return jnp.dot(left, right, preferred_element_type=f32)


def split(number, size):
    if size & (size - 1) == 0:
        return number >> (size.bit_length() - 1), number & (size - 1)
    return number // size, number % size


def slots(rank, length, shards):
    cell = length // shards
    owner, within = split(rank, length)
    return owner * cell + within - lax.axis_index("space") * cell


def one_hot(rows_at, columns_at):
    if columns_at.shape[1] <= 1 << 15:
        rows_at, columns_at = rows_at.astype(jnp.int16), columns_at.astype(jnp.int16)
    one, nil = jnp.ones((), bf16), jnp.zeros((), bf16)
    return jnp.concatenate(
        [
            jnp.where(rows_at == columns_at[:, k : k + LANES], one, nil)
            for k in range(0, columns_at.shape[1], LANES)
        ],
        axis=1,
    )


def blocks_of(length, rows=ROWS):
    return [slice(i * rows, (i + 1) * rows) for i in range(length // rows)]


def params():
    return pltpu.CompilerParams(vmem_limit_bytes=VMEM_BYTES)


def send_kernel(shards, rank_hbm, gain_hbm, points_hbm, out_ref, rank_ref, gain_ref, points_ref, half_ref, small, large):
    length, features = points_ref.shape
    half = features // 2
    core = lax.axis_index("mp")
    gain_copy = pltpu.make_async_copy(gain_hbm, gain_ref, small.at[0])
    rank_copy = pltpu.make_async_copy(rank_hbm, rank_ref, small.at[1])
    rows_of = blocks_of(length)
    copies = [
        pltpu.make_async_copy(points_hbm.at[rows], points_ref.at[rows], large.at[i])
        for i, rows in enumerate(rows_of)
    ]
    gain_copy.start()
    for copy in copies:
        copy.start()
    rank_copy.start()
    gain_copy.wait()
    for copy, rows in zip(copies, rows_of):
        copy.wait()
        normed = normalise(points_ref[rows, :].astype(f32), gain_ref[...])
        half_ref[rows, :] = jnp.where(core == 0, normed[:, :half], normed[:, half:])
    rank_copy.wait()
    slot = slots(rank_ref[...], length, shards)

    def order_block(i, carry):
        start = pl.multiple_of(i * ROWS, ROWS)
        place = lax.broadcasted_iota(jnp.int32, (ROWS, LANES), 0) + start
        out_ref[pl.ds(start, ROWS), :] = dot(one_hot(place, slot), half_ref[...]).astype(bf16)
        return carry

    lax.fori_loop(0, length // ROWS, order_block, 0)


def order_for_owners(shards, rank_row, gain_row, points):
    length, features = points.shape
    return pl.pallas_call(
        functools.partial(send_kernel, shards),
        out_shape=jax.ShapeDtypeStruct((length, features // 2), bf16),
        in_specs=[ANYWHERE] * 3,
        out_specs=pl.BlockSpec(memory_space=pltpu.VMEM),
        scratch_shapes=[
            pltpu.VMEM((1, length), jnp.int32),
            pltpu.VMEM((1, features), f32),
            pltpu.VMEM((length, features), bf16),
            pltpu.VMEM((length, features // 2), bf16),
            pltpu.SemaphoreType.DMA((2,)),
            pltpu.SemaphoreType.DMA((length // ROWS,)),
        ],
        compiler_params=params(),
        cost_estimate=pl.CostEstimate(
            flops=length * length * features, bytes_accessed=4 * length * features, transcendentals=0
        ),
    )(rank_row, gain_row, points)


def attend_kernel(
    pair,
    counts_ref,
    own_hbm,
    other_hbm,
    weight_hbm,
    out_hbm,
    x_ref,
    raw_ref,
    w_ref,
    q_ref,
    k_ref,
    v_ref,
    out_ref,
    x_sems,
    w_sems,
    out_sems,
):
    length, features = x_ref.shape
    half = features // 2
    tiles = counts_ref.shape[1]
    core = lax.axis_index("mp")
    scale = math.log2(math.e) / math.sqrt(HDIM)
    pair_columns = slice(pair * LANES, (pair + 1) * LANES)

    w_copies = [
        pltpu.make_async_copy(
            weight_hbm.at[:, pl.ds(pl.multiple_of(at * half, half), half), pair_columns],
            raw_ref.at[:, k * half : (k + 1) * half],
            w_sems.at[k],
        )
        for k, at in enumerate((core, 1 - core))
    ]
    x_copies = [
        [
            pltpu.make_async_copy(
                source.at[rows], x_ref.at[rows, k * half : (k + 1) * half], x_sems.at[2 * i + k]
            )
            for k, source in enumerate((own_hbm, other_hbm))
        ]
        for i, rows in enumerate(blocks_of(length, 2 * ROWS))
    ]
    for copy in w_copies + sum(x_copies, []):
        copy.start()

    starts = [jnp.int32(0)]
    for t in range(tiles):
        starts.append(starts[-1] + counts_ref[0, t])
    lane = lax.broadcasted_iota(jnp.int32, (1, LANES), 1)
    first = jnp.full((1, LANES), length, jnp.int32)
    last = jnp.zeros((1, LANES), jnp.int32)
    for t in range(tiles):
        first = jnp.where(lane == HDIM + t, starts[t], first)
        last = jnp.where(lane == HDIM + t, starts[t + 1], last)
    flags = jnp.logical_and(lane >= HDIM, lane < HDIM + tiles)
    low_lanes = lane < HDIM

    for copy in w_copies:
        copy.wait()
    for j in range(3):
        both = raw_ref[j].astype(f32)
        at = 2 * j * LANES
        w_ref[:, at : at + LANES] = jnp.where(low_lanes, both, 0.0).astype(bf16)
        odd = jnp.where(low_lanes, pltpu.roll(both, HDIM, 1), 0.0) if j < 2 else jnp.where(low_lanes, 0.0, both)
        w_ref[:, at + LANES : at + 2 * LANES] = odd.astype(bf16)

    def project(i, carry):
        rows = pl.ds(pl.multiple_of(i * ROWS, ROWS), ROWS)
        block = x_ref[rows, :]
        place = lax.broadcasted_iota(jnp.int32, (ROWS, LANES), 0) + i * ROWS
        inside = jnp.logical_and(place >= first, place < last)
        q_flag = jnp.where(inside, 1.0, 0.0)
        k_flag = jnp.where(jnp.logical_and(flags, jnp.logical_not(inside)), -FAR, 0.0)
        spread = dot(block, w_ref[...])
        for h in range(2):
            q, k, v = (spread[:, (2 * j + h) * LANES : (2 * j + h + 1) * LANES] for j in range(3))
            q_ref[h, rows, :] = (q * scale + q_flag).astype(bf16)
            k_ref[h, rows, :] = (k + k_flag).astype(bf16)
            ones = jnp.logical_not(low_lanes) if h == 0 else low_lanes
            v_ref[h, rows, :] = (v + jnp.where(ones, 1.0, 0.0)).astype(bf16)
        return carry

    for i, copies in enumerate(x_copies):
        for copy in copies:
            copy.wait()
        lax.fori_loop(2 * i, 2 * i + 2, project, 0)

    def raise_scores(scores):
        return jnp.exp2(scores - jnp.max(scores, axis=1, keepdims=True)).astype(bf16)

    def send_out(i):
        rows = pl.ds(pl.multiple_of(i * ROWS, ROWS), ROWS)
        return pltpu.make_async_copy(out_ref.at[rows], out_hbm.at[rows], out_sems.at[i])

    def query_block(i, carry):
        begin = i * ROWS
        rows = pl.ds(pl.multiple_of(begin, ROWS), ROWS)
        low, high = jnp.int32(0), jnp.int32(length)
        for t in range(tiles):
            low = jnp.where(starts[t] <= begin, starts[t], low)
            end = starts[tiles - t]
            high = jnp.where(end >= begin + ROWS, end, high)
        low = (low // 16) * 16
        blocks = (high - low + ROWS - 1) // ROWS
        for n in range(1, length // ROWS + 1):

            @pl.when(blocks == n)
            def _(n=n):
                start = jnp.minimum(low, length - n * ROWS)
                keys = pl.ds(pl.multiple_of(start, 16), n * ROWS)
                scores = [
                    lax.dot_general(
                        q_ref[h, rows, :],
                        k_ref[h, keys, :],
                        (((1,), (1,)), ((), ())),
                        preferred_element_type=f32,
                    )
                    for h in range(2)
                ]
                even = dot(raise_scores(scores[0]), v_ref[0, keys, :])
                odd = dot(raise_scores(scores[1]), v_ref[1, keys, :])
                total = pltpu.roll(jnp.where(low_lanes, odd, even), HDIM, 1)
                out_ref[rows, :] = (jnp.where(low_lanes, even, odd) / total).astype(bf16)

        send_out(i).start()
        return carry

    lax.fori_loop(0, length // ROWS, query_block, 0)
    for i in range(length // ROWS):
        send_out(i).wait()


def attend(pair, counts, own, other, w_qkv):
    length, half = own.shape
    features = 2 * half
    return pl.pallas_call(
        functools.partial(attend_kernel, pair),
        out_shape=jax.ShapeDtypeStruct((length, LANES), bf16),
        in_specs=[SCALARS] + [ANYWHERE] * 3,
        out_specs=ANYWHERE,
        scratch_shapes=[
            pltpu.VMEM((length, features), bf16),
            pltpu.VMEM((3, features, LANES), bf16),
            pltpu.VMEM((features, 6 * LANES), bf16),
            pltpu.VMEM((2, length, LANES), bf16),
            pltpu.VMEM((2, length, LANES), bf16),
            pltpu.VMEM((2, length, LANES), bf16),
            pltpu.VMEM((length, LANES), bf16),
            pltpu.SemaphoreType.DMA((length // ROWS,)),
            pltpu.SemaphoreType.DMA((2,)),
            pltpu.SemaphoreType.DMA((length // ROWS,)),
        ],
        compiler_params=params(),
        cost_estimate=pl.CostEstimate(
            flops=32 * length * length * HDIM, bytes_accessed=8 * length * half, transcendentals=2 * length * length
        ),
    )(counts, own, other, w_qkv)


def gelu_of_half(h):
    inner = 2 * math.sqrt(2 / math.pi)
    return h + h * jnp.tanh(h * (inner + (4 * 0.044715 * inner) * (h * h)))


def finish_kernel(
    shards,
    rank_hbm,
    gain_hbm,
    points_hbm,
    own_a_hbm,
    other_a_hbm,
    own_b_hbm,
    other_b_hbm,
    out_own_hbm,
    out_other_hbm,
    fc1_own_hbm,
    fc1_other_hbm,
    fc2_own_hbm,
    fc2_other_hbm,
    done_ref,
    whole_hbm,
    rank_ref,
    gain_ref,
    points_ref,
    context_ref,
    out_ref,
    fc1_ref,
    fc2_ref,
    middle_ref,
    normed_ref,
    in_sems,
    sems,
):
    length = context_ref.shape[0]
    half_rows = done_ref.shape[0]
    base = pl.multiple_of(lax.axis_index("mp") * half_rows, half_rows)
    half = out_own_hbm.shape[0]
    hidden_half = fc2_own_hbm.shape[0]
    early = [
        (rank_hbm, rank_ref),
        (own_a_hbm, context_ref.at[:, :LANES]),
        (own_b_hbm, context_ref.at[:, LANES : 2 * LANES]),
        (other_a_hbm, context_ref.at[:, 2 * LANES : 3 * LANES]),
        (other_b_hbm, context_ref.at[:, 3 * LANES :]),
    ]
    later = [
        (out_own_hbm, out_ref.at[:half]),
        (out_other_hbm, out_ref.at[half:]),
        (gain_hbm, gain_ref),
        (points_hbm.at[pl.ds(base, half_rows)], points_ref),
    ]
    last = [
        (fc1_own_hbm, fc1_ref.at[:, :hidden_half]),
        (fc1_other_hbm, fc1_ref.at[:, hidden_half:]),
        (fc2_own_hbm, fc2_ref.at[:hidden_half]),
        (fc2_other_hbm, fc2_ref.at[hidden_half:]),
    ]
    copies = [pltpu.make_async_copy(*ends, in_sems.at[k]) for k, ends in enumerate(early + later + last)]
    early, later, last = copies[:5], copies[5:9], copies[9:]
    for copy in copies:
        copy.start()

    def here(i):
        return pl.ds(pl.multiple_of(i * ROWS, ROWS), ROWS)

    def attend_out(i):
        start = pl.multiple_of(base + i * ROWS, ROWS)
        slot = slots(rank_ref[:, pl.ds(start, ROWS)], length, shards)
        slot = jnp.transpose(jnp.broadcast_to(slot, (LANES, ROWS)))
        place = lax.broadcasted_iota(jnp.int32, (1, length), 1)
        context = dot(one_hot(slot, place), context_ref[...]).astype(bf16)
        return context

    def residual(i, context):
        attn_out = dot(context, out_ref[...]).astype(bf16).astype(f32)
        middle = (points_ref[here(i), :].astype(f32) + attn_out).astype(bf16)
        middle_ref[here(i), :] = middle
        normed_ref[here(i), :] = normalise(middle.astype(f32), gain_ref[...]) * 0.5

    for copy in early:
        copy.wait()
    context = attend_out(0)
    for copy in later:
        copy.wait()
    residual(0, context)

    def rest(i, carry):
        residual(i, attend_out(i))
        return carry

    lax.fori_loop(1, half_rows // ROWS, rest, 0)
    for copy in last:
        copy.wait()

    def away(i):
        there = pl.multiple_of(base + i * ROWS, ROWS)
        return pltpu.make_async_copy(done_ref.at[here(i)], whole_hbm.at[pl.ds(there, ROWS)], sems.at[i])

    chunks = blocks_of(2 * hidden_half, 2 * ROWS)

    def mlp(i, carry):
        normed = normed_ref[here(i), :]
        total = middle_ref[here(i), :].astype(f32)
        half_hidden = dot(normed, fc1_ref[:, chunks[0]])
        for k, chunk in enumerate(chunks):
            ahead = dot(normed, fc1_ref[:, chunks[k + 1]]) if k + 1 < len(chunks) else None
            total = total + dot(gelu_of_half(half_hidden).astype(bf16), fc2_ref[chunk, :])
            half_hidden = ahead
        done_ref[here(i), :] = total.astype(bf16)
        away(i).start()
        return carry

    lax.fori_loop(0, half_rows // ROWS, mlp, 0)
    for i in range(half_rows // ROWS):
        away(i).wait()


def finish(shards, rank_row, gain_row, points, *arrays):
    length, features = points.shape
    half_rows = length // 2
    hidden = 2 * arrays[-1].shape[0]
    return pl.pallas_call(
        functools.partial(finish_kernel, shards),
        out_shape=(
            jax.ShapeDtypeStruct((half_rows, features), bf16),
            jax.ShapeDtypeStruct((length, features), bf16),
        ),
        in_specs=[ANYWHERE] * 13,
        out_specs=(pl.BlockSpec(memory_space=pltpu.VMEM), ANYWHERE),
        scratch_shapes=[
            pltpu.VMEM((1, length), jnp.int32),
            pltpu.VMEM((1, features), f32),
            pltpu.VMEM((half_rows, features), bf16),
            pltpu.VMEM((length, features), bf16),
            pltpu.VMEM((features, features), bf16),
            pltpu.VMEM((features, hidden), bf16),
            pltpu.VMEM((hidden, features), bf16),
            pltpu.VMEM((half_rows, features), bf16),
            pltpu.VMEM((half_rows, features), bf16),
            pltpu.SemaphoreType.DMA((13,)),
            pltpu.SemaphoreType.DMA((half_rows // ROWS,)),
        ],
        compiler_params=params(),
        cost_estimate=pl.CostEstimate(
            flops=2 * half_rows * features * (length + 9 * features),
            bytes_accessed=16 * length * features,
            transcendentals=half_rows * 4 * features,
        ),
    )(rank_row, gain_row, points, *arrays)


def across(values):
    return lax.ppermute(values, "mp", [(0, 1), (1, 0)])


def exchange(rows, shards):
    length, columns = rows.shape
    cells = rows.reshape(shards, length // shards, columns)
    return lax.all_to_all(cells, "space", split_axis=0, concat_axis=0, tiled=True).reshape(length, columns)


def body(points, curve_rank, patch_counts, norm_gain_attn, w_qkv, w_out, norm_gain_mlp, w_fc1, w_fc2):
    shards = lax.axis_size("space")
    length, features = points.shape
    rank_row = curve_rank.reshape(1, length)
    own = exchange(order_for_owners(shards, rank_row, norm_gain_attn.reshape(1, features), points), shards)
    mlp = w_fc1, across(w_fc1), w_fc2, across(w_fc2)
    other_out = across(w_out)
    other = across(own)
    returned = [exchange(attend(pair, patch_counts, own, other, w_qkv), shards) for pair in range(2)]
    context = [rows for own_rows in returned for rows in (own_rows, across(own_rows))]
    done, whole = finish(
        shards, rank_row, norm_gain_mlp.reshape(1, features), points, *context, w_out, other_out, *mlp
    )
    start = (1 - lax.axis_index("mp")) * (length // 2)
    return lax.dynamic_update_slice(whole, across(done), (start, 0))


def solution(mesh):
    placed = (
        P("space", None),
        P("space"),
        P("space", None),
        P(),
        P(None, None, "mp"),
        P("mp", None),
        P(),
        P(None, "mp"),
        P("mp", None),
    )
    return jax.shard_map(
        body, mesh=mesh, in_specs=placed, out_specs=P("space", None), check_vma=False
    )
```

```python
import functools
import math

import jax
import jax.numpy as jnp
from jax import lax
from jax.experimental import pallas as pl
from jax.experimental.pallas import tpu as pltpu
from jax.sharding import PartitionSpec as P

HDIM = 64
LANES = 128
ROWS = 256
TALL = 512
KEYS = 256
EPSILON = 1e-06
FAR = 1e30
VMEM_BYTES = 58 * 1024 * 1024
SMALL_BYTES = 30 * 1024 * 1024

f32 = jnp.float32
bf16 = jnp.bfloat16

ANYWHERE = pl.BlockSpec(memory_space=pl.ANY)
SCALARS = pl.BlockSpec(memory_space=pltpu.SMEM)


def normalise(values, gain_row):
    average = jnp.mean(values, axis=-1, keepdims=True)
    centred = values - average
    second = jnp.mean(centred * centred, axis=-1, keepdims=True)
    return (centred * lax.rsqrt(second + EPSILON) * gain_row).astype(bf16)


def dot(left, right):
    return jnp.dot(left, right, preferred_element_type=f32)


def split(number, size):
    if size & (size - 1) == 0:
        return number >> (size.bit_length() - 1), number & (size - 1)
    return number // size, number % size


def slots(rank, length, shards):
    cell = length // shards
    owner, within = split(rank, length)
    return owner * cell + within - lax.axis_index("space") * cell


def one_hot(rows_at, columns_at):
    if columns_at.shape[1] <= 1 << 15:
        rows_at, columns_at = rows_at.astype(jnp.int16), columns_at.astype(jnp.int16)
    one, nil = jnp.ones((), bf16), jnp.zeros((), bf16)
    return jnp.concatenate(
        [
            jnp.where(rows_at == columns_at[:, k : k + LANES], one, nil)
            for k in range(0, columns_at.shape[1], LANES)
        ],
        axis=1,
    )


def blocks_of(length, rows=ROWS):
    return [slice(i * rows, (i + 1) * rows) for i in range(length // rows)]


def params(limit=VMEM_BYTES):
    return pltpu.CompilerParams(vmem_limit_bytes=limit)


def send_kernel(shards, rank_hbm, gain_hbm, points_hbm, out_ref, rank_ref, gain_ref, points_ref, half_ref, small, large):
    length, features = points_ref.shape
    half = features // 2
    core = lax.axis_index("mp")
    gain_copy = pltpu.make_async_copy(gain_hbm, gain_ref, small.at[0])
    rank_copy = pltpu.make_async_copy(rank_hbm, rank_ref, small.at[1])
    rows_of = blocks_of(length)
    copies = [
        pltpu.make_async_copy(points_hbm.at[rows], points_ref.at[rows], large.at[i])
        for i, rows in enumerate(rows_of)
    ]
    gain_copy.start()
    for copy in copies:
        copy.start()
    rank_copy.start()
    gain_copy.wait()
    for copy, rows in zip(copies, rows_of):
        copy.wait()
        normed = normalise(points_ref[rows, :].astype(f32), gain_ref[...])
        half_ref[rows, :] = jnp.where(core == 0, normed[:, :half], normed[:, half:])
    rank_copy.wait()
    slot = slots(rank_ref[...], length, shards)

    place = lax.broadcasted_iota(jnp.int32, (TALL, LANES), 0)
    for i, rows in enumerate(blocks_of(length, TALL)):
        out_ref[rows, :] = dot(one_hot(place + i * TALL, slot), half_ref[...]).astype(bf16)


def order_for_owners(shards, rank_row, gain_row, points):
    length, features = points.shape
    return pl.pallas_call(
        functools.partial(send_kernel, shards),
        out_shape=jax.ShapeDtypeStruct((length, features // 2), bf16),
        in_specs=[ANYWHERE] * 3,
        out_specs=pl.BlockSpec(memory_space=pltpu.VMEM),
        scratch_shapes=[
            pltpu.VMEM((1, length), jnp.int32),
            pltpu.VMEM((1, features), f32),
            pltpu.VMEM((length, features), bf16),
            pltpu.VMEM((length, features // 2), bf16),
            pltpu.SemaphoreType.DMA((2,)),
            pltpu.SemaphoreType.DMA((length // ROWS,)),
        ],
        compiler_params=params(),
        cost_estimate=pl.CostEstimate(
            flops=length * length * features, bytes_accessed=4 * length * features, transcendentals=0
        ),
    )(rank_row, gain_row, points)


def attend_kernel(
    pair,
    staged,
    counts_ref,
    own,
    other,
    weight_hbm,
    out_hbm,
    w_ref,
    q_ref,
    k_ref,
    v_ref,
    out_ref,
    w_sems,
    out_sems,
    x_ref=None,
    x_sems=None,
):
    length = out_ref.shape[0]
    features = w_ref.shape[0]
    half = features // 2
    tiles = counts_ref.shape[1]
    core = lax.axis_index("mp")
    scale = math.log2(math.e) / math.sqrt(HDIM)

    copies = [
        pltpu.make_async_copy(
            weight_hbm.at[
                j, pl.ds(pl.multiple_of(at * half, half), half), pair * LANES : (pair + 1) * LANES
            ],
            w_ref.at[k * half : (k + 1) * half, j * LANES : (j + 1) * LANES],
            w_sems.at[2 * j + k],
        )
        for j in range(3)
        for k, at in enumerate((core, 1 - core))
    ]
    if not staged:
        copies += [
            pltpu.make_async_copy(source, x_ref.at[:, k * half : (k + 1) * half], x_sems.at[k])
            for k, source in enumerate((own, other))
        ]
    for copy in copies:
        copy.start()

    starts = [jnp.int32(0)]
    for t in range(tiles):
        starts.append(starts[-1] + counts_ref[0, t])
    lane = lax.broadcasted_iota(jnp.int32, (1, LANES), 1)
    first = jnp.full((1, LANES), length, jnp.int32)
    last = jnp.zeros((1, LANES), jnp.int32)
    for t in range(tiles):
        first = jnp.where(lane == HDIM + t, starts[t], first)
        last = jnp.where(lane == HDIM + t, starts[t + 1], last)
    flags = jnp.logical_and(lane >= HDIM, lane < HDIM + tiles)
    low_lanes = lane < HDIM

    for copy in copies:
        copy.wait()

    def project(i, carry):
        rows = pl.ds(pl.multiple_of(i * TALL, TALL), TALL)
        if staged:
            spread = dot(own[rows, :], w_ref[:half, :]) + dot(other[rows, :], w_ref[half:, :])
        else:
            spread = dot(x_ref[rows, :], w_ref[...])
        q, k, v = (spread[:, j * LANES : (j + 1) * LANES] for j in range(3))
        q = q * scale
        place = lax.broadcasted_iota(jnp.int32, (TALL, LANES), 0) + i * TALL
        inside = jnp.logical_and(place >= first, place < last)
        q_flag = jnp.where(inside, 1.0, 0.0)
        k_flag = jnp.where(jnp.logical_and(flags, jnp.logical_not(inside)), -FAR, 0.0)
        q_ref[0, rows, :] = jnp.where(low_lanes, q, q_flag).astype(bf16)
        q_ref[1, rows, :] = jnp.where(low_lanes, pltpu.roll(q, HDIM, 1), q_flag).astype(bf16)
        k_ref[0, rows, :] = jnp.where(low_lanes, k, k_flag).astype(bf16)
        k_ref[1, rows, :] = jnp.where(low_lanes, pltpu.roll(k, HDIM, 1), k_flag).astype(bf16)
        v_ref[0, rows, :] = jnp.where(low_lanes, v, 1.0).astype(bf16)
        v_ref[1, rows, :] = jnp.where(low_lanes, 1.0, v).astype(bf16)
        return carry

    lax.fori_loop(0, length // TALL, project, 0)

    def raise_scores(scores):
        return jnp.exp2(scores - jnp.max(scores, axis=1, keepdims=True)).astype(bf16)

    def send_out(i):
        rows = pl.ds(pl.multiple_of(i * TALL, TALL), TALL)
        return pltpu.make_async_copy(out_ref.at[rows], out_hbm.at[rows], out_sems.at[i])

    def query_block(i, carry):
        begin = i * TALL
        rows = pl.ds(pl.multiple_of(begin, TALL), TALL)
        low, high = jnp.int32(0), jnp.int32(length)
        for t in range(tiles):
            low = jnp.where(starts[t] <= begin, starts[t], low)
            end = starts[tiles - t]
            high = jnp.where(end >= begin + TALL, end, high)
        low = (low // 16) * 16
        blocks = (high - low + KEYS - 1) // KEYS
        for n in range(TALL // KEYS, length // KEYS + 1):

            @pl.when(blocks == n)
            def _(n=n):
                start = jnp.minimum(low, length - n * KEYS)
                keys = pl.ds(pl.multiple_of(start, 16), n * KEYS)
                scores = [
                    lax.dot_general(
                        q_ref[h, rows, :],
                        k_ref[h, keys, :],
                        (((1,), (1,)), ((), ())),
                        preferred_element_type=f32,
                    )
                    for h in range(2)
                ]
                even = dot(raise_scores(scores[0]), v_ref[0, keys, :])
                odd = dot(raise_scores(scores[1]), v_ref[1, keys, :])
                total = pltpu.roll(jnp.where(low_lanes, odd, even), HDIM, 1)
                out_ref[rows, :] = (jnp.where(low_lanes, even, odd) / total).astype(bf16)

        send_out(i).start()
        return carry

    lax.fori_loop(0, length // TALL, query_block, 0)
    for i in range(length // TALL):
        send_out(i).wait()


def attend(pair, staged, counts, own, other, w_qkv):
    length, half = own.shape
    features = 2 * half
    held = pl.BlockSpec(memory_space=pltpu.VMEM) if staged else ANYWHERE
    scratch = [
        pltpu.VMEM((features, 3 * LANES), bf16),
        pltpu.VMEM((2, length, LANES), bf16),
        pltpu.VMEM((2, length, LANES), bf16),
        pltpu.VMEM((2, length, LANES), bf16),
        pltpu.VMEM((length, LANES), bf16),
        pltpu.SemaphoreType.DMA((6,)),
        pltpu.SemaphoreType.DMA((length // TALL,)),
    ]
    if not staged:
        scratch += [pltpu.VMEM((length, features), bf16), pltpu.SemaphoreType.DMA((2,))]
    return pl.pallas_call(
        functools.partial(attend_kernel, pair, staged),
        out_shape=jax.ShapeDtypeStruct((length, LANES), bf16),
        in_specs=[SCALARS, held, held, ANYWHERE],
        out_specs=ANYWHERE,
        scratch_shapes=scratch,
        compiler_params=params(SMALL_BYTES if staged else VMEM_BYTES),
        cost_estimate=pl.CostEstimate(
            flops=32 * length * length * HDIM, bytes_accessed=8 * length * half, transcendentals=2 * length * length
        ),
    )(counts, own, other, w_qkv)


def unorder(rank_ref, start, rows, length, shards, context_ref):
    slot = slots(rank_ref[:, pl.ds(start, rows)], length, shards)
    slot = jnp.transpose(jnp.broadcast_to(slot, (LANES, rows)))
    place = lax.broadcasted_iota(jnp.int32, (1, length), 1)
    return dot(one_hot(slot, place), context_ref[...]).astype(bf16)


def unorder_kernel(shards, rank_hbm, own_hbm, other_hbm, out_ref, rank_ref, context_ref, sems):
    length = context_ref.shape[0]
    half_rows = out_ref.shape[0]
    base = lax.axis_index("mp") * half_rows
    copies = [
        pltpu.make_async_copy(rank_hbm, rank_ref, sems.at[0]),
        pltpu.make_async_copy(own_hbm, context_ref.at[:, :LANES], sems.at[1]),
        pltpu.make_async_copy(other_hbm, context_ref.at[:, LANES:], sems.at[2]),
    ]
    for copy in copies:
        copy.start()
    for copy in copies:
        copy.wait()
    for i, rows in enumerate(blocks_of(half_rows, TALL)):
        start = pl.multiple_of(base + i * TALL, TALL)
        out_ref[rows, :] = unorder(rank_ref, start, TALL, length, shards, context_ref)


def unorder_pair(shards, rank_row, own, other):
    length = own.shape[0]
    half_rows = length // 2
    return pl.pallas_call(
        functools.partial(unorder_kernel, shards),
        out_shape=jax.ShapeDtypeStruct((half_rows, 2 * LANES), bf16),
        in_specs=[ANYWHERE] * 3,
        out_specs=pl.BlockSpec(memory_space=pltpu.VMEM),
        scratch_shapes=[
            pltpu.VMEM((1, length), jnp.int32),
            pltpu.VMEM((length, 2 * LANES), bf16),
            pltpu.SemaphoreType.DMA((3,)),
        ],
        compiler_params=params(),
        cost_estimate=pl.CostEstimate(
            flops=4 * half_rows * length * LANES, bytes_accessed=8 * length * LANES, transcendentals=0
        ),
    )(rank_row, own, other)


def gelu_of_half(h):
    inner = 2 * math.sqrt(2 / math.pi)
    return h + h * jnp.tanh(h * (inner + (4 * 0.044715 * inner) * (h * h)))


def finish_kernel(
    shards,
    rank_hbm,
    gain_hbm,
    points_hbm,
    first_hbm,
    own_hbm,
    other_hbm,
    out_own_hbm,
    out_other_hbm,
    fc1_own_hbm,
    fc1_other_hbm,
    fc2_own_hbm,
    fc2_other_hbm,
    done_ref,
    whole_hbm,
    rank_ref,
    gain_ref,
    points_ref,
    first_ref,
    context_ref,
    out_ref,
    fc1_ref,
    fc2_ref,
    middle_ref,
    normed_ref,
    in_sems,
    sems,
):
    length = context_ref.shape[0]
    half_rows = done_ref.shape[0]
    base = pl.multiple_of(lax.axis_index("mp") * half_rows, half_rows)
    hidden_half = fc2_own_hbm.shape[0]
    early = [
        (rank_hbm, rank_ref),
        (own_hbm, context_ref.at[:, :LANES]),
        (other_hbm, context_ref.at[:, LANES:]),
    ]
    later = [(first_hbm, first_ref), (gain_hbm, gain_ref), (points_hbm.at[pl.ds(base, half_rows)], points_ref)]
    later += [
        (ref.at[pair * LANES : (pair + 1) * LANES], out_ref.at[(2 * pair + k) * LANES : (2 * pair + k + 1) * LANES])
        for pair in range(2)
        for k, ref in enumerate((out_own_hbm, out_other_hbm))
    ]
    last = [
        (fc1_own_hbm, fc1_ref.at[:, :hidden_half]),
        (fc1_other_hbm, fc1_ref.at[:, hidden_half:]),
        (fc2_own_hbm, fc2_ref.at[:hidden_half]),
        (fc2_other_hbm, fc2_ref.at[hidden_half:]),
    ]
    copies = [pltpu.make_async_copy(*ends, in_sems.at[k]) for k, ends in enumerate(early + later + last)]
    early, later, last = copies[:3], copies[3:10], copies[10:]
    for copy in copies:
        copy.start()

    blocks = blocks_of(half_rows, TALL)
    for copy in early:
        copy.wait()
    for i, rows in enumerate(blocks):
        start = pl.multiple_of(base + i * TALL, TALL)
        second = unorder(rank_ref, start, TALL, length, shards, context_ref)
        if i == 0:
            for copy in later:
                copy.wait()
        split_at = 2 * LANES
        attn_out = dot(first_ref[rows, :], out_ref[:split_at, :]) + dot(second, out_ref[split_at:, :])
        middle = (points_ref[rows, :].astype(f32) + attn_out.astype(bf16).astype(f32)).astype(bf16)
        middle_ref[rows, :] = middle
        normed_ref[rows, :] = normalise(middle.astype(f32), gain_ref[...]) * 0.5
    for copy in last:
        copy.wait()

    def away(i):
        here = pl.ds(pl.multiple_of(i * TALL, TALL), TALL)
        there = pl.ds(pl.multiple_of(base + i * TALL, TALL), TALL)
        return pltpu.make_async_copy(done_ref.at[here], whole_hbm.at[there], sems.at[i])

    chunks = blocks_of(2 * hidden_half, TALL)

    def mlp(i, carry):
        here = pl.ds(pl.multiple_of(i * TALL, TALL), TALL)
        normed = normed_ref[here, :]
        total = middle_ref[here, :].astype(f32)
        half_hidden = dot(normed, fc1_ref[:, chunks[0]])
        for k, chunk in enumerate(chunks):
            ahead = dot(normed, fc1_ref[:, chunks[k + 1]]) if k + 1 < len(chunks) else None
            total = total + dot(gelu_of_half(half_hidden).astype(bf16), fc2_ref[chunk, :])
            half_hidden = ahead
        done_ref[here, :] = total.astype(bf16)
        away(i).start()
        return carry

    lax.fori_loop(0, half_rows // TALL, mlp, 0)
    for i in range(half_rows // TALL):
        away(i).wait()


def finish(shards, rank_row, gain_row, points, *arrays):
    length, features = points.shape
    half_rows = length // 2
    hidden = 2 * arrays[-1].shape[0]
    return pl.pallas_call(
        functools.partial(finish_kernel, shards),
        out_shape=(
            jax.ShapeDtypeStruct((half_rows, features), bf16),
            jax.ShapeDtypeStruct((length, features), bf16),
        ),
        in_specs=[ANYWHERE] * 12,
        out_specs=(pl.BlockSpec(memory_space=pltpu.VMEM), ANYWHERE),
        scratch_shapes=[
            pltpu.VMEM((1, length), jnp.int32),
            pltpu.VMEM((1, features), f32),
            pltpu.VMEM((half_rows, features), bf16),
            pltpu.VMEM((half_rows, 2 * LANES), bf16),
            pltpu.VMEM((length, 2 * LANES), bf16),
            pltpu.VMEM((features, features), bf16),
            pltpu.VMEM((features, hidden), bf16),
            pltpu.VMEM((hidden, features), bf16),
            pltpu.VMEM((half_rows, features), bf16),
            pltpu.VMEM((half_rows, features), bf16),
            pltpu.SemaphoreType.DMA((14,)),
            pltpu.SemaphoreType.DMA((half_rows // TALL,)),
        ],
        compiler_params=params(),
        cost_estimate=pl.CostEstimate(
            flops=2 * half_rows * features * (length + 9 * features),
            bytes_accessed=16 * length * features,
            transcendentals=half_rows * 4 * features,
        ),
    )(rank_row, gain_row, points, *arrays)


def across(values):
    return lax.ppermute(values, "mp", [(0, 1), (1, 0)])


def exchange(rows, shards):
    length, columns = rows.shape
    cells = rows.reshape(shards, length // shards, columns)
    return lax.all_to_all(cells, "space", split_axis=0, concat_axis=0, tiled=True).reshape(length, columns)


def body(points, curve_rank, patch_counts, norm_gain_attn, w_qkv, w_out, norm_gain_mlp, w_fc1, w_fc2):
    shards = lax.axis_size("space")
    length, features = points.shape
    rank_row = curve_rank.reshape(1, length)
    own = exchange(order_for_owners(shards, rank_row, norm_gain_attn.reshape(1, features), points), shards)
    swapped = across(w_fc1), across(w_fc2), across(w_out)
    other = across(own)
    first_own = exchange(attend(0, True, patch_counts, own, other, w_qkv), shards)
    counts, (other_fc1, other_fc2, other_out) = lax.optimization_barrier((patch_counts, swapped))
    second_own = exchange(attend(1, False, counts, own, other, w_qkv), shards)
    first = unorder_pair(shards, rank_row, first_own, across(first_own))
    second_own, first = lax.optimization_barrier((second_own, first))
    done, whole = finish(
        shards,
        rank_row,
        norm_gain_mlp.reshape(1, features),
        points,
        first,
        second_own,
        across(second_own),
        w_out,
        other_out,
        w_fc1,
        other_fc1,
        w_fc2,
        other_fc2,
    )
    start = (1 - lax.axis_index("mp")) * (length // 2)
    return lax.dynamic_update_slice(whole, across(done), (start, 0))


def solution(mesh):
    placed = (
        P("space", None),
        P("space"),
        P("space", None),
        P(),
        P(None, None, "mp"),
        P("mp", None),
        P(),
        P(None, "mp"),
        P("mp", None),
    )
    return jax.shard_map(
        body, mesh=mesh, in_specs=placed, out_specs=P("space", None), check_vma=False
    )
```

```python
import functools
import math

import jax
import jax.numpy as jnp
from jax import lax
from jax.experimental import pallas as pl
from jax.experimental.pallas import tpu as pltpu
from jax.sharding import PartitionSpec as P

HDIM = 64
LANES = 128
ROWS = 256
TALL = 512
KEYS = 256
MOST_PIECES = 16
EPSILON = 1e-06
FAR = 1e30
VMEM_BYTES = 58 * 1024 * 1024
SMALL_BYTES = 30 * 1024 * 1024

f32 = jnp.float32
bf16 = jnp.bfloat16

ANYWHERE = pl.BlockSpec(memory_space=pl.ANY)
SCALARS = pl.BlockSpec(memory_space=pltpu.SMEM)


def normalise(values, gain_row):
    average = jnp.mean(values, axis=-1, keepdims=True)
    centred = values - average
    second = jnp.mean(centred * centred, axis=-1, keepdims=True)
    return (centred * lax.rsqrt(second + EPSILON) * gain_row).astype(bf16)


def dot(left, right):
    return jnp.dot(left, right, preferred_element_type=f32)


def split(number, size):
    if size & (size - 1) == 0:
        return number >> (size.bit_length() - 1), number & (size - 1)
    return number // size, number % size


def slots(rank, length, shards, relative=False):
    cell = length // shards
    owner, within = split(rank, length)
    own_index = lax.axis_index("space")
    within = within - own_index * cell
    if relative:
        owner = owner - own_index
        owner = jnp.where(owner < 0, owner + shards, owner)
    return owner * cell + within


def piece_start(length, count, step):
    if count == 1:
        return 0
    cell = length // count
    return pl.multiple_of(lax.rem(lax.axis_index("space") + count + step, count) * cell, cell)


def one_hot(rows_at, columns_at):
    if columns_at.shape[1] <= 1 << 15:
        rows_at, columns_at = rows_at.astype(jnp.int16), columns_at.astype(jnp.int16)
    one, nil = jnp.ones((), bf16), jnp.zeros((), bf16)
    return jnp.concatenate(
        [
            jnp.where(rows_at == columns_at[:, k : k + LANES], one, nil)
            for k in range(0, columns_at.shape[1], LANES)
        ],
        axis=1,
    )


def blocks_of(length, rows=ROWS):
    return [slice(i * rows, (i + 1) * rows) for i in range(length // rows)]


def params(limit=VMEM_BYTES):
    return pltpu.CompilerParams(vmem_limit_bytes=limit)


def send_kernel(shards, count, rank_hbm, gain_hbm, points_hbm, *refs):
    pieces_hbm = refs[:count]
    rank_ref, gain_ref, points_ref, half_ref, out_ref, small, large, away = refs[count:]
    length, features = points_ref.shape
    half = features // 2
    cell = length // count
    core = lax.axis_index("mp")
    gain_copy = pltpu.make_async_copy(gain_hbm, gain_ref, small.at[0])
    rank_copy = pltpu.make_async_copy(rank_hbm, rank_ref, small.at[1])
    rows_of = blocks_of(length)
    copies = [
        pltpu.make_async_copy(points_hbm.at[rows], points_ref.at[rows], large.at[i])
        for i, rows in enumerate(rows_of)
    ]
    gain_copy.start()
    for copy in copies:
        copy.start()
    rank_copy.start()
    gain_copy.wait()
    for copy, rows in zip(copies, rows_of):
        copy.wait()
        normed = normalise(points_ref[rows, :].astype(f32), gain_ref[...])
        half_ref[rows, :] = jnp.where(core == 0, normed[:, :half], normed[:, half:])
    rank_copy.wait()
    slot = slots(rank_ref[...], length, shards, relative=count > 1)

    place = lax.broadcasted_iota(jnp.int32, (TALL, LANES), 0)
    sends = [
        pltpu.make_async_copy(out_ref.at[s * cell : (s + 1) * cell], pieces_hbm[s], away.at[s]) for s in range(count)
    ]
    sent = 0
    for i, rows in enumerate(blocks_of(length, TALL)):
        out_ref[rows, :] = dot(one_hot(place + i * TALL, slot), half_ref[...]).astype(bf16)
        while sent < count and (sent + 1) * cell <= (i + 1) * TALL:
            sends[sent].start()
            sent += 1
    for send in sends:
        send.wait()


def order_for_owners(shards, count, rank_row, gain_row, points):
    length, features = points.shape
    return pl.pallas_call(
        functools.partial(send_kernel, shards, count),
        out_shape=[jax.ShapeDtypeStruct((length // count, features // 2), bf16)] * count,
        in_specs=[ANYWHERE] * 3,
        out_specs=[ANYWHERE] * count,
        scratch_shapes=[
            pltpu.VMEM((1, length), jnp.int32),
            pltpu.VMEM((1, features), f32),
            pltpu.VMEM((length, features), bf16),
            pltpu.VMEM((length, features // 2), bf16),
            pltpu.VMEM((length, features // 2), bf16),
            pltpu.SemaphoreType.DMA((2,)),
            pltpu.SemaphoreType.DMA((length // ROWS,)),
            pltpu.SemaphoreType.DMA((count,)),
        ],
        compiler_params=params(),
        cost_estimate=pl.CostEstimate(
            flops=length * length * features, bytes_accessed=4 * length * features, transcendentals=0
        ),
    )(rank_row, gain_row, points)


def attend_kernel(pair, staged, count, counts_ref, *refs):
    own, other, weight_hbm = refs[:count], refs[count : 2 * count], refs[2 * count]
    pieces_hbm = refs[2 * count + 1 : 3 * count + 1]
    w_ref, q_ref, k_ref, v_ref, out_ref, w_sems, out_sems = refs[3 * count + 1 : 3 * count + 8]
    x_ref, x_sems = (None, None) if staged else refs[3 * count + 8 :]
    length = out_ref.shape[0]
    features = w_ref.shape[0]
    half = features // 2
    cell = length // count
    tiles = counts_ref.shape[1]
    core = lax.axis_index("mp")
    scale = math.log2(math.e) / math.sqrt(HDIM)

    copies = [
        pltpu.make_async_copy(
            weight_hbm.at[
                j, pl.ds(pl.multiple_of(at * half, half), half), pair * LANES : (pair + 1) * LANES
            ],
            w_ref.at[k * half : (k + 1) * half, j * LANES : (j + 1) * LANES],
            w_sems.at[2 * j + k],
        )
        for j in range(3)
        for k, at in enumerate((core, 1 - core))
    ]
    if not staged:
        copies += [
            pltpu.make_async_copy(
                source[p], x_ref.at[p * cell : (p + 1) * cell, k * half : (k + 1) * half], x_sems.at[2 * p + k]
            )
            for p in range(count)
            for k, source in enumerate((own, other))
        ]
    for copy in copies:
        copy.start()

    starts = [jnp.int32(0)]
    for t in range(tiles):
        starts.append(starts[-1] + counts_ref[0, t])
    lane = lax.broadcasted_iota(jnp.int32, (1, LANES), 1)
    first = jnp.full((1, LANES), length, jnp.int32)
    last = jnp.zeros((1, LANES), jnp.int32)
    for t in range(tiles):
        first = jnp.where(lane == HDIM + t, starts[t], first)
        last = jnp.where(lane == HDIM + t, starts[t + 1], last)
    flags = jnp.logical_and(lane >= HDIM, lane < HDIM + tiles)
    low_lanes = lane < HDIM

    for copy in copies:
        copy.wait()

    unit = min(cell, TALL)

    def rows_of(source, i):
        if count == 1:
            return source[0][i * TALL : (i + 1) * TALL, :]
        first_piece = i * TALL // cell
        return jnp.concatenate([source[p][...] for p in range(first_piece, first_piece + TALL // cell)], axis=0)

    for i in range(length // TALL):
        if staged:
            spread = dot(rows_of(own, i), w_ref[:half, :]) + dot(rows_of(other, i), w_ref[half:, :])
        else:
            spread = dot(x_ref[i * TALL : (i + 1) * TALL, :], w_ref[...])
        for u in range(TALL // unit):
            q, k, v = (spread[u * unit : (u + 1) * unit, j * LANES : (j + 1) * LANES] for j in range(3))
            q = q * scale
            at = i * TALL if count == 1 else piece_start(length, count, -(i * TALL // cell + u))
            rows = pl.ds(at, unit)
            place = lax.broadcasted_iota(jnp.int32, (unit, LANES), 0) + at
            inside = jnp.logical_and(place >= first, place < last)
            q_flag = jnp.where(inside, 1.0, 0.0)
            k_flag = jnp.where(jnp.logical_and(flags, jnp.logical_not(inside)), -FAR, 0.0)
            q_ref[0, rows, :] = jnp.where(low_lanes, q, q_flag).astype(bf16)
            q_ref[1, rows, :] = jnp.where(low_lanes, pltpu.roll(q, HDIM, 1), q_flag).astype(bf16)
            k_ref[0, rows, :] = jnp.where(low_lanes, k, k_flag).astype(bf16)
            k_ref[1, rows, :] = jnp.where(low_lanes, pltpu.roll(k, HDIM, 1), k_flag).astype(bf16)
            v_ref[0, rows, :] = jnp.where(low_lanes, v, 1.0).astype(bf16)
            v_ref[1, rows, :] = jnp.where(low_lanes, 1.0, v).astype(bf16)

    def raise_scores(scores):
        return jnp.exp2(scores - jnp.max(scores, axis=1, keepdims=True)).astype(bf16)

    def query_block(i, carry):
        begin = i * TALL
        rows = pl.ds(pl.multiple_of(begin, TALL), TALL)
        low, high = jnp.int32(0), jnp.int32(length)
        for t in range(tiles):
            low = jnp.where(starts[t] <= begin, starts[t], low)
            end = starts[tiles - t]
            high = jnp.where(end >= begin + TALL, end, high)
        low = (low // 16) * 16
        blocks = (high - low + KEYS - 1) // KEYS
        for n in range(TALL // KEYS, length // KEYS + 1):

            @pl.when(blocks == n)
            def _(n=n):
                start = jnp.minimum(low, length - n * KEYS)
                keys = pl.ds(pl.multiple_of(start, 16), n * KEYS)
                scores = [
                    lax.dot_general(
                        q_ref[h, rows, :],
                        k_ref[h, keys, :],
                        (((1,), (1,)), ((), ())),
                        preferred_element_type=f32,
                    )
                    for h in range(2)
                ]
                even = dot(raise_scores(scores[0]), v_ref[0, keys, :])
                odd = dot(raise_scores(scores[1]), v_ref[1, keys, :])
                total = pltpu.roll(jnp.where(low_lanes, odd, even), HDIM, 1)
                out_ref[rows, :] = (jnp.where(low_lanes, even, odd) / total).astype(bf16)

        return carry

    lax.fori_loop(0, length // TALL, query_block, 0)
    sends = [
        pltpu.make_async_copy(
            out_ref.at[pl.ds(piece_start(length, count, p), cell)], pieces_hbm[p], out_sems.at[p]
        )
        for p in range(count)
    ]
    for send in sends:
        send.start()
    for send in sends:
        send.wait()


def attend(pair, staged, counts, own, other, w_qkv):
    count = len(own)
    cell, half = own[0].shape
    length = count * cell
    features = 2 * half
    held = pl.BlockSpec(memory_space=pltpu.VMEM) if staged else ANYWHERE
    scratch = [
        pltpu.VMEM((features, 3 * LANES), bf16),
        pltpu.VMEM((2, length, LANES), bf16),
        pltpu.VMEM((2, length, LANES), bf16),
        pltpu.VMEM((2, length, LANES), bf16),
        pltpu.VMEM((length, LANES), bf16),
        pltpu.SemaphoreType.DMA((6,)),
        pltpu.SemaphoreType.DMA((count,)),
    ]
    if not staged:
        scratch += [pltpu.VMEM((length, features), bf16), pltpu.SemaphoreType.DMA((2 * count,))]
    return pl.pallas_call(
        functools.partial(attend_kernel, pair, staged, count),
        out_shape=[jax.ShapeDtypeStruct((cell, LANES), bf16)] * count,
        in_specs=[SCALARS] + [held] * (2 * count) + [ANYWHERE],
        out_specs=[ANYWHERE] * count,
        scratch_shapes=scratch,
        compiler_params=params(SMALL_BYTES if staged else VMEM_BYTES),
        cost_estimate=pl.CostEstimate(
            flops=32 * length * length * HDIM, bytes_accessed=8 * length * half, transcendentals=2 * length * length
        ),
    )(counts, *own, *other, w_qkv)


def unorder(rank_ref, start, rows, length, shards, context_ref):
    slot = slots(rank_ref[:, pl.ds(start, rows)], length, shards)
    slot = jnp.transpose(jnp.broadcast_to(slot, (LANES, rows)))
    place = lax.broadcasted_iota(jnp.int32, (1, length), 1)
    return dot(one_hot(slot, place), context_ref[...]).astype(bf16)


def context_ends(own, other, context_ref):
    length, count = context_ref.shape[0], len(own)
    return [
        (source, context_ref.at[pl.ds(piece_start(length, count, -p), length // count), k * LANES : (k + 1) * LANES])
        for p in range(count)
        for k, source in enumerate((own[p], other[p]))
    ]


def unorder_kernel(shards, count, rank_hbm, *refs):
    own, other = refs[:count], refs[count : 2 * count]
    out_ref, rank_ref, context_ref, sems = refs[2 * count :]
    length = context_ref.shape[0]
    half_rows = out_ref.shape[0]
    base = lax.axis_index("mp") * half_rows
    ends = [(rank_hbm, rank_ref)] + context_ends(own, other, context_ref)
    copies = [pltpu.make_async_copy(*two, sems.at[k]) for k, two in enumerate(ends)]
    for copy in copies:
        copy.start()
    for copy in copies:
        copy.wait()
    for i, rows in enumerate(blocks_of(half_rows, TALL)):
        start = pl.multiple_of(base + i * TALL, TALL)
        out_ref[rows, :] = unorder(rank_ref, start, TALL, length, shards, context_ref)


def unorder_pair(shards, rank_row, own, other):
    length = rank_row.shape[1]
    count = len(own)
    half_rows = length // 2
    return pl.pallas_call(
        functools.partial(unorder_kernel, shards, count),
        out_shape=jax.ShapeDtypeStruct((half_rows, 2 * LANES), bf16),
        in_specs=[ANYWHERE] * (1 + 2 * count),
        out_specs=pl.BlockSpec(memory_space=pltpu.VMEM),
        scratch_shapes=[
            pltpu.VMEM((1, length), jnp.int32),
            pltpu.VMEM((length, 2 * LANES), bf16),
            pltpu.SemaphoreType.DMA((1 + 2 * count,)),
        ],
        compiler_params=params(),
        cost_estimate=pl.CostEstimate(
            flops=4 * half_rows * length * LANES, bytes_accessed=8 * length * LANES, transcendentals=0
        ),
    )(rank_row, *own, *other)


def gelu_of_half(h):
    inner = 2 * math.sqrt(2 / math.pi)
    return h + h * jnp.tanh(h * (inner + (4 * 0.044715 * inner) * (h * h)))


def finish_kernel(shards, count, *refs):
    own, other = refs[:count], refs[count : 2 * count]
    rank_hbm, gain_hbm, points_hbm, first_hbm, out_own_hbm, out_other_hbm = refs[2 * count : 2 * count + 6]
    fc1_own_hbm, fc1_other_hbm, fc2_own_hbm, fc2_other_hbm, done_ref, whole_hbm = refs[2 * count + 6 : 2 * count + 12]
    rank_ref, gain_ref, points_ref, first_ref, context_ref, out_ref = refs[2 * count + 12 : 2 * count + 18]
    fc1_ref, fc2_ref, middle_ref, normed_ref, in_sems, sems = refs[2 * count + 18 :]
    length = context_ref.shape[0]
    half_rows = done_ref.shape[0]
    base = pl.multiple_of(lax.axis_index("mp") * half_rows, half_rows)
    hidden_half = fc2_own_hbm.shape[0]
    early = [(rank_hbm, rank_ref)] + context_ends(own, other, context_ref)
    later = [(first_hbm, first_ref), (gain_hbm, gain_ref), (points_hbm.at[pl.ds(base, half_rows)], points_ref)]
    later += [
        (ref.at[pair * LANES : (pair + 1) * LANES], out_ref.at[(2 * pair + k) * LANES : (2 * pair + k + 1) * LANES])
        for pair in range(2)
        for k, ref in enumerate((out_own_hbm, out_other_hbm))
    ]
    last = [
        (fc1_own_hbm, fc1_ref.at[:, :hidden_half]),
        (fc1_other_hbm, fc1_ref.at[:, hidden_half:]),
        (fc2_own_hbm, fc2_ref.at[:hidden_half]),
        (fc2_other_hbm, fc2_ref.at[hidden_half:]),
    ]
    copies = [pltpu.make_async_copy(*ends, in_sems.at[k]) for k, ends in enumerate(early + later + last)]
    early, later, last = copies[: 1 + 2 * count], copies[1 + 2 * count : -4], copies[-4:]
    for copy in copies:
        copy.start()

    blocks = blocks_of(half_rows, TALL)
    for copy in early:
        copy.wait()
    for i, rows in enumerate(blocks):
        start = pl.multiple_of(base + i * TALL, TALL)
        second = unorder(rank_ref, start, TALL, length, shards, context_ref)
        if i == 0:
            for copy in later:
                copy.wait()
        split_at = 2 * LANES
        attn_out = dot(first_ref[rows, :], out_ref[:split_at, :]) + dot(second, out_ref[split_at:, :])
        middle = (points_ref[rows, :].astype(f32) + attn_out.astype(bf16).astype(f32)).astype(bf16)
        middle_ref[rows, :] = middle
        normed_ref[rows, :] = normalise(middle.astype(f32), gain_ref[...]) * 0.5
    for copy in last:
        copy.wait()

    def away(i):
        here = pl.ds(pl.multiple_of(i * TALL, TALL), TALL)
        there = pl.ds(pl.multiple_of(base + i * TALL, TALL), TALL)
        return pltpu.make_async_copy(done_ref.at[here], whole_hbm.at[there], sems.at[i])

    chunks = blocks_of(2 * hidden_half, TALL)

    def mlp(i, carry):
        here = pl.ds(pl.multiple_of(i * TALL, TALL), TALL)
        normed = normed_ref[here, :]
        total = middle_ref[here, :].astype(f32)
        half_hidden = dot(normed, fc1_ref[:, chunks[0]])
        for k, chunk in enumerate(chunks):
            ahead = dot(normed, fc1_ref[:, chunks[k + 1]]) if k + 1 < len(chunks) else None
            total = total + dot(gelu_of_half(half_hidden).astype(bf16), fc2_ref[chunk, :])
            half_hidden = ahead
        done_ref[here, :] = total.astype(bf16)
        away(i).start()
        return carry

    lax.fori_loop(0, half_rows // TALL, mlp, 0)
    for i in range(half_rows // TALL):
        away(i).wait()


def finish(shards, own, other, rank_row, gain_row, points, *arrays):
    length, features = points.shape
    count = len(own)
    half_rows = length // 2
    hidden = 2 * arrays[-1].shape[0]
    return pl.pallas_call(
        functools.partial(finish_kernel, shards, count),
        out_shape=(
            jax.ShapeDtypeStruct((half_rows, features), bf16),
            jax.ShapeDtypeStruct((length, features), bf16),
        ),
        in_specs=[ANYWHERE] * (2 * count + 10),
        out_specs=(pl.BlockSpec(memory_space=pltpu.VMEM), ANYWHERE),
        scratch_shapes=[
            pltpu.VMEM((1, length), jnp.int32),
            pltpu.VMEM((1, features), f32),
            pltpu.VMEM((half_rows, features), bf16),
            pltpu.VMEM((half_rows, 2 * LANES), bf16),
            pltpu.VMEM((length, 2 * LANES), bf16),
            pltpu.VMEM((features, features), bf16),
            pltpu.VMEM((features, hidden), bf16),
            pltpu.VMEM((hidden, features), bf16),
            pltpu.VMEM((half_rows, features), bf16),
            pltpu.VMEM((half_rows, features), bf16),
            pltpu.SemaphoreType.DMA((2 * count + 12,)),
            pltpu.SemaphoreType.DMA((half_rows // TALL,)),
        ],
        compiler_params=params(),
        cost_estimate=pl.CostEstimate(
            flops=2 * half_rows * features * (length + 9 * features),
            bytes_accessed=16 * length * features,
            transcendentals=half_rows * 4 * features,
        ),
    )(*own, *other, rank_row, gain_row, points, *arrays)


def across(values):
    return lax.ppermute(values, "mp", [(0, 1), (1, 0)])


def exchange(pieces, shards):
    if len(pieces) == 1:
        length, columns = pieces[0].shape
        cells = pieces[0].reshape(shards, length // shards, columns)
        return [lax.all_to_all(cells, "space", split_axis=0, concat_axis=0, tiled=True).reshape(length, columns)]
    return [
        lax.ppermute(piece, "space", [(i, (i + p) % shards) for i in range(shards)]) if p else piece
        for p, piece in enumerate(pieces)
    ]


def body(points, curve_rank, patch_counts, norm_gain_attn, w_qkv, w_out, norm_gain_mlp, w_fc1, w_fc2):
    shards = lax.axis_size("space")
    length, features = points.shape
    count = shards if shards <= MOST_PIECES else 1
    rank_row = curve_rank.reshape(1, length)
    own = exchange(order_for_owners(shards, count, rank_row, norm_gain_attn.reshape(1, features), points), shards)
    swapped = across(w_fc1), across(w_fc2), across(w_out)
    other = [across(piece) for piece in own]
    first_own = exchange(attend(0, True, patch_counts, own, other, w_qkv), shards)
    counts, (other_fc1, other_fc2, other_out) = lax.optimization_barrier((patch_counts, swapped))
    second_own = exchange(attend(1, False, counts, own, other, w_qkv), shards)
    first = unorder_pair(shards, rank_row, first_own, [across(piece) for piece in first_own])
    second_own, first = lax.optimization_barrier((second_own, first))
    done, whole = finish(
        shards,
        second_own,
        [across(piece) for piece in second_own],
        rank_row,
        norm_gain_mlp.reshape(1, features),
        points,
        first,
        w_out,
        other_out,
        w_fc1,
        other_fc1,
        w_fc2,
        other_fc2,
    )
    start = (1 - lax.axis_index("mp")) * (length // 2)
    return lax.dynamic_update_slice(whole, across(done), (start, 0))


def solution(mesh):
    placed = (
        P("space", None),
        P("space"),
        P("space", None),
        P(),
        P(None, None, "mp"),
        P("mp", None),
        P(),
        P(None, "mp"),
        P("mp", None),
    )
    return jax.shard_map(
        body, mesh=mesh, in_specs=placed, out_specs=P("space", None), check_vma=False
    )
```

```python
import functools
import math

import jax
import jax.numpy as jnp
from jax import lax
from jax.experimental import pallas as pl
from jax.experimental.pallas import tpu as pltpu
from jax.sharding import PartitionSpec as P

HDIM = 64
LANES = 128
ROWS = 256
TALL = 512
KEYS = 256
EPSILON = 1e-06
FAR = 1e30
SAFE = 95.0
VMEM_BYTES = 58 * 1024 * 1024
SMALL_BYTES = 30 * 1024 * 1024

f32 = jnp.float32
bf16 = jnp.bfloat16

ANYWHERE = pl.BlockSpec(memory_space=pl.ANY)
SCALARS = pl.BlockSpec(memory_space=pltpu.SMEM)


def normalise(values, gain_row):
    average = jnp.mean(values, axis=-1, keepdims=True)
    centred = values - average
    second = jnp.mean(centred * centred, axis=-1, keepdims=True)
    return (centred * lax.rsqrt(second + EPSILON) * gain_row).astype(bf16)


def dot(left, right):
    return jnp.dot(left, right, preferred_element_type=f32)


def split(number, size):
    if size & (size - 1) == 0:
        return number >> (size.bit_length() - 1), number & (size - 1)
    return number // size, number % size


def slots(rank, length, shards):
    cell = length // shards
    owner, within = split(rank, length)
    return owner * cell + within - lax.axis_index("space") * cell


def one_hot(rows_at, columns_at):
    if columns_at.shape[1] <= 1 << 15:
        rows_at, columns_at = rows_at.astype(jnp.int16), columns_at.astype(jnp.int16)
    one, nil = jnp.ones((), bf16), jnp.zeros((), bf16)
    return jnp.concatenate(
        [
            jnp.where(rows_at == columns_at[:, k : k + LANES], one, nil)
            for k in range(0, columns_at.shape[1], LANES)
        ],
        axis=1,
    )


def blocks_of(length, rows=ROWS):
    return [slice(i * rows, (i + 1) * rows) for i in range(length // rows)]


def params(limit=VMEM_BYTES):
    return pltpu.CompilerParams(vmem_limit_bytes=limit)


def send_kernel(shards, rank_hbm, gain_hbm, points_hbm, out_ref, rank_ref, gain_ref, points_ref, half_ref, small, large):
    length, features = points_ref.shape
    half = features // 2
    core = lax.axis_index("mp")
    gain_copy = pltpu.make_async_copy(gain_hbm, gain_ref, small.at[0])
    rank_copy = pltpu.make_async_copy(rank_hbm, rank_ref, small.at[1])
    rows_of = blocks_of(length)
    copies = [
        pltpu.make_async_copy(points_hbm.at[rows], points_ref.at[rows], large.at[i])
        for i, rows in enumerate(rows_of)
    ]
    gain_copy.start()
    for copy in copies:
        copy.start()
    rank_copy.start()
    gain_copy.wait()
    for copy, rows in zip(copies, rows_of):
        copy.wait()
        normed = normalise(points_ref[rows, :].astype(f32), gain_ref[...])
        half_ref[rows, :] = jnp.where(core == 0, normed[:, :half], normed[:, half:])
    rank_copy.wait()
    slot = slots(rank_ref[...], length, shards)

    place = lax.broadcasted_iota(jnp.int32, (TALL, LANES), 0)
    for i, rows in enumerate(blocks_of(length, TALL)):
        out_ref[rows, :] = dot(one_hot(place + i * TALL, slot), half_ref[...]).astype(bf16)


def order_for_owners(shards, rank_row, gain_row, points):
    length, features = points.shape
    return pl.pallas_call(
        functools.partial(send_kernel, shards),
        out_shape=jax.ShapeDtypeStruct((length, features // 2), bf16),
        in_specs=[ANYWHERE] * 3,
        out_specs=pl.BlockSpec(memory_space=pltpu.VMEM),
        scratch_shapes=[
            pltpu.VMEM((1, length), jnp.int32),
            pltpu.VMEM((1, features), f32),
            pltpu.VMEM((length, features), bf16),
            pltpu.VMEM((length, features // 2), bf16),
            pltpu.SemaphoreType.DMA((2,)),
            pltpu.SemaphoreType.DMA((length // ROWS,)),
        ],
        compiler_params=params(),
        cost_estimate=pl.CostEstimate(
            flops=length * length * features, bytes_accessed=4 * length * features, transcendentals=0
        ),
    )(rank_row, gain_row, points)


def attend_kernel(
    pair,
    staged,
    counts_ref,
    own,
    other,
    weight_hbm,
    out_hbm,
    w_ref,
    q_ref,
    k_ref,
    v_ref,
    out_ref,
    q_most,
    k_most,
    w_sems,
    out_sems,
    x_ref=None,
    x_sems=None,
):
    length = out_ref.shape[0]
    features = w_ref.shape[0]
    half = features // 2
    tiles = counts_ref.shape[1]
    core = lax.axis_index("mp")
    scale = math.log2(math.e) / math.sqrt(HDIM)

    copies = [
        pltpu.make_async_copy(
            weight_hbm.at[
                j, pl.ds(pl.multiple_of(at * half, half), half), pair * LANES : (pair + 1) * LANES
            ],
            w_ref.at[k * half : (k + 1) * half, j * LANES : (j + 1) * LANES],
            w_sems.at[2 * j + k],
        )
        for j in range(3)
        for k, at in enumerate((core, 1 - core))
    ]
    if not staged:
        copies += [
            pltpu.make_async_copy(source, x_ref.at[:, k * half : (k + 1) * half], x_sems.at[k])
            for k, source in enumerate((own, other))
        ]
    for copy in copies:
        copy.start()

    starts = [jnp.int32(0)]
    for t in range(tiles):
        starts.append(starts[-1] + counts_ref[0, t])
    lane = lax.broadcasted_iota(jnp.int32, (1, LANES), 1)
    first = jnp.full((1, LANES), length, jnp.int32)
    last = jnp.zeros((1, LANES), jnp.int32)
    for t in range(tiles):
        first = jnp.where(lane == HDIM + t, starts[t], first)
        last = jnp.where(lane == HDIM + t, starts[t + 1], last)
    flags = jnp.logical_and(lane >= HDIM, lane < HDIM + tiles)
    low_lanes = lane < HDIM

    for copy in copies:
        copy.wait()

    row_head = lax.broadcasted_iota(jnp.int32, (LANES, LANES), 0) < HDIM
    column_head = lax.broadcasted_iota(jnp.int32, (LANES, LANES), 1) < HDIM
    sum_head = jnp.where(row_head == column_head, 1.0, 0.0).astype(bf16)

    def most(values):
        return jnp.max(dot((values * values).astype(bf16), sum_head), axis=0, keepdims=True)

    q_most[...] = jnp.zeros_like(q_most)
    k_most[...] = jnp.zeros_like(k_most)

    def project(i, carry):
        rows = pl.ds(pl.multiple_of(i * TALL, TALL), TALL)
        if staged:
            spread = dot(own[rows, :], w_ref[:half, :]) + dot(other[rows, :], w_ref[half:, :])
        else:
            spread = dot(x_ref[rows, :], w_ref[...])
        q, k, v = (spread[:, j * LANES : (j + 1) * LANES] for j in range(3))
        q = q * scale
        q_most[...] = jnp.maximum(q_most[...], most(q))
        k_most[...] = jnp.maximum(k_most[...], most(k))
        place = lax.broadcasted_iota(jnp.int32, (TALL, LANES), 0) + i * TALL
        inside = jnp.logical_and(place >= first, place < last)
        q_flag = jnp.where(inside, 1.0, 0.0)
        k_flag = jnp.where(jnp.logical_and(flags, jnp.logical_not(inside)), -FAR, 0.0)
        q_ref[0, rows, :] = jnp.where(low_lanes, q, q_flag).astype(bf16)
        q_ref[1, rows, :] = jnp.where(low_lanes, pltpu.roll(q, HDIM, 1), q_flag).astype(bf16)
        k_ref[0, rows, :] = jnp.where(low_lanes, k, k_flag).astype(bf16)
        k_ref[1, rows, :] = jnp.where(low_lanes, pltpu.roll(k, HDIM, 1), k_flag).astype(bf16)
        v_ref[0, rows, :] = jnp.where(low_lanes, v, 1.0).astype(bf16)
        v_ref[1, rows, :] = jnp.where(low_lanes, 1.0, v).astype(bf16)
        return carry

    lax.fori_loop(0, length // TALL, project, 0)
    safe = jnp.max(q_most[...] * k_most[...]) < SAFE * SAFE

    def one_head(h, rows, keys, shifted):
        scores = lax.dot_general(
            q_ref[h, rows, :], k_ref[h, keys, :], (((1,), (1,)), ((), ())), preferred_element_type=f32
        )
        if shifted:
            scores = scores - jnp.max(scores, axis=1, keepdims=True)
        return dot(jnp.exp2(scores).astype(bf16), v_ref[h, keys, :])

    def both_heads(rows, keys, shifted):
        even, odd = (one_head(h, rows, keys, shifted) for h in range(2))
        total = pltpu.roll(jnp.where(low_lanes, odd, even), HDIM, 1)
        out_ref[rows, :] = (jnp.where(low_lanes, even, odd) / total).astype(bf16)

    def send_out(i):
        rows = pl.ds(pl.multiple_of(i * TALL, TALL), TALL)
        return pltpu.make_async_copy(out_ref.at[rows], out_hbm.at[rows], out_sems.at[i])

    def query_block(i, carry):
        begin = i * TALL
        rows = pl.ds(pl.multiple_of(begin, TALL), TALL)
        low, high = jnp.int32(0), jnp.int32(length)
        for t in range(tiles):
            low = jnp.where(starts[t] <= begin, starts[t], low)
            end = starts[tiles - t]
            high = jnp.where(end >= begin + TALL, end, high)
        low = (low // 16) * 16
        blocks = (high - low + KEYS - 1) // KEYS
        for n in range(TALL // KEYS, length // KEYS + 1):

            @pl.when(jnp.logical_and(safe, blocks == n))
            def _(n=n):
                start = jnp.minimum(low, length - n * KEYS)
                both_heads(rows, pl.ds(pl.multiple_of(start, 16), n * KEYS), False)

        @pl.when(jnp.logical_not(safe))
        def _():
            both_heads(rows, slice(None), True)

        send_out(i).start()
        return carry

    lax.fori_loop(0, length // TALL, query_block, 0)
    for i in range(length // TALL):
        send_out(i).wait()


def attend(pair, staged, counts, own, other, w_qkv):
    length, half = own.shape
    features = 2 * half
    held = pl.BlockSpec(memory_space=pltpu.VMEM) if staged else ANYWHERE
    scratch = [
        pltpu.VMEM((features, 3 * LANES), bf16),
        pltpu.VMEM((2, length, LANES), bf16),
        pltpu.VMEM((2, length, LANES), bf16),
        pltpu.VMEM((2, length, LANES), bf16),
        pltpu.VMEM((length, LANES), bf16),
        pltpu.VMEM((1, LANES), f32),
        pltpu.VMEM((1, LANES), f32),
        pltpu.SemaphoreType.DMA((6,)),
        pltpu.SemaphoreType.DMA((length // TALL,)),
    ]
    if not staged:
        scratch += [pltpu.VMEM((length, features), bf16), pltpu.SemaphoreType.DMA((2,))]
    return pl.pallas_call(
        functools.partial(attend_kernel, pair, staged),
        out_shape=jax.ShapeDtypeStruct((length, LANES), bf16),
        in_specs=[SCALARS, held, held, ANYWHERE],
        out_specs=ANYWHERE,
        scratch_shapes=scratch,
        compiler_params=params(SMALL_BYTES if staged else VMEM_BYTES),
        cost_estimate=pl.CostEstimate(
            flops=32 * length * length * HDIM, bytes_accessed=8 * length * half, transcendentals=2 * length * length
        ),
    )(counts, own, other, w_qkv)


def unorder(rank_ref, start, rows, length, shards, context_ref):
    slot = slots(rank_ref[:, pl.ds(start, rows)], length, shards)
    slot = jnp.transpose(jnp.broadcast_to(slot, (LANES, rows)))
    place = lax.broadcasted_iota(jnp.int32, (1, length), 1)
    return dot(one_hot(slot, place), context_ref[...]).astype(bf16)


def unorder_kernel(shards, rank_hbm, own_hbm, other_hbm, out_ref, rank_ref, context_ref, sems):
    length = context_ref.shape[0]
    half_rows = out_ref.shape[0]
    base = lax.axis_index("mp") * half_rows
    copies = [
        pltpu.make_async_copy(rank_hbm, rank_ref, sems.at[0]),
        pltpu.make_async_copy(own_hbm, context_ref.at[:, :LANES], sems.at[1]),
        pltpu.make_async_copy(other_hbm, context_ref.at[:, LANES:], sems.at[2]),
    ]
    for copy in copies:
        copy.start()
    for copy in copies:
        copy.wait()
    for i, rows in enumerate(blocks_of(half_rows, TALL)):
        start = pl.multiple_of(base + i * TALL, TALL)
        out_ref[rows, :] = unorder(rank_ref, start, TALL, length, shards, context_ref)


def unorder_pair(shards, rank_row, own, other):
    length = own.shape[0]
    half_rows = length // 2
    return pl.pallas_call(
        functools.partial(unorder_kernel, shards),
        out_shape=jax.ShapeDtypeStruct((half_rows, 2 * LANES), bf16),
        in_specs=[ANYWHERE] * 3,
        out_specs=pl.BlockSpec(memory_space=pltpu.VMEM),
        scratch_shapes=[
            pltpu.VMEM((1, length), jnp.int32),
            pltpu.VMEM((length, 2 * LANES), bf16),
            pltpu.SemaphoreType.DMA((3,)),
        ],
        compiler_params=params(),
        cost_estimate=pl.CostEstimate(
            flops=4 * half_rows * length * LANES, bytes_accessed=8 * length * LANES, transcendentals=0
        ),
    )(rank_row, own, other)


def gelu_of_half(h):
    inner = 2 * math.sqrt(2 / math.pi)
    return h + h * jnp.tanh(h * (inner + (4 * 0.044715 * inner) * (h * h)))


def finish_kernel(
    shards,
    rank_hbm,
    gain_hbm,
    points_hbm,
    first_hbm,
    own_hbm,
    other_hbm,
    out_own_hbm,
    out_other_hbm,
    fc1_own_hbm,
    fc1_other_hbm,
    fc2_own_hbm,
    fc2_other_hbm,
    done_ref,
    whole_hbm,
    rank_ref,
    gain_ref,
    points_ref,
    first_ref,
    context_ref,
    out_ref,
    fc1_ref,
    fc2_ref,
    middle_ref,
    normed_ref,
    in_sems,
    sems,
):
    length = context_ref.shape[0]
    half_rows = done_ref.shape[0]
    base = pl.multiple_of(lax.axis_index("mp") * half_rows, half_rows)
    hidden_half = fc2_own_hbm.shape[0]
    early = [
        (rank_hbm, rank_ref),
        (own_hbm, context_ref.at[:, :LANES]),
        (other_hbm, context_ref.at[:, LANES:]),
    ]
    later = [(first_hbm, first_ref), (gain_hbm, gain_ref), (points_hbm.at[pl.ds(base, half_rows)], points_ref)]
    later += [
        (ref.at[pair * LANES : (pair + 1) * LANES], out_ref.at[(2 * pair + k) * LANES : (2 * pair + k + 1) * LANES])
        for pair in range(2)
        for k, ref in enumerate((out_own_hbm, out_other_hbm))
    ]
    last = [
        (fc1_own_hbm, fc1_ref.at[:, :hidden_half]),
        (fc1_other_hbm, fc1_ref.at[:, hidden_half:]),
        (fc2_own_hbm, fc2_ref.at[:hidden_half]),
        (fc2_other_hbm, fc2_ref.at[hidden_half:]),
    ]
    copies = [pltpu.make_async_copy(*ends, in_sems.at[k]) for k, ends in enumerate(early + later + last)]
    early, later, last = copies[:3], copies[3:10], copies[10:]
    for copy in copies:
        copy.start()

    blocks = blocks_of(half_rows, TALL)
    for copy in early:
        copy.wait()
    for i, rows in enumerate(blocks):
        start = pl.multiple_of(base + i * TALL, TALL)
        second = unorder(rank_ref, start, TALL, length, shards, context_ref)
        if i == 0:
            for copy in later:
                copy.wait()
        split_at = 2 * LANES
        attn_out = dot(first_ref[rows, :], out_ref[:split_at, :]) + dot(second, out_ref[split_at:, :])
        middle = (points_ref[rows, :].astype(f32) + attn_out.astype(bf16).astype(f32)).astype(bf16)
        middle_ref[rows, :] = middle
        normed_ref[rows, :] = normalise(middle.astype(f32), gain_ref[...]) * 0.5
    for copy in last:
        copy.wait()

    def away(i):
        here = pl.ds(pl.multiple_of(i * TALL, TALL), TALL)
        there = pl.ds(pl.multiple_of(base + i * TALL, TALL), TALL)
        return pltpu.make_async_copy(done_ref.at[here], whole_hbm.at[there], sems.at[i])

    chunks = blocks_of(2 * hidden_half, TALL)

    def mlp(i, carry):
        here = pl.ds(pl.multiple_of(i * TALL, TALL), TALL)
        normed = normed_ref[here, :]
        total = middle_ref[here, :].astype(f32)
        half_hidden = dot(normed, fc1_ref[:, chunks[0]])
        for k, chunk in enumerate(chunks):
            ahead = dot(normed, fc1_ref[:, chunks[k + 1]]) if k + 1 < len(chunks) else None
            total = total + dot(gelu_of_half(half_hidden).astype(bf16), fc2_ref[chunk, :])
            half_hidden = ahead
        done_ref[here, :] = total.astype(bf16)
        away(i).start()
        return carry

    lax.fori_loop(0, half_rows // TALL, mlp, 0)
    for i in range(half_rows // TALL):
        away(i).wait()


def finish(shards, rank_row, gain_row, points, *arrays):
    length, features = points.shape
    half_rows = length // 2
    hidden = 2 * arrays[-1].shape[0]
    return pl.pallas_call(
        functools.partial(finish_kernel, shards),
        out_shape=(
            jax.ShapeDtypeStruct((half_rows, features), bf16),
            jax.ShapeDtypeStruct((length, features), bf16),
        ),
        in_specs=[ANYWHERE] * 12,
        out_specs=(pl.BlockSpec(memory_space=pltpu.VMEM), ANYWHERE),
        scratch_shapes=[
            pltpu.VMEM((1, length), jnp.int32),
            pltpu.VMEM((1, features), f32),
            pltpu.VMEM((half_rows, features), bf16),
            pltpu.VMEM((half_rows, 2 * LANES), bf16),
            pltpu.VMEM((length, 2 * LANES), bf16),
            pltpu.VMEM((features, features), bf16),
            pltpu.VMEM((features, hidden), bf16),
            pltpu.VMEM((hidden, features), bf16),
            pltpu.VMEM((half_rows, features), bf16),
            pltpu.VMEM((half_rows, features), bf16),
            pltpu.SemaphoreType.DMA((14,)),
            pltpu.SemaphoreType.DMA((half_rows // TALL,)),
        ],
        compiler_params=params(),
        cost_estimate=pl.CostEstimate(
            flops=2 * half_rows * features * (length + 9 * features),
            bytes_accessed=16 * length * features,
            transcendentals=half_rows * 4 * features,
        ),
    )(rank_row, gain_row, points, *arrays)


def across(values):
    return lax.ppermute(values, "mp", [(0, 1), (1, 0)])


def exchange(rows, shards):
    length, columns = rows.shape
    cells = rows.reshape(shards, length // shards, columns)
    return lax.all_to_all(cells, "space", split_axis=0, concat_axis=0, tiled=True).reshape(length, columns)


def body(points, curve_rank, patch_counts, norm_gain_attn, w_qkv, w_out, norm_gain_mlp, w_fc1, w_fc2):
    shards = lax.axis_size("space")
    length, features = points.shape
    rank_row = curve_rank.reshape(1, length)
    own = exchange(order_for_owners(shards, rank_row, norm_gain_attn.reshape(1, features), points), shards)
    swapped = across(w_fc1), across(w_fc2), across(w_out)
    other = across(own)
    first_own = exchange(attend(0, True, patch_counts, own, other, w_qkv), shards)
    counts, (other_fc1, other_fc2, other_out) = lax.optimization_barrier((patch_counts, swapped))
    second_own = exchange(attend(1, False, counts, own, other, w_qkv), shards)
    first = unorder_pair(shards, rank_row, first_own, across(first_own))
    second_own, first = lax.optimization_barrier((second_own, first))
    done, whole = finish(
        shards,
        rank_row,
        norm_gain_mlp.reshape(1, features),
        points,
        first,
        second_own,
        across(second_own),
        w_out,
        other_out,
        w_fc1,
        other_fc1,
        w_fc2,
        other_fc2,
    )
    start = (1 - lax.axis_index("mp")) * (length // 2)
    return lax.dynamic_update_slice(whole, across(done), (start, 0))


def solution(mesh):
    placed = (
        P("space", None),
        P("space"),
        P("space", None),
        P(),
        P(None, None, "mp"),
        P("mp", None),
        P(),
        P(None, "mp"),
        P("mp", None),
    )
    return jax.shard_map(
        body, mesh=mesh, in_specs=placed, out_specs=P("space", None), check_vma=False
    )
```

```python
import functools
import math

import jax
import jax.numpy as jnp
from jax import lax
from jax.experimental import pallas as pl
from jax.experimental.pallas import tpu as pltpu
from jax.sharding import PartitionSpec as P

HDIM = 64
LANES = 128
ROWS = 256
TALL = 512
KEYS = 256
PADDED = HDIM + 16
EPSILON = 1e-06
FAR = 1e30
VMEM_BYTES = 58 * 1024 * 1024
SMALL_BYTES = 30 * 1024 * 1024

f32 = jnp.float32
bf16 = jnp.bfloat16

ANYWHERE = pl.BlockSpec(memory_space=pl.ANY)
SCALARS = pl.BlockSpec(memory_space=pltpu.SMEM)


def normalise(values, gain_row):
    average = jnp.mean(values, axis=-1, keepdims=True)
    centred = values - average
    second = jnp.mean(centred * centred, axis=-1, keepdims=True)
    return (centred * lax.rsqrt(second + EPSILON) * gain_row).astype(bf16)


def dot(left, right):
    return jnp.dot(left, right, preferred_element_type=f32)


def split(number, size):
    if size & (size - 1) == 0:
        return number >> (size.bit_length() - 1), number & (size - 1)
    return number // size, number % size


def slots(rank, length, shards):
    cell = length // shards
    owner, within = split(rank, length)
    return owner * cell + within - lax.axis_index("space") * cell


def one_hot(rows_at, columns_at):
    if columns_at.shape[1] <= 1 << 15:
        rows_at, columns_at = rows_at.astype(jnp.int16), columns_at.astype(jnp.int16)
    one, nil = jnp.ones((), bf16), jnp.zeros((), bf16)
    return jnp.concatenate(
        [
            jnp.where(rows_at == columns_at[:, k : k + LANES], one, nil)
            for k in range(0, columns_at.shape[1], LANES)
        ],
        axis=1,
    )


def blocks_of(length, rows=ROWS):
    return [slice(i * rows, (i + 1) * rows) for i in range(length // rows)]


def params(limit=VMEM_BYTES):
    return pltpu.CompilerParams(vmem_limit_bytes=limit)


def send_kernel(shards, rank_hbm, gain_hbm, points_hbm, out_ref, rank_ref, gain_ref, points_ref, half_ref, small, large):
    length, features = points_ref.shape
    half = features // 2
    core = lax.axis_index("mp")
    gain_copy = pltpu.make_async_copy(gain_hbm, gain_ref, small.at[0])
    rank_copy = pltpu.make_async_copy(rank_hbm, rank_ref, small.at[1])
    rows_of = blocks_of(length)
    copies = [
        pltpu.make_async_copy(points_hbm.at[rows], points_ref.at[rows], large.at[i])
        for i, rows in enumerate(rows_of)
    ]
    gain_copy.start()
    for copy in copies:
        copy.start()
    rank_copy.start()
    gain_copy.wait()
    for copy, rows in zip(copies, rows_of):
        copy.wait()
        normed = normalise(points_ref[rows, :].astype(f32), gain_ref[...])
        half_ref[rows, :] = jnp.where(core == 0, normed[:, :half], normed[:, half:])
    rank_copy.wait()
    slot = slots(rank_ref[...], length, shards)

    place = lax.broadcasted_iota(jnp.int32, (TALL, LANES), 0)
    for i, rows in enumerate(blocks_of(length, TALL)):
        out_ref[rows, :] = dot(one_hot(place + i * TALL, slot), half_ref[...]).astype(bf16)


def order_for_owners(shards, rank_row, gain_row, points):
    length, features = points.shape
    return pl.pallas_call(
        functools.partial(send_kernel, shards),
        out_shape=jax.ShapeDtypeStruct((length, features // 2), bf16),
        in_specs=[ANYWHERE] * 3,
        out_specs=pl.BlockSpec(memory_space=pltpu.VMEM),
        scratch_shapes=[
            pltpu.VMEM((1, length), jnp.int32),
            pltpu.VMEM((1, features), f32),
            pltpu.VMEM((length, features), bf16),
            pltpu.VMEM((length, features // 2), bf16),
            pltpu.SemaphoreType.DMA((2,)),
            pltpu.SemaphoreType.DMA((length // ROWS,)),
        ],
        compiler_params=params(),
        cost_estimate=pl.CostEstimate(
            flops=length * length * features, bytes_accessed=4 * length * features, transcendentals=0
        ),
    )(rank_row, gain_row, points)


def attend_kernel(
    counts_ref, own_ref, other_ref, weight_hbm, out_hbm, w_ref, q_ref, k_ref, v_ref, out_ref, w_sems, out_sems
):
    length, half = own_ref.shape
    tiles = counts_ref.shape[1]
    pairs = out_ref.shape[0]
    core = lax.axis_index("mp")
    scale = math.log2(math.e) / math.sqrt(HDIM)

    copies = [
        pltpu.make_async_copy(
            weight_hbm.at[j, pl.ds(pl.multiple_of(at * half, half), half)],
            w_ref.at[k * half : (k + 1) * half, j * pairs * LANES : (j + 1) * pairs * LANES],
            w_sems.at[2 * j + k],
        )
        for j in range(3)
        for k, at in enumerate((core, 1 - core))
    ]
    for copy in copies:
        copy.start()

    starts = [jnp.int32(0)]
    for t in range(tiles):
        starts.append(starts[-1] + counts_ref[0, t])
    lane = lax.broadcasted_iota(jnp.int32, (1, LANES), 1)
    first = jnp.full((1, LANES), length, jnp.int32)
    last = jnp.zeros((1, LANES), jnp.int32)
    for t in range(tiles):
        first = jnp.where(lane == HDIM + t, starts[t], first)
        last = jnp.where(lane == HDIM + t, starts[t + 1], last)
    flags = jnp.logical_and(lane >= HDIM, lane < HDIM + tiles)
    low_lanes = lane < HDIM
    v_ref[:, HDIM:, :] = jnp.ones((2 * pairs, PADDED - HDIM, length), bf16)
    for copy in copies:
        copy.wait()

    for i, rows in enumerate(blocks_of(length, TALL)):
        spread = dot(own_ref[rows, :], w_ref[:half, :]) + dot(other_ref[rows, :], w_ref[half:, :])
        place = lax.broadcasted_iota(jnp.int32, (TALL, LANES), 0) + i * TALL
        inside = jnp.logical_and(place >= first, place < last)
        q_flag = jnp.where(inside, 1.0, 0.0)
        k_flag = jnp.where(jnp.logical_and(flags, jnp.logical_not(inside)), -FAR, 0.0)
        for pair in range(pairs):
            q, k, v = (spread[:, (j * pairs + pair) * LANES : (j * pairs + pair + 1) * LANES] for j in range(3))
            q = q * scale
            q_ref[2 * pair, rows, :] = jnp.where(low_lanes, q, q_flag).astype(bf16)
            q_ref[2 * pair + 1, rows, :] = jnp.where(low_lanes, pltpu.roll(q, HDIM, 1), q_flag).astype(bf16)
            k_ref[2 * pair, rows, :] = jnp.where(low_lanes, k, k_flag).astype(bf16)
            k_ref[2 * pair + 1, rows, :] = jnp.where(low_lanes, pltpu.roll(k, HDIM, 1), k_flag).astype(bf16)
            v = jnp.transpose(v).astype(bf16)
            v_ref[2 * pair, :HDIM, rows] = v[:HDIM]
            v_ref[2 * pair + 1, :HDIM, rows] = v[HDIM:]

    def weigh(scores):
        return jnp.exp2(scores - jnp.max(scores, axis=0, keepdims=True)).astype(bf16)

    def send_out(i, pair):
        rows = pl.ds(pl.multiple_of(i * TALL, TALL), TALL)
        return pltpu.make_async_copy(
            out_ref.at[pair, rows], out_hbm.at[rows, pair * LANES : (pair + 1) * LANES], out_sems.at[i, pair]
        )

    def query_block(i, carry):
        begin = i * TALL
        rows = pl.ds(pl.multiple_of(begin, TALL), TALL)
        low, high = jnp.int32(0), jnp.int32(length)
        for t in range(tiles):
            low = jnp.where(starts[t] <= begin, starts[t], low)
            end = starts[tiles - t]
            high = jnp.where(end >= begin + TALL, end, high)
        low = (low // LANES) * LANES
        blocks = (high - low + KEYS - 1) // KEYS
        for n in range(TALL // KEYS, length // KEYS + 1):

            @pl.when(blocks == n)
            def _(n=n):
                start = pl.multiple_of(jnp.minimum(low, length - n * KEYS), LANES)
                keys = pl.ds(start, n * KEYS)

                def one_pair(pair, carry):
                    scores = [
                        lax.dot_general(
                            k_ref[2 * pair + h, keys, :],
                            q_ref[2 * pair + h, rows, :],
                            (((1,), (1,)), ((), ())),
                            preferred_element_type=f32,
                        )
                        for h in range(2)
                    ]
                    sums = [dot(v_ref[2 * pair + h, :, keys], weigh(scores[h])) for h in range(2)]
                    value = jnp.concatenate([both[:HDIM] / both[HDIM : HDIM + 1] for both in sums], axis=0)
                    out_ref[pair, rows, :] = jnp.transpose(value).astype(bf16)
                    return carry

                lax.fori_loop(0, pairs, one_pair, 0)

        for pair in range(pairs):
            send_out(i, pair).start()
        return carry

    lax.fori_loop(0, length // TALL, query_block, 0)
    for i in range(length // TALL):
        for pair in range(pairs):
            send_out(i, pair).wait()


def attend(counts, own, other, w_qkv):
    length, half = own.shape
    features, columns = w_qkv.shape[1:]
    heads = columns // HDIM
    held = pl.BlockSpec(memory_space=pltpu.VMEM)
    return pl.pallas_call(
        attend_kernel,
        out_shape=jax.ShapeDtypeStruct((length, columns), bf16),
        in_specs=[SCALARS, held, held, ANYWHERE],
        out_specs=ANYWHERE,
        scratch_shapes=[
            pltpu.VMEM((features, 3 * columns), bf16),
            pltpu.VMEM((heads, length, LANES), bf16),
            pltpu.VMEM((heads, length, LANES), bf16),
            pltpu.VMEM((heads, PADDED, length), bf16),
            pltpu.VMEM((heads // 2, length, LANES), bf16),
            pltpu.SemaphoreType.DMA((6,)),
            pltpu.SemaphoreType.DMA((length // TALL, heads // 2)),
        ],
        compiler_params=params(SMALL_BYTES),
        cost_estimate=pl.CostEstimate(
            flops=64 * length * length * HDIM, bytes_accessed=8 * length * half, transcendentals=4 * length * length
        ),
    )(counts, own, other, w_qkv)


def unorder(rank_ref, start, rows, length, shards, context_ref):
    slot = slots(rank_ref[:, pl.ds(start, rows)], length, shards)
    slot = jnp.transpose(jnp.broadcast_to(slot, (LANES, rows)))
    place = lax.broadcasted_iota(jnp.int32, (1, length), 1)
    return dot(one_hot(slot, place), context_ref[...]).astype(bf16)


def gelu_of_half(h):
    inner = 2 * math.sqrt(2 / math.pi)
    return h + h * jnp.tanh(h * (inner + (4 * 0.044715 * inner) * (h * h)))


def finish_kernel(
    shards,
    rank_hbm,
    gain_hbm,
    points_hbm,
    own_hbm,
    other_hbm,
    out_own_hbm,
    out_other_hbm,
    fc1_own_hbm,
    fc1_other_hbm,
    fc2_own_hbm,
    fc2_other_hbm,
    done_ref,
    whole_hbm,
    rank_ref,
    gain_ref,
    points_ref,
    context_ref,
    out_ref,
    fc1_ref,
    fc2_ref,
    middle_ref,
    normed_ref,
    in_sems,
    sems,
):
    length = context_ref.shape[0]
    half_rows = done_ref.shape[0]
    base = pl.multiple_of(lax.axis_index("mp") * half_rows, half_rows)
    hidden_half = fc2_own_hbm.shape[0]
    half = out_own_hbm.shape[0]
    early = [(rank_hbm, rank_ref), (own_hbm, context_ref.at[:, :half]), (other_hbm, context_ref.at[:, half:])]
    later = [
        (gain_hbm, gain_ref),
        (points_hbm.at[pl.ds(base, half_rows)], points_ref),
        (out_own_hbm, out_ref.at[:half]),
        (out_other_hbm, out_ref.at[half:]),
    ]
    last = [
        (fc1_own_hbm, fc1_ref.at[:, :hidden_half]),
        (fc1_other_hbm, fc1_ref.at[:, hidden_half:]),
        (fc2_own_hbm, fc2_ref.at[:hidden_half]),
        (fc2_other_hbm, fc2_ref.at[hidden_half:]),
    ]
    copies = [pltpu.make_async_copy(*ends, in_sems.at[k]) for k, ends in enumerate(early + later + last)]
    early, later, last = copies[:3], copies[3:7], copies[7:]
    for copy in copies:
        copy.start()

    blocks = blocks_of(half_rows, TALL)
    for copy in early:
        copy.wait()
    for i, rows in enumerate(blocks):
        start = pl.multiple_of(base + i * TALL, TALL)
        context = unorder(rank_ref, start, TALL, length, shards, context_ref)
        if i == 0:
            for copy in later:
                copy.wait()
        attn_out = dot(context, out_ref[...])
        middle = (points_ref[rows, :].astype(f32) + attn_out.astype(bf16).astype(f32)).astype(bf16)
        middle_ref[rows, :] = middle
        normed_ref[rows, :] = normalise(middle.astype(f32), gain_ref[...]) * 0.5
    for copy in last:
        copy.wait()

    def away(i):
        here = pl.ds(pl.multiple_of(i * TALL, TALL), TALL)
        there = pl.ds(pl.multiple_of(base + i * TALL, TALL), TALL)
        return pltpu.make_async_copy(done_ref.at[here], whole_hbm.at[there], sems.at[i])

    chunks = blocks_of(2 * hidden_half, TALL)

    def mlp(i, carry):
        here = pl.ds(pl.multiple_of(i * TALL, TALL), TALL)
        normed = normed_ref[here, :]
        total = middle_ref[here, :].astype(f32)
        half_hidden = dot(normed, fc1_ref[:, chunks[0]])
        for k, chunk in enumerate(chunks):
            ahead = dot(normed, fc1_ref[:, chunks[k + 1]]) if k + 1 < len(chunks) else None
            total = total + dot(gelu_of_half(half_hidden).astype(bf16), fc2_ref[chunk, :])
            half_hidden = ahead
        done_ref[here, :] = total.astype(bf16)
        away(i).start()
        return carry

    lax.fori_loop(0, half_rows // TALL, mlp, 0)
    for i in range(half_rows // TALL):
        away(i).wait()


def finish(shards, rank_row, gain_row, points, *arrays):
    length, features = points.shape
    half_rows = length // 2
    hidden = 2 * arrays[-1].shape[0]
    return pl.pallas_call(
        functools.partial(finish_kernel, shards),
        out_shape=(
            jax.ShapeDtypeStruct((half_rows, features), bf16),
            jax.ShapeDtypeStruct((length, features), bf16),
        ),
        in_specs=[ANYWHERE] * 11,
        out_specs=(pl.BlockSpec(memory_space=pltpu.VMEM), ANYWHERE),
        scratch_shapes=[
            pltpu.VMEM((1, length), jnp.int32),
            pltpu.VMEM((1, features), f32),
            pltpu.VMEM((half_rows, features), bf16),
            pltpu.VMEM((length, features), bf16),
            pltpu.VMEM((features, features), bf16),
            pltpu.VMEM((features, hidden), bf16),
            pltpu.VMEM((hidden, features), bf16),
            pltpu.VMEM((half_rows, features), bf16),
            pltpu.VMEM((half_rows, features), bf16),
            pltpu.SemaphoreType.DMA((11,)),
            pltpu.SemaphoreType.DMA((half_rows // TALL,)),
        ],
        compiler_params=params(),
        cost_estimate=pl.CostEstimate(
            flops=2 * half_rows * features * (length + 9 * features),
            bytes_accessed=16 * length * features,
            transcendentals=half_rows * 4 * features,
        ),
    )(rank_row, gain_row, points, *arrays)


def across(values):
    return lax.ppermute(values, "mp", [(0, 1), (1, 0)])


def exchange(rows, shards):
    length, columns = rows.shape
    cells = rows.reshape(shards, length // shards, columns)
    return lax.all_to_all(cells, "space", split_axis=0, concat_axis=0, tiled=True).reshape(length, columns)


def body(points, curve_rank, patch_counts, norm_gain_attn, w_qkv, w_out, norm_gain_mlp, w_fc1, w_fc2):
    shards = lax.axis_size("space")
    length, features = points.shape
    rank_row = curve_rank.reshape(1, length)
    own = exchange(order_for_owners(shards, rank_row, norm_gain_attn.reshape(1, features), points), shards)
    swapped = across(w_fc1), across(w_fc2), across(w_out)
    other = across(own)
    context = attend(patch_counts, own, other, w_qkv)
    context, (other_fc1, other_fc2, other_out) = lax.optimization_barrier((context, swapped))
    returned = exchange(context, shards)
    done, whole = finish(
        shards,
        rank_row,
        norm_gain_mlp.reshape(1, features),
        points,
        returned,
        across(returned),
        w_out,
        other_out,
        w_fc1,
        other_fc1,
        w_fc2,
        other_fc2,
    )
    start = (1 - lax.axis_index("mp")) * (length // 2)
    return lax.dynamic_update_slice(whole, across(done), (start, 0))


def solution(mesh):
    placed = (
        P("space", None),
        P("space"),
        P("space", None),
        P(),
        P(None, None, "mp"),
        P("mp", None),
        P(),
        P(None, "mp"),
        P("mp", None),
    )
    return jax.shard_map(
        body, mesh=mesh, in_specs=placed, out_specs=P("space", None), check_vma=False
    )
```

```python
import functools
import math

import jax
import jax.numpy as jnp
from jax import lax
from jax.experimental import pallas as pl
from jax.experimental.pallas import tpu as pltpu
from jax.sharding import PartitionSpec as P

HDIM = 64
LANES = 128
ROWS = 256
TALL = 512
KEYS = 256
PADDED = HDIM + 16
EPSILON = 1e-06
FAR = 1e30
VMEM_BYTES = 58 * 1024 * 1024
SMALL_BYTES = 30 * 1024 * 1024

f32 = jnp.float32
bf16 = jnp.bfloat16

ANYWHERE = pl.BlockSpec(memory_space=pl.ANY)
SCALARS = pl.BlockSpec(memory_space=pltpu.SMEM)


def normalise(values, gain_row):
    average = jnp.mean(values, axis=-1, keepdims=True)
    centred = values - average
    second = jnp.mean(centred * centred, axis=-1, keepdims=True)
    return (centred * lax.rsqrt(second + EPSILON) * gain_row).astype(bf16)


def dot(left, right):
    return jnp.dot(left, right, preferred_element_type=f32)


def split(number, size):
    if size & (size - 1) == 0:
        return number >> (size.bit_length() - 1), number & (size - 1)
    return number // size, number % size


def slots(rank, length, shards):
    cell = length // shards
    owner, within = split(rank, length)
    return owner * cell + within - lax.axis_index("space") * cell


def one_hot(rows_at, columns_at):
    if columns_at.shape[1] <= 1 << 15:
        rows_at, columns_at = rows_at.astype(jnp.int16), columns_at.astype(jnp.int16)
    one, nil = jnp.ones((), bf16), jnp.zeros((), bf16)
    return jnp.concatenate(
        [
            jnp.where(rows_at == columns_at[:, k : k + LANES], one, nil)
            for k in range(0, columns_at.shape[1], LANES)
        ],
        axis=1,
    )


def blocks_of(length, rows=ROWS):
    return [slice(i * rows, (i + 1) * rows) for i in range(length // rows)]


def params(limit=VMEM_BYTES):
    return pltpu.CompilerParams(vmem_limit_bytes=limit)


def send_kernel(shards, by_rows, rank_hbm, gain_hbm, points_hbm, out_ref, rank_ref, gain_ref, points_ref, normed_ref, small, large):
    length, features = points_ref.shape
    half = features // 2
    core = lax.axis_index("mp")
    gain_copy = pltpu.make_async_copy(gain_hbm, gain_ref, small.at[0])
    rank_copy = pltpu.make_async_copy(rank_hbm, rank_ref, small.at[1])
    rows_of = blocks_of(length)
    copies = [
        pltpu.make_async_copy(points_hbm.at[rows], points_ref.at[rows], large.at[i])
        for i, rows in enumerate(rows_of)
    ]
    gain_copy.start()
    for copy in copies:
        copy.start()
    rank_copy.start()
    gain_copy.wait()
    for copy, rows in zip(copies, rows_of):
        copy.wait()
        normed = normalise(points_ref[rows, :].astype(f32), gain_ref[...])
        if not by_rows:
            normed = jnp.where(core == 0, normed[:, :half], normed[:, half:])
        normed_ref[rows, :] = normed
    rank_copy.wait()
    slot = slots(rank_ref[...], length, shards)
    if by_rows:
        half_cell = length // shards // 2
        piece, row = split(slot, half_cell)
        owner, which = split(piece, 2)
        slot = jnp.where(which == core, owner * half_cell + row, length)

    place = lax.broadcasted_iota(jnp.int32, (TALL, LANES), 0)
    for i, rows in enumerate(blocks_of(out_ref.shape[0], TALL)):
        out_ref[rows, :] = dot(one_hot(place + i * TALL, slot), normed_ref[...]).astype(bf16)


def order_for_owners(shards, by_rows, rank_row, gain_row, points):
    length, features = points.shape
    rows, columns = (length // 2, features) if by_rows else (length, features // 2)
    return pl.pallas_call(
        functools.partial(send_kernel, shards, by_rows),
        out_shape=jax.ShapeDtypeStruct((rows, columns), bf16),
        in_specs=[ANYWHERE] * 3,
        out_specs=pl.BlockSpec(memory_space=pltpu.VMEM),
        scratch_shapes=[
            pltpu.VMEM((1, length), jnp.int32),
            pltpu.VMEM((1, features), f32),
            pltpu.VMEM((length, features), bf16),
            pltpu.VMEM((length, columns), bf16),
            pltpu.SemaphoreType.DMA((2,)),
            pltpu.SemaphoreType.DMA((length // ROWS,)),
        ],
        compiler_params=params(),
        cost_estimate=pl.CostEstimate(
            flops=length * length * features, bytes_accessed=4 * length * features, transcendentals=0
        ),
    )(rank_row, gain_row, points)


def interleave(own_ref, other_ref, start, half_cell, core):
    halves = []
    for at in range(start, start + TALL // 2, half_cell):
        mine, theirs = (ref[at : at + half_cell, :] for ref in (own_ref, other_ref))
        halves += [jnp.where(core == 0, mine, theirs), jnp.where(core == 0, theirs, mine)]
    return jnp.concatenate(halves, axis=0)


def attend_kernel(
    half_cell, counts_ref, own_ref, other_ref, weight_hbm, out_hbm, w_ref, q_ref, k_ref, v_ref, out_ref, w_sems, out_sems
):
    length, features = q_ref.shape[1], w_ref.shape[0]
    half = features // 2
    tiles = counts_ref.shape[1]
    pairs = out_ref.shape[0]
    core = lax.axis_index("mp")
    scale = math.log2(math.e) / math.sqrt(HDIM)

    def in_rows(k, at):
        return pl.ds(pl.multiple_of((at if half_cell else k) * half, half), half)

    copies = [
        pltpu.make_async_copy(
            weight_hbm.at[j, pl.ds(pl.multiple_of(at * half, half), half)],
            w_ref.at[in_rows(k, at), j * pairs * LANES : (j + 1) * pairs * LANES],
            w_sems.at[2 * j + k],
        )
        for j in range(3)
        for k, at in enumerate((core, 1 - core))
    ]
    for copy in copies:
        copy.start()

    starts = [jnp.int32(0)]
    for t in range(tiles):
        starts.append(starts[-1] + counts_ref[0, t])
    lane = lax.broadcasted_iota(jnp.int32, (1, LANES), 1)
    first = jnp.full((1, LANES), length, jnp.int32)
    last = jnp.zeros((1, LANES), jnp.int32)
    for t in range(tiles):
        first = jnp.where(lane == HDIM + t, starts[t], first)
        last = jnp.where(lane == HDIM + t, starts[t + 1], last)
    flags = jnp.logical_and(lane >= HDIM, lane < HDIM + tiles)
    low_lanes = lane < HDIM
    v_ref[:, HDIM:, :] = jnp.ones((2 * pairs, PADDED - HDIM, length), bf16)
    for copy in copies:
        copy.wait()

    for i, rows in enumerate(blocks_of(length, TALL)):
        if half_cell:
            block = interleave(own_ref, other_ref, i * TALL // 2, half_cell, core)
            spread = dot(block, w_ref[...])
        else:
            spread = dot(own_ref[rows, :], w_ref[:half, :]) + dot(other_ref[rows, :], w_ref[half:, :])
        place = lax.broadcasted_iota(jnp.int32, (TALL, LANES), 0) + i * TALL
        inside = jnp.logical_and(place >= first, place < last)
        q_flag = jnp.where(inside, 1.0, 0.0)
        k_flag = jnp.where(jnp.logical_and(flags, jnp.logical_not(inside)), -FAR, 0.0)
        for pair in range(pairs):
            q, k, v = (spread[:, (j * pairs + pair) * LANES : (j * pairs + pair + 1) * LANES] for j in range(3))
            q = q * scale
            q_ref[2 * pair, rows, :] = jnp.where(low_lanes, q, q_flag).astype(bf16)
            q_ref[2 * pair + 1, rows, :] = jnp.where(low_lanes, pltpu.roll(q, HDIM, 1), q_flag).astype(bf16)
            k_ref[2 * pair, rows, :] = jnp.where(low_lanes, k, k_flag).astype(bf16)
            k_ref[2 * pair + 1, rows, :] = jnp.where(low_lanes, pltpu.roll(k, HDIM, 1), k_flag).astype(bf16)
            v = jnp.transpose(v).astype(bf16)
            v_ref[2 * pair, :HDIM, rows] = v[:HDIM]
            v_ref[2 * pair + 1, :HDIM, rows] = v[HDIM:]

    def weigh(scores):
        return jnp.exp2((scores - jnp.max(scores, axis=0, keepdims=True)).astype(bf16))

    def send_out(i, pair):
        rows = pl.ds(pl.multiple_of(i * TALL, TALL), TALL)
        return pltpu.make_async_copy(
            out_ref.at[pair, rows], out_hbm.at[rows, pair * LANES : (pair + 1) * LANES], out_sems.at[i, pair]
        )

    def query_block(i, carry):
        begin = i * TALL
        rows = pl.ds(pl.multiple_of(begin, TALL), TALL)
        low, high = jnp.int32(0), jnp.int32(length)
        for t in range(tiles):
            low = jnp.where(starts[t] <= begin, starts[t], low)
            end = starts[tiles - t]
            high = jnp.where(end >= begin + TALL, end, high)
        low = (low // LANES) * LANES
        blocks = (high - low + KEYS - 1) // KEYS
        for n in range(TALL // KEYS, length // KEYS + 1):

            @pl.when(blocks == n)
            def _(n=n):
                start = pl.multiple_of(jnp.minimum(low, length - n * KEYS), LANES)
                keys = pl.ds(start, n * KEYS)

                def one_pair(pair, carry):
                    scores = [
                        lax.dot_general(
                            k_ref[2 * pair + h, keys, :],
                            q_ref[2 * pair + h, rows, :],
                            (((1,), (1,)), ((), ())),
                            preferred_element_type=f32,
                        )
                        for h in range(2)
                    ]
                    sums = [dot(v_ref[2 * pair + h, :, keys], weigh(scores[h])) for h in range(2)]
                    value = jnp.concatenate([both[:HDIM] / both[HDIM : HDIM + 1] for both in sums], axis=0)
                    out_ref[pair, rows, :] = jnp.transpose(value).astype(bf16)
                    return carry

                lax.fori_loop(0, pairs, one_pair, 0)

        for pair in range(pairs):
            send_out(i, pair).start()
        return carry

    lax.fori_loop(0, length // TALL, query_block, 0)
    for i in range(length // TALL):
        for pair in range(pairs):
            send_out(i, pair).wait()


def attend(half_cell, counts, own, other, w_qkv):
    features, columns = w_qkv.shape[1:]
    length = own.size * 2 // features
    heads = columns // HDIM
    held = pl.BlockSpec(memory_space=pltpu.VMEM)
    return pl.pallas_call(
        functools.partial(attend_kernel, half_cell),
        out_shape=jax.ShapeDtypeStruct((length, columns), bf16),
        in_specs=[SCALARS, held, held, ANYWHERE],
        out_specs=ANYWHERE,
        scratch_shapes=[
            pltpu.VMEM((features, 3 * columns), bf16),
            pltpu.VMEM((heads, length, LANES), bf16),
            pltpu.VMEM((heads, length, LANES), bf16),
            pltpu.VMEM((heads, PADDED, length), bf16),
            pltpu.VMEM((heads // 2, length, LANES), bf16),
            pltpu.SemaphoreType.DMA((6,)),
            pltpu.SemaphoreType.DMA((length // TALL, heads // 2)),
        ],
        compiler_params=params(SMALL_BYTES),
        cost_estimate=pl.CostEstimate(
            flops=64 * length * length * HDIM, bytes_accessed=4 * length * features, transcendentals=4 * length * length
        ),
    )(counts, own, other, w_qkv)


def unorder(rank_ref, start, rows, length, shards, context_ref):
    slot = slots(rank_ref[:, pl.ds(start, rows)], length, shards)
    slot = jnp.transpose(jnp.broadcast_to(slot, (LANES, rows)))
    place = lax.broadcasted_iota(jnp.int32, (1, length), 1)
    return dot(one_hot(slot, place), context_ref[...]).astype(bf16)


def gelu_of_half(h):
    inner = 2 * math.sqrt(2 / math.pi)
    return h + h * jnp.tanh(h * (inner + (4 * 0.044715 * inner) * (h * h)))


def finish_kernel(
    shards,
    rank_hbm,
    gain_hbm,
    points_hbm,
    own_hbm,
    other_hbm,
    out_own_hbm,
    out_other_hbm,
    fc1_own_hbm,
    fc1_other_hbm,
    fc2_own_hbm,
    fc2_other_hbm,
    done_ref,
    whole_hbm,
    rank_ref,
    gain_ref,
    points_ref,
    context_ref,
    out_ref,
    fc1_ref,
    fc2_ref,
    middle_ref,
    normed_ref,
    in_sems,
    sems,
):
    length = context_ref.shape[0]
    half_rows = done_ref.shape[0]
    base = pl.multiple_of(lax.axis_index("mp") * half_rows, half_rows)
    hidden_half = fc2_own_hbm.shape[0]
    half = out_own_hbm.shape[0]
    early = [(rank_hbm, rank_ref), (own_hbm, context_ref.at[:, :half]), (other_hbm, context_ref.at[:, half:])]
    later = [
        (gain_hbm, gain_ref),
        (points_hbm.at[pl.ds(base, half_rows)], points_ref),
        (out_own_hbm, out_ref.at[:half]),
        (out_other_hbm, out_ref.at[half:]),
    ]
    last = [
        (fc1_own_hbm, fc1_ref.at[:, :hidden_half]),
        (fc1_other_hbm, fc1_ref.at[:, hidden_half:]),
        (fc2_own_hbm, fc2_ref.at[:hidden_half]),
        (fc2_other_hbm, fc2_ref.at[hidden_half:]),
    ]
    copies = [pltpu.make_async_copy(*ends, in_sems.at[k]) for k, ends in enumerate(early + later + last)]
    early, later, last = copies[:3], copies[3:7], copies[7:]
    for copy in copies:
        copy.start()

    blocks = blocks_of(half_rows, TALL)
    for copy in early:
        copy.wait()
    for i, rows in enumerate(blocks):
        start = pl.multiple_of(base + i * TALL, TALL)
        context = unorder(rank_ref, start, TALL, length, shards, context_ref)
        if i == 0:
            for copy in later:
                copy.wait()
        attn_out = dot(context, out_ref[...])
        middle = (points_ref[rows, :].astype(f32) + attn_out.astype(bf16).astype(f32)).astype(bf16)
        middle_ref[rows, :] = middle
        normed_ref[rows, :] = normalise(middle.astype(f32), gain_ref[...]) * 0.5
    for copy in last:
        copy.wait()

    def away(i):
        here = pl.ds(pl.multiple_of(i * TALL, TALL), TALL)
        there = pl.ds(pl.multiple_of(base + i * TALL, TALL), TALL)
        return pltpu.make_async_copy(done_ref.at[here], whole_hbm.at[there], sems.at[i])

    chunks = blocks_of(2 * hidden_half, TALL)

    def mlp(i, carry):
        here = pl.ds(pl.multiple_of(i * TALL, TALL), TALL)
        normed = normed_ref[here, :]
        total = middle_ref[here, :].astype(f32)
        half_hidden = dot(normed, fc1_ref[:, chunks[0]])
        for k, chunk in enumerate(chunks):
            ahead = dot(normed, fc1_ref[:, chunks[k + 1]]) if k + 1 < len(chunks) else None
            total = total + dot(gelu_of_half(half_hidden).astype(bf16), fc2_ref[chunk, :])
            half_hidden = ahead
        done_ref[here, :] = total.astype(bf16)
        away(i).start()
        return carry

    lax.fori_loop(0, half_rows // TALL, mlp, 0)
    for i in range(half_rows // TALL):
        away(i).wait()


def finish(shards, rank_row, gain_row, points, *arrays):
    length, features = points.shape
    half_rows = length // 2
    hidden = 2 * arrays[-1].shape[0]
    return pl.pallas_call(
        functools.partial(finish_kernel, shards),
        out_shape=(
            jax.ShapeDtypeStruct((half_rows, features), bf16),
            jax.ShapeDtypeStruct((length, features), bf16),
        ),
        in_specs=[ANYWHERE] * 11,
        out_specs=(pl.BlockSpec(memory_space=pltpu.VMEM), ANYWHERE),
        scratch_shapes=[
            pltpu.VMEM((1, length), jnp.int32),
            pltpu.VMEM((1, features), f32),
            pltpu.VMEM((half_rows, features), bf16),
            pltpu.VMEM((length, features), bf16),
            pltpu.VMEM((features, features), bf16),
            pltpu.VMEM((features, hidden), bf16),
            pltpu.VMEM((hidden, features), bf16),
            pltpu.VMEM((half_rows, features), bf16),
            pltpu.VMEM((half_rows, features), bf16),
            pltpu.SemaphoreType.DMA((11,)),
            pltpu.SemaphoreType.DMA((half_rows // TALL,)),
        ],
        compiler_params=params(),
        cost_estimate=pl.CostEstimate(
            flops=2 * half_rows * features * (length + 9 * features),
            bytes_accessed=16 * length * features,
            transcendentals=half_rows * 4 * features,
        ),
    )(rank_row, gain_row, points, *arrays)


def across(values):
    return lax.ppermute(values, "mp", [(0, 1), (1, 0)])


def exchange(rows, shards):
    length, columns = rows.shape
    cells = rows.reshape(shards, length // shards, columns)
    return lax.all_to_all(cells, "space", split_axis=0, concat_axis=0, tiled=True).reshape(length, columns)


def body(points, curve_rank, patch_counts, norm_gain_attn, w_qkv, w_out, norm_gain_mlp, w_fc1, w_fc2):
    shards = lax.axis_size("space")
    length, features = points.shape
    rank_row = curve_rank.reshape(1, length)
    half_cell = length // shards // 2
    half_cell = half_cell if half_cell % 16 == 0 and half_cell <= TALL // 2 else 0
    own = exchange(order_for_owners(shards, half_cell > 0, rank_row, norm_gain_attn.reshape(1, features), points), shards)
    swapped = across(w_fc1), across(w_fc2), across(w_out)
    other = across(own)
    context = attend(half_cell, patch_counts, own, other, w_qkv)
    context, (other_fc1, other_fc2, other_out) = lax.optimization_barrier((context, swapped))
    returned = exchange(context, shards)
    done, whole = finish(
        shards,
        rank_row,
        norm_gain_mlp.reshape(1, features),
        points,
        returned,
        across(returned),
        w_out,
        other_out,
        w_fc1,
        other_fc1,
        w_fc2,
        other_fc2,
    )
    start = (1 - lax.axis_index("mp")) * (length // 2)
    return lax.dynamic_update_slice(whole, across(done), (start, 0))


def solution(mesh):
    placed = (
        P("space", None),
        P("space"),
        P("space", None),
        P(),
        P(None, None, "mp"),
        P("mp", None),
        P(),
        P(None, "mp"),
        P("mp", None),
    )
    return jax.shard_map(
        body, mesh=mesh, in_specs=placed, out_specs=P("space", None), check_vma=False
    )
```

```python
import functools
import math

import jax
import jax.numpy as jnp
from jax import lax
from jax.experimental import pallas as pl
from jax.experimental.pallas import tpu as pltpu
from jax.sharding import PartitionSpec as P

HDIM = 64
LANES = 128
ROWS = 256
TALL = 512
KEYS = 256
PADDED = HDIM + 16
EPSILON = 1e-06
FAR = 1e30
SAFE = 105.0
VMEM_BYTES = 58 * 1024 * 1024
SMALL_BYTES = 30 * 1024 * 1024

f32 = jnp.float32
bf16 = jnp.bfloat16

ANYWHERE = pl.BlockSpec(memory_space=pl.ANY)
SCALARS = pl.BlockSpec(memory_space=pltpu.SMEM)


def normalise(values, gain_row):
    average = jnp.mean(values, axis=-1, keepdims=True)
    centred = values - average
    second = jnp.mean(centred * centred, axis=-1, keepdims=True)
    return (centred * lax.rsqrt(second + EPSILON) * gain_row).astype(bf16)


def dot(left, right):
    return jnp.dot(left, right, preferred_element_type=f32)


def split(number, size):
    if size & (size - 1) == 0:
        return number >> (size.bit_length() - 1), number & (size - 1)
    return number // size, number % size


def slots(rank, length, shards):
    cell = length // shards
    owner, within = split(rank, length)
    return owner * cell + within - lax.axis_index("space") * cell


def one_hot(rows_at, columns_at):
    if columns_at.shape[1] <= 1 << 15:
        rows_at, columns_at = rows_at.astype(jnp.int16), columns_at.astype(jnp.int16)
    one, nil = jnp.ones((), bf16), jnp.zeros((), bf16)
    return jnp.concatenate(
        [
            jnp.where(rows_at == columns_at[:, k : k + LANES], one, nil)
            for k in range(0, columns_at.shape[1], LANES)
        ],
        axis=1,
    )


def blocks_of(length, rows=ROWS):
    return [slice(i * rows, (i + 1) * rows) for i in range(length // rows)]


def params(limit=VMEM_BYTES):
    return pltpu.CompilerParams(vmem_limit_bytes=limit)


def send_kernel(shards, rank_hbm, gain_hbm, points_hbm, out_ref, rank_ref, gain_ref, points_ref, half_ref, small, large):
    length, features = points_ref.shape
    half = features // 2
    core = lax.axis_index("mp")
    gain_copy = pltpu.make_async_copy(gain_hbm, gain_ref, small.at[0])
    rank_copy = pltpu.make_async_copy(rank_hbm, rank_ref, small.at[1])
    rows_of = blocks_of(length)
    copies = [
        pltpu.make_async_copy(points_hbm.at[rows], points_ref.at[rows], large.at[i])
        for i, rows in enumerate(rows_of)
    ]
    gain_copy.start()
    for copy in copies:
        copy.start()
    rank_copy.start()
    gain_copy.wait()
    for copy, rows in zip(copies, rows_of):
        copy.wait()
        normed = normalise(points_ref[rows, :].astype(f32), gain_ref[...])
        half_ref[rows, :] = jnp.where(core == 0, normed[:, :half], normed[:, half:])
    rank_copy.wait()
    slot = slots(rank_ref[...], length, shards)

    place = lax.broadcasted_iota(jnp.int32, (TALL, LANES), 0)
    for i, rows in enumerate(blocks_of(length, TALL)):
        out_ref[rows, :] = dot(one_hot(place + i * TALL, slot), half_ref[...]).astype(bf16)


def order_for_owners(shards, rank_row, gain_row, points):
    length, features = points.shape
    return pl.pallas_call(
        functools.partial(send_kernel, shards),
        out_shape=jax.ShapeDtypeStruct((length, features // 2), bf16),
        in_specs=[ANYWHERE] * 3,
        out_specs=pl.BlockSpec(memory_space=pltpu.VMEM),
        scratch_shapes=[
            pltpu.VMEM((1, length), jnp.int32),
            pltpu.VMEM((1, features), f32),
            pltpu.VMEM((length, features), bf16),
            pltpu.VMEM((length, features // 2), bf16),
            pltpu.SemaphoreType.DMA((2,)),
            pltpu.SemaphoreType.DMA((length // ROWS,)),
        ],
        compiler_params=params(),
        cost_estimate=pl.CostEstimate(
            flops=length * length * features, bytes_accessed=4 * length * features, transcendentals=0
        ),
    )(rank_row, gain_row, points)


def attend_kernel(
    counts_ref, own_ref, other_ref, weight_hbm, out_hbm, w_ref, q_ref, k_ref, v_ref, out_ref, w_sems, out_sems
):
    length, half = own_ref.shape
    tiles = counts_ref.shape[1]
    pairs = out_ref.shape[0]
    core = lax.axis_index("mp")
    scale = math.log2(math.e) / math.sqrt(HDIM)

    copies = [
        pltpu.make_async_copy(
            weight_hbm.at[j, pl.ds(pl.multiple_of(at * half, half), half)],
            w_ref.at[k * half : (k + 1) * half, j * pairs * LANES : (j + 1) * pairs * LANES],
            w_sems.at[2 * j + k],
        )
        for j in range(3)
        for k, at in enumerate((core, 1 - core))
    ]
    for copy in copies:
        copy.start()

    starts = [jnp.int32(0)]
    for t in range(tiles):
        starts.append(starts[-1] + counts_ref[0, t])
    lane = lax.broadcasted_iota(jnp.int32, (1, LANES), 1)
    first = jnp.full((1, LANES), length, jnp.int32)
    last = jnp.zeros((1, LANES), jnp.int32)
    for t in range(tiles):
        first = jnp.where(lane == HDIM + t, starts[t], first)
        last = jnp.where(lane == HDIM + t, starts[t + 1], last)
    flags = jnp.logical_and(lane >= HDIM, lane < HDIM + tiles)
    low_lanes = lane < HDIM
    v_ref[:, HDIM:, :] = jnp.ones((2 * pairs, PADDED - HDIM, length), bf16)
    for copy in copies:
        copy.wait()

    most = [[jnp.zeros((1, 1), f32)] * 2 for _ in range(pairs)]

    def squares(values):
        return jnp.max(jnp.sum(values * values, axis=1, keepdims=True), axis=0, keepdims=True)

    for i, rows in enumerate(blocks_of(length, TALL)):
        spread = dot(own_ref[rows, :], w_ref[:half, :]) + dot(other_ref[rows, :], w_ref[half:, :])
        place = lax.broadcasted_iota(jnp.int32, (TALL, LANES), 0) + i * TALL
        inside = jnp.logical_and(place >= first, place < last)
        q_flag = jnp.where(inside, 1.0, 0.0)
        k_flag = jnp.where(jnp.logical_and(flags, jnp.logical_not(inside)), -FAR, 0.0)
        for pair in range(pairs):
            q, k, v = (spread[:, (j * pairs + pair) * LANES : (j * pairs + pair + 1) * LANES] for j in range(3))
            q = q * scale
            most[pair] = [jnp.maximum(old, squares(new)) for old, new in zip(most[pair], (q, k))]
            q_ref[2 * pair, rows, :] = jnp.where(low_lanes, q, q_flag).astype(bf16)
            q_ref[2 * pair + 1, rows, :] = jnp.where(low_lanes, pltpu.roll(q, HDIM, 1), q_flag).astype(bf16)
            k_ref[2 * pair, rows, :] = jnp.where(low_lanes, k, k_flag).astype(bf16)
            k_ref[2 * pair + 1, rows, :] = jnp.where(low_lanes, pltpu.roll(k, HDIM, 1), k_flag).astype(bf16)
            v = jnp.transpose(v).astype(bf16)
            v_ref[2 * pair, :HDIM, rows] = v[:HDIM]
            v_ref[2 * pair + 1, :HDIM, rows] = v[HDIM:]

    bound = functools.reduce(jnp.maximum, [q_most * k_most for q_most, k_most in most])
    safe = jnp.max(bound) < SAFE * SAFE

    def attend_pair(pair, rows, keys, shifted):
        scores = [
            lax.dot_general(
                k_ref[2 * pair + h, keys, :],
                q_ref[2 * pair + h, rows, :],
                (((1,), (1,)), ((), ())),
                preferred_element_type=f32,
            )
            for h in range(2)
        ]
        if shifted:
            scores = [values - jnp.max(values, axis=0, keepdims=True) for values in scores]
        sums = [dot(v_ref[2 * pair + h, :, keys], jnp.exp2(scores[h]).astype(bf16)) for h in range(2)]
        value = jnp.concatenate([both[:HDIM] / both[HDIM : HDIM + 1] for both in sums], axis=0)
        out_ref[pair, rows, :] = jnp.transpose(value).astype(bf16)

    def attend_rows(rows, keys, shifted):
        def one_pair(pair, carry):
            attend_pair(pair, rows, keys, shifted)
            return carry

        lax.fori_loop(0, pairs, one_pair, 0)

    def send_out(i, pair):
        rows = pl.ds(pl.multiple_of(i * TALL, TALL), TALL)
        return pltpu.make_async_copy(
            out_ref.at[pair, rows], out_hbm.at[rows, pair * LANES : (pair + 1) * LANES], out_sems.at[i, pair]
        )

    def query_block(i, carry):
        begin = i * TALL
        rows = pl.ds(pl.multiple_of(begin, TALL), TALL)
        low, high = jnp.int32(0), jnp.int32(length)
        for t in range(tiles):
            low = jnp.where(starts[t] <= begin, starts[t], low)
            end = starts[tiles - t]
            high = jnp.where(end >= begin + TALL, end, high)
        low = (low // LANES) * LANES
        blocks = (high - low + KEYS - 1) // KEYS
        for n in range(TALL // KEYS, length // KEYS + 1):

            @pl.when(jnp.logical_and(safe, blocks == n))
            def _(n=n):
                start = pl.multiple_of(jnp.minimum(low, length - n * KEYS), LANES)
                attend_rows(rows, pl.ds(start, n * KEYS), False)

        @pl.when(jnp.logical_not(safe))
        def _():
            attend_rows(rows, slice(None), True)

        for pair in range(pairs):
            send_out(i, pair).start()
        return carry

    lax.fori_loop(0, length // TALL, query_block, 0)
    for i in range(length // TALL):
        for pair in range(pairs):
            send_out(i, pair).wait()


def attend(counts, own, other, w_qkv):
    length, half = own.shape
    features, columns = w_qkv.shape[1:]
    heads = columns // HDIM
    held = pl.BlockSpec(memory_space=pltpu.VMEM)
    return pl.pallas_call(
        attend_kernel,
        out_shape=jax.ShapeDtypeStruct((length, columns), bf16),
        in_specs=[SCALARS, held, held, ANYWHERE],
        out_specs=ANYWHERE,
        scratch_shapes=[
            pltpu.VMEM((features, 3 * columns), bf16),
            pltpu.VMEM((heads, length, LANES), bf16),
            pltpu.VMEM((heads, length, LANES), bf16),
            pltpu.VMEM((heads, PADDED, length), bf16),
            pltpu.VMEM((heads // 2, length, LANES), bf16),
            pltpu.SemaphoreType.DMA((6,)),
            pltpu.SemaphoreType.DMA((length // TALL, heads // 2)),
        ],
        compiler_params=params(SMALL_BYTES),
        cost_estimate=pl.CostEstimate(
            flops=64 * length * length * HDIM, bytes_accessed=8 * length * half, transcendentals=4 * length * length
        ),
    )(counts, own, other, w_qkv)


def unorder(rank_ref, start, rows, length, shards, context_ref):
    slot = slots(rank_ref[:, pl.ds(start, rows)], length, shards)
    slot = jnp.transpose(jnp.broadcast_to(slot, (LANES, rows)))
    place = lax.broadcasted_iota(jnp.int32, (1, length), 1)
    return dot(one_hot(slot, place), context_ref[...]).astype(bf16)


def gelu_of_half(h):
    inner = 2 * math.sqrt(2 / math.pi)
    return h + h * jnp.tanh(h * (inner + (4 * 0.044715 * inner) * (h * h)))


def finish_kernel(
    shards,
    rank_hbm,
    gain_hbm,
    points_hbm,
    own_hbm,
    other_hbm,
    out_own_hbm,
    out_other_hbm,
    fc1_own_hbm,
    fc1_other_hbm,
    fc2_own_hbm,
    fc2_other_hbm,
    done_ref,
    whole_hbm,
    rank_ref,
    gain_ref,
    points_ref,
    context_ref,
    out_ref,
    fc1_ref,
    fc2_ref,
    middle_ref,
    normed_ref,
    in_sems,
    sems,
):
    length = context_ref.shape[0]
    half_rows = done_ref.shape[0]
    base = pl.multiple_of(lax.axis_index("mp") * half_rows, half_rows)
    hidden_half = fc2_own_hbm.shape[0]
    half = out_own_hbm.shape[0]
    early = [(rank_hbm, rank_ref), (own_hbm, context_ref.at[:, :half]), (other_hbm, context_ref.at[:, half:])]
    later = [
        (gain_hbm, gain_ref),
        (points_hbm.at[pl.ds(base, half_rows)], points_ref),
        (out_own_hbm, out_ref.at[:half]),
        (out_other_hbm, out_ref.at[half:]),
    ]
    last = [
        (fc1_own_hbm, fc1_ref.at[:, :hidden_half]),
        (fc1_other_hbm, fc1_ref.at[:, hidden_half:]),
        (fc2_own_hbm, fc2_ref.at[:hidden_half]),
        (fc2_other_hbm, fc2_ref.at[hidden_half:]),
    ]
    copies = [pltpu.make_async_copy(*ends, in_sems.at[k]) for k, ends in enumerate(early + later + last)]
    early, later, last = copies[:3], copies[3:7], copies[7:]
    for copy in copies:
        copy.start()

    blocks = blocks_of(half_rows, TALL)
    for copy in early:
        copy.wait()
    for i, rows in enumerate(blocks):
        start = pl.multiple_of(base + i * TALL, TALL)
        context = unorder(rank_ref, start, TALL, length, shards, context_ref)
        if i == 0:
            for copy in later:
                copy.wait()
        attn_out = dot(context, out_ref[...])
        middle = (points_ref[rows, :].astype(f32) + attn_out.astype(bf16).astype(f32)).astype(bf16)
        middle_ref[rows, :] = middle
        normed_ref[rows, :] = normalise(middle.astype(f32), gain_ref[...]) * 0.5
    for copy in last:
        copy.wait()

    def away(i):
        here = pl.ds(pl.multiple_of(i * TALL, TALL), TALL)
        there = pl.ds(pl.multiple_of(base + i * TALL, TALL), TALL)
        return pltpu.make_async_copy(done_ref.at[here], whole_hbm.at[there], sems.at[i])

    chunks = blocks_of(2 * hidden_half, TALL)

    def mlp(i, carry):
        here = pl.ds(pl.multiple_of(i * TALL, TALL), TALL)
        normed = normed_ref[here, :]
        total = middle_ref[here, :].astype(f32)
        half_hidden = dot(normed, fc1_ref[:, chunks[0]])
        for k, chunk in enumerate(chunks):
            ahead = dot(normed, fc1_ref[:, chunks[k + 1]]) if k + 1 < len(chunks) else None
            total = total + dot(gelu_of_half(half_hidden).astype(bf16), fc2_ref[chunk, :])
            half_hidden = ahead
        done_ref[here, :] = total.astype(bf16)
        away(i).start()
        return carry

    lax.fori_loop(0, half_rows // TALL, mlp, 0)
    for i in range(half_rows // TALL):
        away(i).wait()


def finish(shards, rank_row, gain_row, points, *arrays):
    length, features = points.shape
    half_rows = length // 2
    hidden = 2 * arrays[-1].shape[0]
    return pl.pallas_call(
        functools.partial(finish_kernel, shards),
        out_shape=(
            jax.ShapeDtypeStruct((half_rows, features), bf16),
            jax.ShapeDtypeStruct((length, features), bf16),
        ),
        in_specs=[ANYWHERE] * 11,
        out_specs=(pl.BlockSpec(memory_space=pltpu.VMEM), ANYWHERE),
        scratch_shapes=[
            pltpu.VMEM((1, length), jnp.int32),
            pltpu.VMEM((1, features), f32),
            pltpu.VMEM((half_rows, features), bf16),
            pltpu.VMEM((length, features), bf16),
            pltpu.VMEM((features, features), bf16),
            pltpu.VMEM((features, hidden), bf16),
            pltpu.VMEM((hidden, features), bf16),
            pltpu.VMEM((half_rows, features), bf16),
            pltpu.VMEM((half_rows, features), bf16),
            pltpu.SemaphoreType.DMA((11,)),
            pltpu.SemaphoreType.DMA((half_rows // TALL,)),
        ],
        compiler_params=params(),
        cost_estimate=pl.CostEstimate(
            flops=2 * half_rows * features * (length + 9 * features),
            bytes_accessed=16 * length * features,
            transcendentals=half_rows * 4 * features,
        ),
    )(rank_row, gain_row, points, *arrays)


def across(values):
    return lax.ppermute(values, "mp", [(0, 1), (1, 0)])


def exchange(rows, shards):
    length, columns = rows.shape
    cells = rows.reshape(shards, length // shards, columns)
    return lax.all_to_all(cells, "space", split_axis=0, concat_axis=0, tiled=True).reshape(length, columns)


def body(points, curve_rank, patch_counts, norm_gain_attn, w_qkv, w_out, norm_gain_mlp, w_fc1, w_fc2):
    shards = lax.axis_size("space")
    length, features = points.shape
    rank_row = curve_rank.reshape(1, length)
    own = exchange(order_for_owners(shards, rank_row, norm_gain_attn.reshape(1, features), points), shards)
    swapped = across(w_fc1), across(w_fc2), across(w_out)
    other = across(own)
    context = attend(patch_counts, own, other, w_qkv)
    context, (other_fc1, other_fc2, other_out) = lax.optimization_barrier((context, swapped))
    returned = exchange(context, shards)
    done, whole = finish(
        shards,
        rank_row,
        norm_gain_mlp.reshape(1, features),
        points,
        returned,
        across(returned),
        w_out,
        other_out,
        w_fc1,
        other_fc1,
        w_fc2,
        other_fc2,
    )
    start = (1 - lax.axis_index("mp")) * (length // 2)
    return lax.dynamic_update_slice(whole, across(done), (start, 0))


def solution(mesh):
    placed = (
        P("space", None),
        P("space"),
        P("space", None),
        P(),
        P(None, None, "mp"),
        P("mp", None),
        P(),
        P(None, "mp"),
        P("mp", None),
    )
    return jax.shard_map(
        body, mesh=mesh, in_specs=placed, out_specs=P("space", None), check_vma=False
    )
```

```python
import functools
import math

import jax
import jax.numpy as jnp
from jax import lax
from jax.experimental import pallas as pl
from jax.experimental.pallas import tpu as pltpu
from jax.sharding import PartitionSpec as P

HDIM = 64
LANES = 128
ROWS = 256
TALL = 512
KEYS = 256
PADDED = HDIM + 16
EPSILON = 1e-06
FAR = 1e30
SAFE = 105.0
VMEM_BYTES = 58 * 1024 * 1024
SMALL_BYTES = 30 * 1024 * 1024

f32 = jnp.float32
bf16 = jnp.bfloat16

ANYWHERE = pl.BlockSpec(memory_space=pl.ANY)
SCALARS = pl.BlockSpec(memory_space=pltpu.SMEM)


def normalise(values, gain_row):
    average = jnp.mean(values, axis=-1, keepdims=True)
    centred = values - average
    second = jnp.mean(centred * centred, axis=-1, keepdims=True)
    return (centred * lax.rsqrt(second + EPSILON) * gain_row).astype(bf16)


def dot(left, right):
    return jnp.dot(left, right, preferred_element_type=f32)


def split(number, size):
    if size & (size - 1) == 0:
        return number >> (size.bit_length() - 1), number & (size - 1)
    return number // size, number % size


def slots(rank, length, shards):
    cell = length // shards
    owner, within = split(rank, length)
    return owner * cell + within - lax.axis_index("space") * cell


def one_hot(rows_at, columns_at):
    if columns_at.shape[1] <= 1 << 15:
        rows_at, columns_at = rows_at.astype(jnp.int16), columns_at.astype(jnp.int16)
    one, nil = jnp.ones((), bf16), jnp.zeros((), bf16)
    return jnp.concatenate(
        [
            jnp.where(rows_at == columns_at[:, k : k + LANES], one, nil)
            for k in range(0, columns_at.shape[1], LANES)
        ],
        axis=1,
    )


def blocks_of(length, rows=ROWS):
    return [slice(i * rows, (i + 1) * rows) for i in range(length // rows)]


def params(limit=VMEM_BYTES):
    return pltpu.CompilerParams(vmem_limit_bytes=limit)


def send_kernel(shards, rank_hbm, gain_hbm, points_hbm, out_ref, rank_ref, gain_ref, points_ref, half_ref, small, large):
    length, features = points_ref.shape
    half = features // 2
    core = lax.axis_index("mp")
    gain_copy = pltpu.make_async_copy(gain_hbm, gain_ref, small.at[0])
    rank_copy = pltpu.make_async_copy(rank_hbm, rank_ref, small.at[1])
    rows_of = blocks_of(length)
    copies = [
        pltpu.make_async_copy(points_hbm.at[rows], points_ref.at[rows], large.at[i])
        for i, rows in enumerate(rows_of)
    ]
    gain_copy.start()
    for copy in copies:
        copy.start()
    rank_copy.start()
    gain_copy.wait()
    for copy, rows in zip(copies, rows_of):
        copy.wait()
        normed = normalise(points_ref[rows, :].astype(f32), gain_ref[...])
        half_ref[rows, :] = jnp.where(core == 0, normed[:, :half], normed[:, half:])
    rank_copy.wait()
    slot = slots(rank_ref[...], length, shards)

    place = lax.broadcasted_iota(jnp.int32, (TALL, LANES), 0)
    for i, rows in enumerate(blocks_of(length, TALL)):
        out_ref[rows, :] = dot(one_hot(place + i * TALL, slot), half_ref[...]).astype(bf16)


def order_for_owners(shards, rank_row, gain_row, points):
    length, features = points.shape
    return pl.pallas_call(
        functools.partial(send_kernel, shards),
        out_shape=jax.ShapeDtypeStruct((length, features // 2), bf16),
        in_specs=[ANYWHERE] * 3,
        out_specs=pl.BlockSpec(memory_space=pltpu.VMEM),
        scratch_shapes=[
            pltpu.VMEM((1, length), jnp.int32),
            pltpu.VMEM((1, features), f32),
            pltpu.VMEM((length, features), bf16),
            pltpu.VMEM((length, features // 2), bf16),
            pltpu.SemaphoreType.DMA((2,)),
            pltpu.SemaphoreType.DMA((length // ROWS,)),
        ],
        compiler_params=params(),
        cost_estimate=pl.CostEstimate(
            flops=length * length * features, bytes_accessed=4 * length * features, transcendentals=0
        ),
    )(rank_row, gain_row, points)


def attend_kernel(
    counts_ref, own_ref, other_ref, weight_hbm, out_hbm, w_ref, q_ref, k_ref, v_ref, out_ref, sum_ref, w_sems, out_sems
):
    length, half = own_ref.shape
    tiles = counts_ref.shape[1]
    pairs = out_ref.shape[0]
    core = lax.axis_index("mp")
    scale = math.log2(math.e) / math.sqrt(HDIM)

    copies = [
        pltpu.make_async_copy(
            weight_hbm.at[j, pl.ds(pl.multiple_of(at * half, half), half)],
            w_ref.at[k * half : (k + 1) * half, j * pairs * LANES : (j + 1) * pairs * LANES],
            w_sems.at[2 * j + k],
        )
        for j in range(3)
        for k, at in enumerate((core, 1 - core))
    ]
    for copy in copies:
        copy.start()

    starts = [jnp.int32(0)]
    for t in range(tiles):
        starts.append(starts[-1] + counts_ref[0, t])
    lane = lax.broadcasted_iota(jnp.int32, (1, LANES), 1)
    first = jnp.full((1, LANES), length, jnp.int32)
    last = jnp.zeros((1, LANES), jnp.int32)
    for t in range(tiles):
        first = jnp.where(lane == HDIM + t, starts[t], first)
        last = jnp.where(lane == HDIM + t, starts[t + 1], last)
    flags = jnp.logical_and(lane >= HDIM, lane < HDIM + tiles)
    low_lanes = lane < HDIM
    v_ref[:, HDIM:, :] = jnp.ones((2 * pairs, PADDED - HDIM, length), bf16)
    for copy in copies:
        copy.wait()

    most = [[jnp.zeros((1, 1), f32)] * 2 for _ in range(pairs)]

    def squares(values):
        return jnp.max(jnp.sum(values * values, axis=1, keepdims=True), axis=0, keepdims=True)

    for i, rows in enumerate(blocks_of(length, TALL)):
        spread = dot(own_ref[rows, :], w_ref[:half, :]) + dot(other_ref[rows, :], w_ref[half:, :])
        place = lax.broadcasted_iota(jnp.int32, (TALL, LANES), 0) + i * TALL
        inside = jnp.logical_and(place >= first, place < last)
        q_flag = jnp.where(inside, 1.0, 0.0)
        k_flag = jnp.where(jnp.logical_and(flags, jnp.logical_not(inside)), -FAR, 0.0)
        for pair in range(pairs):
            q, k, v = (spread[:, (j * pairs + pair) * LANES : (j * pairs + pair + 1) * LANES] for j in range(3))
            q = q * scale
            most[pair] = [jnp.maximum(old, squares(new)) for old, new in zip(most[pair], (q, k))]
            q_ref[2 * pair, rows, :] = jnp.where(low_lanes, q, q_flag).astype(bf16)
            q_ref[2 * pair + 1, rows, :] = jnp.where(low_lanes, pltpu.roll(q, HDIM, 1), q_flag).astype(bf16)
            k_ref[2 * pair, rows, :] = jnp.where(low_lanes, k, k_flag).astype(bf16)
            k_ref[2 * pair + 1, rows, :] = jnp.where(low_lanes, pltpu.roll(k, HDIM, 1), k_flag).astype(bf16)
            v = jnp.transpose(v).astype(bf16)
            v_ref[2 * pair, :HDIM, rows] = v[:HDIM]
            v_ref[2 * pair + 1, :HDIM, rows] = v[HDIM:]

    bound = functools.reduce(jnp.maximum, [q_most * k_most for q_most, k_most in most])
    safe = jnp.max(bound) < SAFE * SAFE

    def score(h, rows, keys):
        return lax.dot_general(
            k_ref[h, keys, :], q_ref[h, rows, :], (((1,), (1,)), ((), ())), preferred_element_type=f32
        )

    def add_keys(rows, keys):
        ahead = score(0, rows, keys)
        for h in range(2 * pairs):
            scores = ahead
            ahead = score(h + 1, rows, keys) if h + 1 < 2 * pairs else None
            sum_ref[h] += dot(v_ref[h, :, keys], jnp.exp2(scores).astype(bf16))

    def add_shifted(h, rows):
        scores = score(h, rows, slice(None))
        scores = scores - jnp.max(scores, axis=0, keepdims=True)
        sum_ref[h] = dot(v_ref[h], jnp.exp2(scores).astype(bf16))

    def send_out(i, pair):
        rows = pl.ds(pl.multiple_of(i * TALL, TALL), TALL)
        return pltpu.make_async_copy(
            out_ref.at[pair, rows], out_hbm.at[rows, pair * LANES : (pair + 1) * LANES], out_sems.at[i, pair]
        )

    def query_block(i, carry):
        begin = i * TALL
        rows = pl.ds(pl.multiple_of(begin, TALL), TALL)
        low, high = jnp.int32(0), jnp.int32(length)
        for t in range(tiles):
            low = jnp.where(starts[t] <= begin, starts[t], low)
            end = starts[tiles - t]
            high = jnp.where(end >= begin + TALL, end, high)
        low = (low // LANES) * LANES
        blocks = (high - low + KEYS - 1) // KEYS
        start = jnp.minimum(low, length - blocks * KEYS)

        @pl.when(safe)
        def _():
            sum_ref[...] = jnp.zeros_like(sum_ref)

            def step(j, carry):
                add_keys(rows, pl.ds(pl.multiple_of(start + j * KEYS, LANES), KEYS))
                return carry

            lax.fori_loop(0, blocks, step, 0)

        @pl.when(jnp.logical_not(safe))
        def _():
            def step(h, carry):
                add_shifted(h, rows)
                return carry

            lax.fori_loop(0, 2 * pairs, step, 0)

        for pair in range(pairs):
            both = sum_ref[2 * pair], sum_ref[2 * pair + 1]
            value = jnp.concatenate([head[:HDIM] / head[HDIM : HDIM + 1] for head in both], axis=0)
            out_ref[pair, rows, :] = jnp.transpose(value).astype(bf16)
        for pair in range(pairs):
            send_out(i, pair).start()
        return carry

    lax.fori_loop(0, length // TALL, query_block, 0)
    for i in range(length // TALL):
        for pair in range(pairs):
            send_out(i, pair).wait()


def attend(counts, own, other, w_qkv):
    length, half = own.shape
    features, columns = w_qkv.shape[1:]
    heads = columns // HDIM
    held = pl.BlockSpec(memory_space=pltpu.VMEM)
    return pl.pallas_call(
        attend_kernel,
        out_shape=jax.ShapeDtypeStruct((length, columns), bf16),
        in_specs=[SCALARS, held, held, ANYWHERE],
        out_specs=ANYWHERE,
        scratch_shapes=[
            pltpu.VMEM((features, 3 * columns), bf16),
            pltpu.VMEM((heads, length, LANES), bf16),
            pltpu.VMEM((heads, length, LANES), bf16),
            pltpu.VMEM((heads, PADDED, length), bf16),
            pltpu.VMEM((heads // 2, length, LANES), bf16),
            pltpu.VMEM((heads, PADDED, TALL), f32),
            pltpu.SemaphoreType.DMA((6,)),
            pltpu.SemaphoreType.DMA((length // TALL, heads // 2)),
        ],
        compiler_params=params(SMALL_BYTES),
        cost_estimate=pl.CostEstimate(
            flops=64 * length * length * HDIM, bytes_accessed=8 * length * half, transcendentals=4 * length * length
        ),
    )(counts, own, other, w_qkv)


def unorder(rank_ref, start, rows, length, shards, context_ref):
    slot = slots(rank_ref[:, pl.ds(start, rows)], length, shards)
    slot = jnp.transpose(jnp.broadcast_to(slot, (LANES, rows)))
    place = lax.broadcasted_iota(jnp.int32, (1, length), 1)
    return dot(one_hot(slot, place), context_ref[...]).astype(bf16)


def gelu_of_half(h):
    inner = 2 * math.sqrt(2 / math.pi)
    return h + h * jnp.tanh(h * (inner + (4 * 0.044715 * inner) * (h * h)))


def finish_kernel(
    shards,
    rank_hbm,
    gain_hbm,
    points_hbm,
    own_hbm,
    other_hbm,
    out_own_hbm,
    out_other_hbm,
    fc1_own_hbm,
    fc1_other_hbm,
    fc2_own_hbm,
    fc2_other_hbm,
    done_ref,
    whole_hbm,
    rank_ref,
    gain_ref,
    points_ref,
    context_ref,
    out_ref,
    fc1_ref,
    fc2_ref,
    middle_ref,
    normed_ref,
    in_sems,
    sems,
):
    length = context_ref.shape[0]
    half_rows = done_ref.shape[0]
    base = pl.multiple_of(lax.axis_index("mp") * half_rows, half_rows)
    hidden_half = fc2_own_hbm.shape[0]
    half = out_own_hbm.shape[0]
    early = [(rank_hbm, rank_ref), (own_hbm, context_ref.at[:, :half]), (other_hbm, context_ref.at[:, half:])]
    later = [
        (gain_hbm, gain_ref),
        (points_hbm.at[pl.ds(base, half_rows)], points_ref),
        (out_own_hbm, out_ref.at[:half]),
        (out_other_hbm, out_ref.at[half:]),
    ]
    last = [
        (fc1_own_hbm, fc1_ref.at[:, :hidden_half]),
        (fc1_other_hbm, fc1_ref.at[:, hidden_half:]),
        (fc2_own_hbm, fc2_ref.at[:hidden_half]),
        (fc2_other_hbm, fc2_ref.at[hidden_half:]),
    ]
    copies = [pltpu.make_async_copy(*ends, in_sems.at[k]) for k, ends in enumerate(early + later + last)]
    early, later, last = copies[:3], copies[3:7], copies[7:]
    for copy in copies:
        copy.start()

    blocks = blocks_of(half_rows, TALL)
    for copy in early:
        copy.wait()
    for i, rows in enumerate(blocks):
        start = pl.multiple_of(base + i * TALL, TALL)
        context = unorder(rank_ref, start, TALL, length, shards, context_ref)
        if i == 0:
            for copy in later:
                copy.wait()
        attn_out = dot(context, out_ref[...])
        middle = (points_ref[rows, :].astype(f32) + attn_out.astype(bf16).astype(f32)).astype(bf16)
        middle_ref[rows, :] = middle
        normed_ref[rows, :] = normalise(middle.astype(f32), gain_ref[...]) * 0.5
    for copy in last:
        copy.wait()

    def away(i):
        here = pl.ds(pl.multiple_of(i * TALL, TALL), TALL)
        there = pl.ds(pl.multiple_of(base + i * TALL, TALL), TALL)
        return pltpu.make_async_copy(done_ref.at[here], whole_hbm.at[there], sems.at[i])

    chunks = blocks_of(2 * hidden_half, TALL)

    def mlp(i, carry):
        here = pl.ds(pl.multiple_of(i * TALL, TALL), TALL)
        normed = normed_ref[here, :]
        total = middle_ref[here, :].astype(f32)
        half_hidden = dot(normed, fc1_ref[:, chunks[0]])
        for k, chunk in enumerate(chunks):
            ahead = dot(normed, fc1_ref[:, chunks[k + 1]]) if k + 1 < len(chunks) else None
            total = total + dot(gelu_of_half(half_hidden).astype(bf16), fc2_ref[chunk, :])
            half_hidden = ahead
        done_ref[here, :] = total.astype(bf16)
        away(i).start()
        return carry

    lax.fori_loop(0, half_rows // TALL, mlp, 0)
    for i in range(half_rows // TALL):
        away(i).wait()


def finish(shards, rank_row, gain_row, points, *arrays):
    length, features = points.shape
    half_rows = length // 2
    hidden = 2 * arrays[-1].shape[0]
    return pl.pallas_call(
        functools.partial(finish_kernel, shards),
        out_shape=(
            jax.ShapeDtypeStruct((half_rows, features), bf16),
            jax.ShapeDtypeStruct((length, features), bf16),
        ),
        in_specs=[ANYWHERE] * 11,
        out_specs=(pl.BlockSpec(memory_space=pltpu.VMEM), ANYWHERE),
        scratch_shapes=[
            pltpu.VMEM((1, length), jnp.int32),
            pltpu.VMEM((1, features), f32),
            pltpu.VMEM((half_rows, features), bf16),
            pltpu.VMEM((length, features), bf16),
            pltpu.VMEM((features, features), bf16),
            pltpu.VMEM((features, hidden), bf16),
            pltpu.VMEM((hidden, features), bf16),
            pltpu.VMEM((half_rows, features), bf16),
            pltpu.VMEM((half_rows, features), bf16),
            pltpu.SemaphoreType.DMA((11,)),
            pltpu.SemaphoreType.DMA((half_rows // TALL,)),
        ],
        compiler_params=params(),
        cost_estimate=pl.CostEstimate(
            flops=2 * half_rows * features * (length + 9 * features),
            bytes_accessed=16 * length * features,
            transcendentals=half_rows * 4 * features,
        ),
    )(rank_row, gain_row, points, *arrays)


def across(values):
    return lax.ppermute(values, "mp", [(0, 1), (1, 0)])


def exchange(rows, shards):
    length, columns = rows.shape
    cells = rows.reshape(shards, length // shards, columns)
    return lax.all_to_all(cells, "space", split_axis=0, concat_axis=0, tiled=True).reshape(length, columns)


def body(points, curve_rank, patch_counts, norm_gain_attn, w_qkv, w_out, norm_gain_mlp, w_fc1, w_fc2):
    shards = lax.axis_size("space")
    length, features = points.shape
    rank_row = curve_rank.reshape(1, length)
    own = exchange(order_for_owners(shards, rank_row, norm_gain_attn.reshape(1, features), points), shards)
    swapped = across(w_fc1), across(w_fc2), across(w_out)
    other = across(own)
    context = attend(patch_counts, own, other, w_qkv)
    context, (other_fc1, other_fc2, other_out) = lax.optimization_barrier((context, swapped))
    returned = exchange(context, shards)
    done, whole = finish(
        shards,
        rank_row,
        norm_gain_mlp.reshape(1, features),
        points,
        returned,
        across(returned),
        w_out,
        other_out,
        w_fc1,
        other_fc1,
        w_fc2,
        other_fc2,
    )
    start = (1 - lax.axis_index("mp")) * (length // 2)
    return lax.dynamic_update_slice(whole, across(done), (start, 0))


def solution(mesh):
    placed = (
        P("space", None),
        P("space"),
        P("space", None),
        P(),
        P(None, None, "mp"),
        P("mp", None),
        P(),
        P(None, "mp"),
        P("mp", None),
    )
    return jax.shard_map(
        body, mesh=mesh, in_specs=placed, out_specs=P("space", None), check_vma=False
    )
```

```python
import functools
import math

import jax
import jax.numpy as jnp
from jax import lax
from jax.experimental import pallas as pl
from jax.experimental.pallas import tpu as pltpu
from jax.sharding import PartitionSpec as P

HDIM = 64
LANES = 128
ROWS = 256
TALL = 512
KEYS = 256
PADDED = HDIM + 16
EPSILON = 1e-06
FAR = 1e30
VMEM_BYTES = 58 * 1024 * 1024
SMALL_BYTES = 30 * 1024 * 1024

f32 = jnp.float32
bf16 = jnp.bfloat16

ANYWHERE = pl.BlockSpec(memory_space=pl.ANY)
SCALARS = pl.BlockSpec(memory_space=pltpu.SMEM)


def normalise(values, gain_row):
    average = jnp.mean(values, axis=-1, keepdims=True)
    centred = values - average
    second = jnp.mean(centred * centred, axis=-1, keepdims=True)
    return (centred * lax.rsqrt(second + EPSILON) * gain_row).astype(bf16)


def dot(left, right):
    return jnp.dot(left, right, preferred_element_type=f32)


def split(number, size):
    if size & (size - 1) == 0:
        return number >> (size.bit_length() - 1), number & (size - 1)
    return number // size, number % size


def slots(rank, length, shards):
    cell = length // shards
    owner, within = split(rank, length)
    return owner * cell + within - lax.axis_index("space") * cell


def one_hot(rows_at, columns_at):
    if columns_at.shape[1] <= 1 << 15:
        rows_at, columns_at = rows_at.astype(jnp.int16), columns_at.astype(jnp.int16)
    one, nil = jnp.ones((), bf16), jnp.zeros((), bf16)
    return jnp.concatenate(
        [
            jnp.where(rows_at == columns_at[:, k : k + LANES], one, nil)
            for k in range(0, columns_at.shape[1], LANES)
        ],
        axis=1,
    )


def blocks_of(length, rows=ROWS):
    return [slice(i * rows, (i + 1) * rows) for i in range(length // rows)]


def params(limit=VMEM_BYTES):
    return pltpu.CompilerParams(vmem_limit_bytes=limit)


def send_kernel(shards, rank_hbm, gain_hbm, points_hbm, out_ref, rank_ref, gain_ref, points_ref, half_ref, small, large):
    length, features = points_ref.shape
    half = features // 2
    core = lax.axis_index("mp")
    gain_copy = pltpu.make_async_copy(gain_hbm, gain_ref, small.at[0])
    rank_copy = pltpu.make_async_copy(rank_hbm, rank_ref, small.at[1])
    rows_of = blocks_of(length)
    copies = [
        pltpu.make_async_copy(points_hbm.at[rows], points_ref.at[rows], large.at[i])
        for i, rows in enumerate(rows_of)
    ]
    gain_copy.start()
    for copy in copies:
        copy.start()
    rank_copy.start()
    gain_copy.wait()
    for copy, rows in zip(copies, rows_of):
        copy.wait()
        normed = normalise(points_ref[rows, :].astype(f32), gain_ref[...])
        half_ref[rows, :] = jnp.where(core == 0, normed[:, :half], normed[:, half:])
    rank_copy.wait()
    slot = slots(rank_ref[...], length, shards)

    place = lax.broadcasted_iota(jnp.int32, (TALL, LANES), 0)
    for i, rows in enumerate(blocks_of(length, TALL)):
        out_ref[rows, :] = dot(one_hot(place + i * TALL, slot), half_ref[...]).astype(bf16)


def order_for_owners(shards, rank_row, gain_row, points):
    length, features = points.shape
    return pl.pallas_call(
        functools.partial(send_kernel, shards),
        out_shape=jax.ShapeDtypeStruct((length, features // 2), bf16),
        in_specs=[ANYWHERE] * 3,
        out_specs=pl.BlockSpec(memory_space=pltpu.VMEM),
        scratch_shapes=[
            pltpu.VMEM((1, length), jnp.int32),
            pltpu.VMEM((1, features), f32),
            pltpu.VMEM((length, features), bf16),
            pltpu.VMEM((length, features // 2), bf16),
            pltpu.SemaphoreType.DMA((2,)),
            pltpu.SemaphoreType.DMA((length // ROWS,)),
        ],
        compiler_params=params(),
        cost_estimate=pl.CostEstimate(
            flops=length * length * features, bytes_accessed=4 * length * features, transcendentals=0
        ),
    )(rank_row, gain_row, points)


def attend_kernel(
    pair,
    staged,
    counts_ref,
    own,
    other,
    weight_hbm,
    out_hbm,
    w_ref,
    q_ref,
    k_ref,
    v_ref,
    out_ref,
    w_sems,
    out_sems,
    x_ref=None,
    x_sems=None,
):
    length = out_ref.shape[0]
    features = w_ref.shape[0]
    half = features // 2
    tiles = counts_ref.shape[1]
    core = lax.axis_index("mp")
    scale = math.log2(math.e) / math.sqrt(HDIM)

    copies = [
        pltpu.make_async_copy(
            weight_hbm.at[
                j, pl.ds(pl.multiple_of(at * half, half), half), pair * LANES : (pair + 1) * LANES
            ],
            w_ref.at[k * half : (k + 1) * half, j * LANES : (j + 1) * LANES],
            w_sems.at[2 * j + k],
        )
        for j in range(3)
        for k, at in enumerate((core, 1 - core))
    ]
    if not staged:
        copies += [
            pltpu.make_async_copy(source, x_ref.at[:, k * half : (k + 1) * half], x_sems.at[k])
            for k, source in enumerate((own, other))
        ]
    for copy in copies:
        copy.start()

    starts = [jnp.int32(0)]
    for t in range(tiles):
        starts.append(starts[-1] + counts_ref[0, t])
    lane = lax.broadcasted_iota(jnp.int32, (1, LANES), 1)
    first = jnp.full((1, LANES), length, jnp.int32)
    last = jnp.zeros((1, LANES), jnp.int32)
    for t in range(tiles):
        first = jnp.where(lane == HDIM + t, starts[t], first)
        last = jnp.where(lane == HDIM + t, starts[t + 1], last)
    flags = jnp.logical_and(lane >= HDIM, lane < HDIM + tiles)
    low_lanes = lane < HDIM

    for copy in copies:
        copy.wait()

    v_ref[:, HDIM:, :] = jnp.ones((2, PADDED - HDIM, length), bf16)

    def project(i):
        rows = slice(i * TALL, (i + 1) * TALL)
        if staged:
            spread = dot(own[rows, :], w_ref[:half, :]) + dot(other[rows, :], w_ref[half:, :])
        else:
            spread = dot(x_ref[rows, :], w_ref[...])
        q, k, v = (spread[:, j * LANES : (j + 1) * LANES] for j in range(3))
        q = q * scale
        place = lax.broadcasted_iota(jnp.int32, (TALL, LANES), 0) + i * TALL
        inside = jnp.logical_and(place >= first, place < last)
        q_flag = jnp.where(inside, 1.0, 0.0)
        k_flag = jnp.where(jnp.logical_and(flags, jnp.logical_not(inside)), -FAR, 0.0)
        q_ref[0, rows, :] = jnp.where(low_lanes, q, q_flag).astype(bf16)
        q_ref[1, rows, :] = jnp.where(low_lanes, pltpu.roll(q, HDIM, 1), q_flag).astype(bf16)
        k_ref[0, rows, :] = jnp.where(low_lanes, k, k_flag).astype(bf16)
        k_ref[1, rows, :] = jnp.where(low_lanes, pltpu.roll(k, HDIM, 1), k_flag).astype(bf16)
        v = jnp.transpose(v).astype(bf16)
        v_ref[0, :HDIM, rows] = v[:HDIM]
        v_ref[1, :HDIM, rows] = v[HDIM:]

    for i in range(length // TALL):
        project(i)

    def weigh(scores):
        return jnp.exp2(scores - jnp.max(scores, axis=0, keepdims=True)).astype(bf16)

    def send_out(i):
        rows = pl.ds(pl.multiple_of(i * TALL, TALL), TALL)
        return pltpu.make_async_copy(out_ref.at[rows], out_hbm.at[rows], out_sems.at[i])

    def query_block(i, carry):
        begin = i * TALL
        rows = pl.ds(pl.multiple_of(begin, TALL), TALL)
        low, high = jnp.int32(0), jnp.int32(length)
        for t in range(tiles):
            low = jnp.where(starts[t] <= begin, starts[t], low)
            end = starts[tiles - t]
            high = jnp.where(end >= begin + TALL, end, high)
        low = (low // LANES) * LANES
        blocks = (high - low + KEYS - 1) // KEYS
        for n in range(TALL // KEYS, length // KEYS + 1):

            @pl.when(blocks == n)
            def _(n=n):
                start = pl.multiple_of(jnp.minimum(low, length - n * KEYS), LANES)
                keys = pl.ds(start, n * KEYS)
                scores = [
                    lax.dot_general(
                        k_ref[h, keys, :],
                        q_ref[h, rows, :],
                        (((1,), (1,)), ((), ())),
                        preferred_element_type=f32,
                    )
                    for h in range(2)
                ]
                sums = [dot(v_ref[h, :, keys], weigh(scores[h])) for h in range(2)]
                value = jnp.concatenate([both[:HDIM] / both[HDIM : HDIM + 1] for both in sums], axis=0)
                out_ref[rows, :] = jnp.transpose(value).astype(bf16)

        send_out(i).start()
        return carry

    lax.fori_loop(0, length // TALL, query_block, 0)
    for i in range(length // TALL):
        send_out(i).wait()


def attend(pair, staged, counts, own, other, w_qkv):
    length, half = own.shape
    features = 2 * half
    held = pl.BlockSpec(memory_space=pltpu.VMEM) if staged else ANYWHERE
    scratch = [
        pltpu.VMEM((features, 3 * LANES), bf16),
        pltpu.VMEM((2, length, LANES), bf16),
        pltpu.VMEM((2, length, LANES), bf16),
        pltpu.VMEM((2, PADDED, length), bf16),
        pltpu.VMEM((length, LANES), bf16),
        pltpu.SemaphoreType.DMA((6,)),
        pltpu.SemaphoreType.DMA((length // TALL,)),
    ]
    if not staged:
        scratch += [pltpu.VMEM((length, features), bf16), pltpu.SemaphoreType.DMA((2,))]
    return pl.pallas_call(
        functools.partial(attend_kernel, pair, staged),
        out_shape=jax.ShapeDtypeStruct((length, LANES), bf16),
        in_specs=[SCALARS, held, held, ANYWHERE],
        out_specs=ANYWHERE,
        scratch_shapes=scratch,
        compiler_params=params(SMALL_BYTES if staged else VMEM_BYTES),
        cost_estimate=pl.CostEstimate(
            flops=32 * length * length * HDIM, bytes_accessed=8 * length * half, transcendentals=2 * length * length
        ),
    )(counts, own, other, w_qkv)


def unorder(rank_ref, start, rows, length, shards, context_ref):
    slot = slots(rank_ref[:, pl.ds(start, rows)], length, shards)
    slot = jnp.transpose(jnp.broadcast_to(slot, (LANES, rows)))
    place = lax.broadcasted_iota(jnp.int32, (1, length), 1)
    return dot(one_hot(slot, place), context_ref[...]).astype(bf16)


def unorder_kernel(shards, rank_hbm, own_hbm, other_hbm, out_ref, rank_ref, context_ref, sems):
    length = context_ref.shape[0]
    half_rows = out_ref.shape[0]
    base = lax.axis_index("mp") * half_rows
    copies = [
        pltpu.make_async_copy(rank_hbm, rank_ref, sems.at[0]),
        pltpu.make_async_copy(own_hbm, context_ref.at[:, :LANES], sems.at[1]),
        pltpu.make_async_copy(other_hbm, context_ref.at[:, LANES:], sems.at[2]),
    ]
    for copy in copies:
        copy.start()
    for copy in copies:
        copy.wait()
    for i, rows in enumerate(blocks_of(half_rows, TALL)):
        start = pl.multiple_of(base + i * TALL, TALL)
        out_ref[rows, :] = unorder(rank_ref, start, TALL, length, shards, context_ref)


def unorder_pair(shards, rank_row, own, other):
    length = own.shape[0]
    half_rows = length // 2
    return pl.pallas_call(
        functools.partial(unorder_kernel, shards),
        out_shape=jax.ShapeDtypeStruct((half_rows, 2 * LANES), bf16),
        in_specs=[ANYWHERE] * 3,
        out_specs=pl.BlockSpec(memory_space=pltpu.VMEM),
        scratch_shapes=[
            pltpu.VMEM((1, length), jnp.int32),
            pltpu.VMEM((length, 2 * LANES), bf16),
            pltpu.SemaphoreType.DMA((3,)),
        ],
        compiler_params=params(),
        cost_estimate=pl.CostEstimate(
            flops=4 * half_rows * length * LANES, bytes_accessed=8 * length * LANES, transcendentals=0
        ),
    )(rank_row, own, other)


def gelu_of_half(h):
    inner = 2 * math.sqrt(2 / math.pi)
    return h + h * jnp.tanh(h * (inner + (4 * 0.044715 * inner) * (h * h)))


def finish_kernel(
    shards,
    rank_hbm,
    gain_hbm,
    points_hbm,
    first_hbm,
    own_hbm,
    other_hbm,
    out_own_hbm,
    out_other_hbm,
    fc1_own_hbm,
    fc1_other_hbm,
    fc2_own_hbm,
    fc2_other_hbm,
    done_a_ref,
    done_b_ref,
    whole_hbm,
    rank_ref,
    gain_ref,
    points_ref,
    first_ref,
    context_ref,
    out_ref,
    fc1_ref,
    fc2_ref,
    middle_ref,
    normed_ref,
    in_sems,
    sems,
):
    length = context_ref.shape[0]
    done_refs = done_a_ref, done_b_ref
    part = done_a_ref.shape[0]
    half_rows = 2 * part
    base = pl.multiple_of(lax.axis_index("mp") * half_rows, half_rows)
    hidden_half = fc2_own_hbm.shape[0]
    early = [
        (rank_hbm, rank_ref),
        (own_hbm, context_ref.at[:, :LANES]),
        (other_hbm, context_ref.at[:, LANES:]),
    ]
    later = [(first_hbm, first_ref), (gain_hbm, gain_ref), (points_hbm.at[pl.ds(base, half_rows)], points_ref)]
    later += [
        (ref.at[pair * LANES : (pair + 1) * LANES], out_ref.at[(2 * pair + k) * LANES : (2 * pair + k + 1) * LANES])
        for pair in range(2)
        for k, ref in enumerate((out_own_hbm, out_other_hbm))
    ]
    last = [
        (fc1_own_hbm, fc1_ref.at[:, :hidden_half]),
        (fc1_other_hbm, fc1_ref.at[:, hidden_half:]),
        (fc2_own_hbm, fc2_ref.at[:hidden_half]),
        (fc2_other_hbm, fc2_ref.at[hidden_half:]),
    ]
    copies = [pltpu.make_async_copy(*ends, in_sems.at[k]) for k, ends in enumerate(early + later + last)]
    early, later, last = copies[:3], copies[3:10], copies[10:]
    for copy in copies:
        copy.start()

    blocks = blocks_of(half_rows, part)
    for copy in early:
        copy.wait()
    for i, rows in enumerate(blocks):
        start = pl.multiple_of(base + i * part, part)
        second = unorder(rank_ref, start, part, length, shards, context_ref)
        if i == 0:
            for copy in later:
                copy.wait()
        split_at = 2 * LANES
        attn_out = dot(first_ref[rows, :], out_ref[:split_at, :]) + dot(second, out_ref[split_at:, :])
        middle = (points_ref[rows, :].astype(f32) + attn_out.astype(bf16).astype(f32)).astype(bf16)
        middle_ref[rows, :] = middle
        normed_ref[rows, :] = normalise(middle.astype(f32), gain_ref[...]) * 0.5
    for copy in last:
        copy.wait()

    chunks = blocks_of(2 * hidden_half, TALL)
    sends = []
    for i, rows in enumerate(blocks):
        normed = normed_ref[rows, :]
        total = middle_ref[rows, :].astype(f32)
        half_hidden = dot(normed, fc1_ref[:, chunks[0]])
        for k, chunk in enumerate(chunks):
            ahead = dot(normed, fc1_ref[:, chunks[k + 1]]) if k + 1 < len(chunks) else None
            total = total + dot(gelu_of_half(half_hidden).astype(bf16), fc2_ref[chunk, :])
            half_hidden = ahead
        done_refs[i][...] = total.astype(bf16)
        there = pl.ds(pl.multiple_of(base + i * part, part), part)
        sends.append(pltpu.make_async_copy(done_refs[i], whole_hbm.at[there], sems.at[i]))
        sends[i].start()
    for send in sends:
        send.wait()


def finish(shards, rank_row, gain_row, points, *arrays):
    length, features = points.shape
    half_rows = length // 2
    hidden = 2 * arrays[-1].shape[0]
    held = pl.BlockSpec(memory_space=pltpu.VMEM)
    return pl.pallas_call(
        functools.partial(finish_kernel, shards),
        out_shape=(
            jax.ShapeDtypeStruct((half_rows // 2, features), bf16),
            jax.ShapeDtypeStruct((half_rows // 2, features), bf16),
            jax.ShapeDtypeStruct((length, features), bf16),
        ),
        in_specs=[ANYWHERE] * 12,
        out_specs=(held, held, ANYWHERE),
        scratch_shapes=[
            pltpu.VMEM((1, length), jnp.int32),
            pltpu.VMEM((1, features), f32),
            pltpu.VMEM((half_rows, features), bf16),
            pltpu.VMEM((half_rows, 2 * LANES), bf16),
            pltpu.VMEM((length, 2 * LANES), bf16),
            pltpu.VMEM((features, features), bf16),
            pltpu.VMEM((features, hidden), bf16),
            pltpu.VMEM((hidden, features), bf16),
            pltpu.VMEM((half_rows, features), bf16),
            pltpu.VMEM((half_rows, features), bf16),
            pltpu.SemaphoreType.DMA((14,)),
            pltpu.SemaphoreType.DMA((2,)),
        ],
        compiler_params=params(),
        cost_estimate=pl.CostEstimate(
            flops=2 * half_rows * features * (length + 9 * features),
            bytes_accessed=16 * length * features,
            transcendentals=half_rows * 4 * features,
        ),
    )(rank_row, gain_row, points, *arrays)


def across(values):
    return lax.ppermute(values, "mp", [(0, 1), (1, 0)])


def exchange(rows, shards):
    length, columns = rows.shape
    cells = rows.reshape(shards, length // shards, columns)
    return lax.all_to_all(cells, "space", split_axis=0, concat_axis=0, tiled=True).reshape(length, columns)


def body(points, curve_rank, patch_counts, norm_gain_attn, w_qkv, w_out, norm_gain_mlp, w_fc1, w_fc2):
    shards = lax.axis_size("space")
    length, features = points.shape
    rank_row = curve_rank.reshape(1, length)
    own = exchange(order_for_owners(shards, rank_row, norm_gain_attn.reshape(1, features), points), shards)
    swapped = across(w_fc1), across(w_fc2), across(w_out)
    other = across(own)
    first_own = exchange(attend(0, True, patch_counts, own, other, w_qkv), shards)
    counts, (other_fc1, other_fc2, other_out) = lax.optimization_barrier((patch_counts, swapped))
    second_own = exchange(attend(1, False, counts, own, other, w_qkv), shards)
    first = unorder_pair(shards, rank_row, first_own, across(first_own))
    second_own, first = lax.optimization_barrier((second_own, first))
    *done, whole = finish(
        shards,
        rank_row,
        norm_gain_mlp.reshape(1, features),
        points,
        first,
        second_own,
        across(second_own),
        w_out,
        other_out,
        w_fc1,
        other_fc1,
        w_fc2,
        other_fc2,
    )
    start = (1 - lax.axis_index("mp")) * (length // 2)
    for i, rows in enumerate(done):
        whole = lax.dynamic_update_slice(whole, across(rows), (start + i * rows.shape[0], 0))
    return whole


def solution(mesh):
    placed = (
        P("space", None),
        P("space"),
        P("space", None),
        P(),
        P(None, None, "mp"),
        P("mp", None),
        P(),
        P(None, "mp"),
        P("mp", None),
    )
    return jax.shard_map(
        body, mesh=mesh, in_specs=placed, out_specs=P("space", None), check_vma=False
    )
```

```python
import functools
import math

import jax
import jax.numpy as jnp
from jax import lax
from jax.experimental import pallas as pl
from jax.experimental.pallas import tpu as pltpu
from jax.sharding import PartitionSpec as P

HDIM = 64
LANES = 128
ROWS = 256
TALL = 512
KEYS = 256
PADDED = HDIM + 16
EPSILON = 1e-06
FAR = 1e30
VMEM_BYTES = 58 * 1024 * 1024
SMALL_BYTES = 30 * 1024 * 1024

f32 = jnp.float32
bf16 = jnp.bfloat16

ANYWHERE = pl.BlockSpec(memory_space=pl.ANY)
SCALARS = pl.BlockSpec(memory_space=pltpu.SMEM)


def normalise(values, gain_row):
    average = jnp.mean(values, axis=-1, keepdims=True)
    centred = values - average
    second = jnp.mean(centred * centred, axis=-1, keepdims=True)
    return (centred * lax.rsqrt(second + EPSILON) * gain_row).astype(bf16)


def dot(left, right):
    return jnp.dot(left, right, preferred_element_type=f32)


def split(number, size):
    if size & (size - 1) == 0:
        return number >> (size.bit_length() - 1), number & (size - 1)
    return number // size, number % size


def slots(rank, length, shards):
    cell = length // shards
    owner, within = split(rank, length)
    return owner * cell + within - lax.axis_index("space") * cell


def one_hot(rows_at, columns_at):
    if columns_at.shape[1] <= 1 << 15:
        rows_at, columns_at = rows_at.astype(jnp.int16), columns_at.astype(jnp.int16)
    one, nil = jnp.ones((), bf16), jnp.zeros((), bf16)
    return jnp.concatenate(
        [
            jnp.where(rows_at == columns_at[:, k : k + LANES], one, nil)
            for k in range(0, columns_at.shape[1], LANES)
        ],
        axis=1,
    )


def blocks_of(length, rows=ROWS):
    return [slice(i * rows, (i + 1) * rows) for i in range(length // rows)]


def params(limit=VMEM_BYTES):
    return pltpu.CompilerParams(vmem_limit_bytes=limit)


def send_kernel(shards, rank_hbm, gain_hbm, points_hbm, out_ref, rank_ref, gain_ref, points_ref, half_ref, small, large):
    length, features = points_ref.shape
    half = features // 2
    core = lax.axis_index("mp")
    gain_copy = pltpu.make_async_copy(gain_hbm, gain_ref, small.at[0])
    rank_copy = pltpu.make_async_copy(rank_hbm, rank_ref, small.at[1])
    rows_of = blocks_of(length)
    copies = [
        pltpu.make_async_copy(points_hbm.at[rows], points_ref.at[rows], large.at[i])
        for i, rows in enumerate(rows_of)
    ]
    gain_copy.start()
    for copy in copies:
        copy.start()
    rank_copy.start()
    gain_copy.wait()
    for copy, rows in zip(copies, rows_of):
        copy.wait()
        normed = normalise(points_ref[rows, :].astype(f32), gain_ref[...])
        half_ref[rows, :] = jnp.where(core == 0, normed[:, :half], normed[:, half:])
    rank_copy.wait()
    slot = slots(rank_ref[...], length, shards)

    place = lax.broadcasted_iota(jnp.int32, (TALL, LANES), 0)
    for i, rows in enumerate(blocks_of(length, TALL)):
        out_ref[rows, :] = dot(one_hot(place + i * TALL, slot), half_ref[...]).astype(bf16)


def order_for_owners(shards, rank_row, gain_row, points):
    length, features = points.shape
    return pl.pallas_call(
        functools.partial(send_kernel, shards),
        out_shape=jax.ShapeDtypeStruct((length, features // 2), bf16),
        in_specs=[ANYWHERE] * 3,
        out_specs=pl.BlockSpec(memory_space=pltpu.VMEM),
        scratch_shapes=[
            pltpu.VMEM((1, length), jnp.int32),
            pltpu.VMEM((1, features), f32),
            pltpu.VMEM((length, features), bf16),
            pltpu.VMEM((length, features // 2), bf16),
            pltpu.SemaphoreType.DMA((2,)),
            pltpu.SemaphoreType.DMA((length // ROWS,)),
        ],
        compiler_params=params(),
        cost_estimate=pl.CostEstimate(
            flops=length * length * features, bytes_accessed=4 * length * features, transcendentals=0
        ),
    )(rank_row, gain_row, points)


def attend_kernel(
    counts_ref, own_ref, other_ref, weight_hbm, out_hbm, w_ref, q_ref, k_ref, v_ref, out_ref, w_sems, out_sems
):
    length, half = own_ref.shape
    tiles = counts_ref.shape[1]
    pairs = out_ref.shape[0]
    core = lax.axis_index("mp")
    scale = math.log2(math.e) / math.sqrt(HDIM)

    copies = [
        pltpu.make_async_copy(
            weight_hbm.at[j, pl.ds(pl.multiple_of(at * half, half), half)],
            w_ref.at[k * half : (k + 1) * half, j * pairs * LANES : (j + 1) * pairs * LANES],
            w_sems.at[2 * j + k],
        )
        for j in range(3)
        for k, at in enumerate((core, 1 - core))
    ]
    for copy in copies:
        copy.start()

    starts = [jnp.int32(0)]
    for t in range(tiles):
        starts.append(starts[-1] + counts_ref[0, t])
    lane = lax.broadcasted_iota(jnp.int32, (1, LANES), 1)
    first = jnp.full((1, LANES), length, jnp.int32)
    last = jnp.zeros((1, LANES), jnp.int32)
    for t in range(tiles):
        first = jnp.where(lane == HDIM + t, starts[t], first)
        last = jnp.where(lane == HDIM + t, starts[t + 1], last)
    flags = jnp.logical_and(lane >= HDIM, lane < HDIM + tiles)
    low_lanes = lane < HDIM
    v_ref[:, HDIM:, :] = jnp.ones((2 * pairs, PADDED - HDIM, length), bf16)
    for copy in copies:
        copy.wait()

    for i, rows in enumerate(blocks_of(length, TALL)):
        spread = dot(own_ref[rows, :], w_ref[:half, :]) + dot(other_ref[rows, :], w_ref[half:, :])
        place = lax.broadcasted_iota(jnp.int32, (TALL, LANES), 0) + i * TALL
        inside = jnp.logical_and(place >= first, place < last)
        q_flag = jnp.where(inside, 1.0, 0.0)
        k_flag = jnp.where(jnp.logical_and(flags, jnp.logical_not(inside)), -FAR, 0.0)
        for pair in range(pairs):
            q, k, v = (spread[:, (j * pairs + pair) * LANES : (j * pairs + pair + 1) * LANES] for j in range(3))
            q = q * scale
            q_ref[2 * pair, rows, :] = jnp.where(low_lanes, q, q_flag).astype(bf16)
            q_ref[2 * pair + 1, rows, :] = jnp.where(low_lanes, pltpu.roll(q, HDIM, 1), q_flag).astype(bf16)
            k_ref[2 * pair, rows, :] = jnp.where(low_lanes, k, k_flag).astype(bf16)
            k_ref[2 * pair + 1, rows, :] = jnp.where(low_lanes, pltpu.roll(k, HDIM, 1), k_flag).astype(bf16)
            v = jnp.transpose(v).astype(bf16)
            v_ref[2 * pair, :HDIM, rows] = v[:HDIM]
            v_ref[2 * pair + 1, :HDIM, rows] = v[HDIM:]

    def weigh(scores):
        return jnp.exp2(scores - jnp.max(scores, axis=0, keepdims=True)).astype(bf16)

    def send_out(i, pair):
        rows = pl.ds(pl.multiple_of(i * TALL, TALL), TALL)
        return pltpu.make_async_copy(
            out_ref.at[pair, rows], out_hbm.at[rows, pair * LANES : (pair + 1) * LANES], out_sems.at[i, pair]
        )

    def query_block(i, carry):
        begin = i * TALL
        rows = pl.ds(pl.multiple_of(begin, TALL), TALL)
        low, high = jnp.int32(0), jnp.int32(length)
        for t in range(tiles):
            low = jnp.where(starts[t] <= begin, starts[t], low)
            end = starts[tiles - t]
            high = jnp.where(end >= begin + TALL, end, high)
        low = (low // LANES) * LANES
        blocks = (high - low + KEYS - 1) // KEYS
        for n in range(TALL // KEYS, length // KEYS + 1):

            @pl.when(blocks == n)
            def _(n=n):
                start = pl.multiple_of(jnp.minimum(low, length - n * KEYS), LANES)
                keys = pl.ds(start, n * KEYS)

                def score(h):
                    return lax.dot_general(
                        k_ref[h, keys, :], q_ref[h, rows, :], (((1,), (1,)), ((), ())), preferred_element_type=f32
                    )

                ahead, sums = score(0), []
                for h in range(2 * pairs):
                    scores = ahead
                    ahead = score(h + 1) if h + 1 < 2 * pairs else None
                    sums.append(dot(v_ref[h, :, keys], weigh(scores)))
                for pair in range(pairs):
                    value = jnp.concatenate(
                        [both[:HDIM] / both[HDIM : HDIM + 1] for both in sums[2 * pair : 2 * pair + 2]], axis=0
                    )
                    out_ref[pair, rows, :] = jnp.transpose(value).astype(bf16)

        for pair in range(pairs):
            send_out(i, pair).start()
        return carry

    lax.fori_loop(0, length // TALL, query_block, 0)
    for i in range(length // TALL):
        for pair in range(pairs):
            send_out(i, pair).wait()


def attend(counts, own, other, w_qkv):
    length, half = own.shape
    features, columns = w_qkv.shape[1:]
    heads = columns // HDIM
    held = pl.BlockSpec(memory_space=pltpu.VMEM)
    return pl.pallas_call(
        attend_kernel,
        out_shape=jax.ShapeDtypeStruct((length, columns), bf16),
        in_specs=[SCALARS, held, held, ANYWHERE],
        out_specs=ANYWHERE,
        scratch_shapes=[
            pltpu.VMEM((features, 3 * columns), bf16),
            pltpu.VMEM((heads, length, LANES), bf16),
            pltpu.VMEM((heads, length, LANES), bf16),
            pltpu.VMEM((heads, PADDED, length), bf16),
            pltpu.VMEM((heads // 2, length, LANES), bf16),
            pltpu.SemaphoreType.DMA((6,)),
            pltpu.SemaphoreType.DMA((length // TALL, heads // 2)),
        ],
        compiler_params=params(SMALL_BYTES),
        cost_estimate=pl.CostEstimate(
            flops=64 * length * length * HDIM, bytes_accessed=8 * length * half, transcendentals=4 * length * length
        ),
    )(counts, own, other, w_qkv)


def unorder(rank_ref, start, rows, length, shards, context_ref):
    slot = slots(rank_ref[:, pl.ds(start, rows)], length, shards)
    slot = jnp.transpose(jnp.broadcast_to(slot, (LANES, rows)))
    place = lax.broadcasted_iota(jnp.int32, (1, length), 1)
    return dot(one_hot(slot, place), context_ref[...]).astype(bf16)


def gelu_of_half(h):
    inner = 2 * math.sqrt(2 / math.pi)
    return h + h * jnp.tanh(h * (inner + (4 * 0.044715 * inner) * (h * h)))


def finish_kernel(
    shards,
    rank_hbm,
    gain_hbm,
    points_hbm,
    own_hbm,
    other_hbm,
    out_own_hbm,
    out_other_hbm,
    fc1_own_hbm,
    fc1_other_hbm,
    fc2_own_hbm,
    fc2_other_hbm,
    done_ref,
    whole_hbm,
    rank_ref,
    gain_ref,
    points_ref,
    context_ref,
    out_ref,
    fc1_ref,
    fc2_ref,
    middle_ref,
    normed_ref,
    in_sems,
    sems,
):
    length = context_ref.shape[0]
    half_rows = done_ref.shape[0]
    base = pl.multiple_of(lax.axis_index("mp") * half_rows, half_rows)
    hidden_half = fc2_own_hbm.shape[0]
    half = out_own_hbm.shape[0]
    early = [(rank_hbm, rank_ref), (own_hbm, context_ref.at[:, :half]), (other_hbm, context_ref.at[:, half:])]
    later = [
        (gain_hbm, gain_ref),
        (points_hbm.at[pl.ds(base, half_rows)], points_ref),
        (out_own_hbm, out_ref.at[:half]),
        (out_other_hbm, out_ref.at[half:]),
    ]
    last = [
        (fc1_own_hbm, fc1_ref.at[:, :hidden_half]),
        (fc1_other_hbm, fc1_ref.at[:, hidden_half:]),
        (fc2_own_hbm, fc2_ref.at[:hidden_half]),
        (fc2_other_hbm, fc2_ref.at[hidden_half:]),
    ]
    copies = [pltpu.make_async_copy(*ends, in_sems.at[k]) for k, ends in enumerate(early + later + last)]
    early, later, last = copies[:3], copies[3:7], copies[7:]
    for copy in copies:
        copy.start()

    blocks = blocks_of(half_rows, TALL)
    for copy in early:
        copy.wait()
    for i, rows in enumerate(blocks):
        start = pl.multiple_of(base + i * TALL, TALL)
        context = unorder(rank_ref, start, TALL, length, shards, context_ref)
        if i == 0:
            for copy in later:
                copy.wait()
        attn_out = dot(context, out_ref[...])
        middle = (points_ref[rows, :].astype(f32) + attn_out.astype(bf16).astype(f32)).astype(bf16)
        middle_ref[rows, :] = middle
        normed_ref[rows, :] = normalise(middle.astype(f32), gain_ref[...]) * 0.5
    for copy in last:
        copy.wait()

    def away(i):
        here = pl.ds(pl.multiple_of(i * TALL, TALL), TALL)
        there = pl.ds(pl.multiple_of(base + i * TALL, TALL), TALL)
        return pltpu.make_async_copy(done_ref.at[here], whole_hbm.at[there], sems.at[i])

    chunks = blocks_of(2 * hidden_half, TALL)

    def mlp(i, carry):
        here = pl.ds(pl.multiple_of(i * TALL, TALL), TALL)
        normed = normed_ref[here, :]
        total = middle_ref[here, :].astype(f32)
        half_hidden = dot(normed, fc1_ref[:, chunks[0]])
        for k, chunk in enumerate(chunks):
            ahead = dot(normed, fc1_ref[:, chunks[k + 1]]) if k + 1 < len(chunks) else None
            total = total + dot(gelu_of_half(half_hidden).astype(bf16), fc2_ref[chunk, :])
            half_hidden = ahead
        done_ref[here, :] = total.astype(bf16)
        away(i).start()
        return carry

    lax.fori_loop(0, half_rows // TALL, mlp, 0)
    for i in range(half_rows // TALL):
        away(i).wait()


def finish(shards, rank_row, gain_row, points, *arrays):
    length, features = points.shape
    half_rows = length // 2
    hidden = 2 * arrays[-1].shape[0]
    return pl.pallas_call(
        functools.partial(finish_kernel, shards),
        out_shape=(
            jax.ShapeDtypeStruct((half_rows, features), bf16),
            jax.ShapeDtypeStruct((length, features), bf16),
        ),
        in_specs=[ANYWHERE] * 11,
        out_specs=(pl.BlockSpec(memory_space=pltpu.VMEM), ANYWHERE),
        scratch_shapes=[
            pltpu.VMEM((1, length), jnp.int32),
            pltpu.VMEM((1, features), f32),
            pltpu.VMEM((half_rows, features), bf16),
            pltpu.VMEM((length, features), bf16),
            pltpu.VMEM((features, features), bf16),
            pltpu.VMEM((features, hidden), bf16),
            pltpu.VMEM((hidden, features), bf16),
            pltpu.VMEM((half_rows, features), bf16),
            pltpu.VMEM((half_rows, features), bf16),
            pltpu.SemaphoreType.DMA((11,)),
            pltpu.SemaphoreType.DMA((half_rows // TALL,)),
        ],
        compiler_params=params(),
        cost_estimate=pl.CostEstimate(
            flops=2 * half_rows * features * (length + 9 * features),
            bytes_accessed=16 * length * features,
            transcendentals=half_rows * 4 * features,
        ),
    )(rank_row, gain_row, points, *arrays)


def across(values):
    return lax.ppermute(values, "mp", [(0, 1), (1, 0)])


def exchange(rows, shards):
    length, columns = rows.shape
    cells = rows.reshape(shards, length // shards, columns)
    return lax.all_to_all(cells, "space", split_axis=0, concat_axis=0, tiled=True).reshape(length, columns)


def body(points, curve_rank, patch_counts, norm_gain_attn, w_qkv, w_out, norm_gain_mlp, w_fc1, w_fc2):
    shards = lax.axis_size("space")
    length, features = points.shape
    rank_row = curve_rank.reshape(1, length)
    own = exchange(order_for_owners(shards, rank_row, norm_gain_attn.reshape(1, features), points), shards)
    swapped = across(w_fc1), across(w_fc2), across(w_out)
    other = across(own)
    context = attend(patch_counts, own, other, w_qkv)
    context, (other_fc1, other_fc2, other_out) = lax.optimization_barrier((context, swapped))
    returned = exchange(context, shards)
    done, whole = finish(
        shards,
        rank_row,
        norm_gain_mlp.reshape(1, features),
        points,
        returned,
        across(returned),
        w_out,
        other_out,
        w_fc1,
        other_fc1,
        w_fc2,
        other_fc2,
    )
    start = (1 - lax.axis_index("mp")) * (length // 2)
    return lax.dynamic_update_slice(whole, across(done), (start, 0))


def solution(mesh):
    placed = (
        P("space", None),
        P("space"),
        P("space", None),
        P(),
        P(None, None, "mp"),
        P("mp", None),
        P(),
        P(None, "mp"),
        P("mp", None),
    )
    return jax.shard_map(
        body, mesh=mesh, in_specs=placed, out_specs=P("space", None), check_vma=False
    )
```

```python
import functools
import math

import jax
import jax.numpy as jnp
from jax import lax
from jax.experimental import pallas as pl
from jax.experimental.pallas import tpu as pltpu
from jax.sharding import PartitionSpec as P

HDIM = 64
LANES = 128
ROWS = 256
TALL = 512
KEYS = 128
PADDED = HDIM + 16
EPSILON = 1e-06
FAR = 1e30
VMEM_BYTES = 58 * 1024 * 1024
SMALL_BYTES = 30 * 1024 * 1024

f32 = jnp.float32
bf16 = jnp.bfloat16

ANYWHERE = pl.BlockSpec(memory_space=pl.ANY)
SCALARS = pl.BlockSpec(memory_space=pltpu.SMEM)


def normalise(values, gain_row):
    average = jnp.mean(values, axis=-1, keepdims=True)
    centred = values - average
    second = jnp.mean(centred * centred, axis=-1, keepdims=True)
    return (centred * lax.rsqrt(second + EPSILON) * gain_row).astype(bf16)


def dot(left, right):
    return jnp.dot(left, right, preferred_element_type=f32)


def split(number, size):
    if size & (size - 1) == 0:
        return number >> (size.bit_length() - 1), number & (size - 1)
    return number // size, number % size


def slots(rank, length, shards):
    cell = length // shards
    owner, within = split(rank, length)
    return owner * cell + within - lax.axis_index("space") * cell


def one_hot(rows_at, columns_at):
    if columns_at.shape[1] <= 1 << 15:
        rows_at, columns_at = rows_at.astype(jnp.int16), columns_at.astype(jnp.int16)
    one, nil = jnp.ones((), bf16), jnp.zeros((), bf16)
    return jnp.concatenate(
        [
            jnp.where(rows_at == columns_at[:, k : k + LANES], one, nil)
            for k in range(0, columns_at.shape[1], LANES)
        ],
        axis=1,
    )


def blocks_of(length, rows=ROWS):
    return [slice(i * rows, (i + 1) * rows) for i in range(length // rows)]


def params(limit=VMEM_BYTES):
    return pltpu.CompilerParams(vmem_limit_bytes=limit)


def send_kernel(shards, rank_hbm, gain_hbm, points_hbm, out_ref, rank_ref, gain_ref, points_ref, half_ref, small, large):
    length, features = points_ref.shape
    half = features // 2
    core = lax.axis_index("mp")
    gain_copy = pltpu.make_async_copy(gain_hbm, gain_ref, small.at[0])
    rank_copy = pltpu.make_async_copy(rank_hbm, rank_ref, small.at[1])
    rows_of = blocks_of(length)
    copies = [
        pltpu.make_async_copy(points_hbm.at[rows], points_ref.at[rows], large.at[i])
        for i, rows in enumerate(rows_of)
    ]
    gain_copy.start()
    for copy in copies:
        copy.start()
    rank_copy.start()
    gain_copy.wait()
    for copy, rows in zip(copies, rows_of):
        copy.wait()
        normed = normalise(points_ref[rows, :].astype(f32), gain_ref[...])
        half_ref[rows, :] = jnp.where(core == 0, normed[:, :half], normed[:, half:])
    rank_copy.wait()
    slot = slots(rank_ref[...], length, shards)

    place = lax.broadcasted_iota(jnp.int32, (TALL, LANES), 0)
    for i, rows in enumerate(blocks_of(length, TALL)):
        out_ref[rows, :] = dot(one_hot(place + i * TALL, slot), half_ref[...]).astype(bf16)


def order_for_owners(shards, rank_row, gain_row, points):
    length, features = points.shape
    return pl.pallas_call(
        functools.partial(send_kernel, shards),
        out_shape=jax.ShapeDtypeStruct((length, features // 2), bf16),
        in_specs=[ANYWHERE] * 3,
        out_specs=pl.BlockSpec(memory_space=pltpu.VMEM),
        scratch_shapes=[
            pltpu.VMEM((1, length), jnp.int32),
            pltpu.VMEM((1, features), f32),
            pltpu.VMEM((length, features), bf16),
            pltpu.VMEM((length, features // 2), bf16),
            pltpu.SemaphoreType.DMA((2,)),
            pltpu.SemaphoreType.DMA((length // ROWS,)),
        ],
        compiler_params=params(),
        cost_estimate=pl.CostEstimate(
            flops=length * length * features, bytes_accessed=4 * length * features, transcendentals=0
        ),
    )(rank_row, gain_row, points)


def attend_kernel(
    counts_ref, own_ref, other_ref, weight_hbm, out_hbm, w_ref, q_ref, k_ref, v_ref, out_ref, w_sems, out_sems
):
    length, half = own_ref.shape
    tiles = counts_ref.shape[1]
    pairs = out_ref.shape[0]
    core = lax.axis_index("mp")
    scale = math.log2(math.e) / math.sqrt(HDIM)

    copies = [
        pltpu.make_async_copy(
            weight_hbm.at[j, pl.ds(pl.multiple_of(at * half, half), half)],
            w_ref.at[k * half : (k + 1) * half, j * pairs * LANES : (j + 1) * pairs * LANES],
            w_sems.at[2 * j + k],
        )
        for j in range(3)
        for k, at in enumerate((core, 1 - core))
    ]
    for copy in copies:
        copy.start()

    starts = [jnp.int32(0)]
    for t in range(tiles):
        starts.append(starts[-1] + counts_ref[0, t])
    lane = lax.broadcasted_iota(jnp.int32, (1, LANES), 1)
    first = jnp.full((1, LANES), length, jnp.int32)
    last = jnp.zeros((1, LANES), jnp.int32)
    for t in range(tiles):
        first = jnp.where(lane == HDIM + t, starts[t], first)
        last = jnp.where(lane == HDIM + t, starts[t + 1], last)
    flags = jnp.logical_and(lane >= HDIM, lane < HDIM + tiles)
    low_lanes = lane < HDIM
    v_ref[:, HDIM:, :] = jnp.ones((2 * pairs, PADDED - HDIM, length), bf16)
    for copy in copies:
        copy.wait()

    for i, rows in enumerate(blocks_of(length, TALL)):
        spread = dot(own_ref[rows, :], w_ref[:half, :]) + dot(other_ref[rows, :], w_ref[half:, :])
        place = lax.broadcasted_iota(jnp.int32, (TALL, LANES), 0) + i * TALL
        inside = jnp.logical_and(place >= first, place < last)
        q_flag = jnp.where(inside, 1.0, 0.0)
        k_flag = jnp.where(jnp.logical_and(flags, jnp.logical_not(inside)), -FAR, 0.0)
        for pair in range(pairs):
            q, k, v = (spread[:, (j * pairs + pair) * LANES : (j * pairs + pair + 1) * LANES] for j in range(3))
            q = q * scale
            q_ref[2 * pair, rows, :] = jnp.where(low_lanes, q, q_flag).astype(bf16)
            q_ref[2 * pair + 1, rows, :] = jnp.where(low_lanes, pltpu.roll(q, HDIM, 1), q_flag).astype(bf16)
            k_ref[2 * pair, rows, :] = jnp.where(low_lanes, k, k_flag).astype(bf16)
            k_ref[2 * pair + 1, rows, :] = jnp.where(low_lanes, pltpu.roll(k, HDIM, 1), k_flag).astype(bf16)
            v = jnp.transpose(v).astype(bf16)
            v_ref[2 * pair, :HDIM, rows] = v[:HDIM]
            v_ref[2 * pair + 1, :HDIM, rows] = v[HDIM:]

    def weigh(scores):
        return jnp.exp2(scores - jnp.max(scores, axis=0, keepdims=True)).astype(bf16)

    def send_out(i, pair):
        rows = pl.ds(pl.multiple_of(i * TALL, TALL), TALL)
        return pltpu.make_async_copy(
            out_ref.at[pair, rows], out_hbm.at[rows, pair * LANES : (pair + 1) * LANES], out_sems.at[i, pair]
        )

    def query_block(i, carry):
        begin = i * TALL
        rows = pl.ds(pl.multiple_of(begin, TALL), TALL)
        low, high = jnp.int32(0), jnp.int32(length)
        for t in range(tiles):
            low = jnp.where(starts[t] <= begin, starts[t], low)
            end = starts[tiles - t]
            high = jnp.where(end >= begin + TALL, end, high)
        low = (low // LANES) * LANES
        blocks = (high - low + KEYS - 1) // KEYS
        for n in range(TALL // KEYS, length // KEYS + 1):

            @pl.when(blocks == n)
            def _(n=n):
                start = pl.multiple_of(jnp.minimum(low, length - n * KEYS), LANES)
                keys = pl.ds(start, n * KEYS)

                def score(h):
                    return lax.dot_general(
                        k_ref[h, keys, :], q_ref[h, rows, :], (((1,), (1,)), ((), ())), preferred_element_type=f32
                    )

                ahead, sums = score(0), []
                for h in range(2 * pairs):
                    scores = ahead
                    ahead = score(h + 1) if h + 1 < 2 * pairs else None
                    sums.append(dot(v_ref[h, :, keys], weigh(scores)))
                for pair in range(pairs):
                    value = jnp.concatenate(
                        [both[:HDIM] / both[HDIM : HDIM + 1] for both in sums[2 * pair : 2 * pair + 2]], axis=0
                    )
                    out_ref[pair, rows, :] = jnp.transpose(value).astype(bf16)

        for pair in range(pairs):
            send_out(i, pair).start()
        return carry

    lax.fori_loop(0, length // TALL, query_block, 0)
    for i in range(length // TALL):
        for pair in range(pairs):
            send_out(i, pair).wait()


def attend(counts, own, other, w_qkv):
    length, half = own.shape
    features, columns = w_qkv.shape[1:]
    heads = columns // HDIM
    held = pl.BlockSpec(memory_space=pltpu.VMEM)
    return pl.pallas_call(
        attend_kernel,
        out_shape=jax.ShapeDtypeStruct((length, columns), bf16),
        in_specs=[SCALARS, held, held, ANYWHERE],
        out_specs=ANYWHERE,
        scratch_shapes=[
            pltpu.VMEM((features, 3 * columns), bf16),
            pltpu.VMEM((heads, length, LANES), bf16),
            pltpu.VMEM((heads, length, LANES), bf16),
            pltpu.VMEM((heads, PADDED, length), bf16),
            pltpu.VMEM((heads // 2, length, LANES), bf16),
            pltpu.SemaphoreType.DMA((6,)),
            pltpu.SemaphoreType.DMA((length // TALL, heads // 2)),
        ],
        compiler_params=params(SMALL_BYTES),
        cost_estimate=pl.CostEstimate(
            flops=64 * length * length * HDIM, bytes_accessed=8 * length * half, transcendentals=4 * length * length
        ),
    )(counts, own, other, w_qkv)


def unorder(rank_ref, start, rows, length, shards, context_ref):
    slot = slots(rank_ref[:, pl.ds(start, rows)], length, shards)
    slot = jnp.transpose(jnp.broadcast_to(slot, (LANES, rows)))
    place = lax.broadcasted_iota(jnp.int32, (1, length), 1)
    return dot(one_hot(slot, place), context_ref[...]).astype(bf16)


def gelu_of_half(h):
    inner = 2 * math.sqrt(2 / math.pi)
    return h + h * jnp.tanh(h * (inner + (4 * 0.044715 * inner) * (h * h)))


def finish_kernel(
    shards,
    rank_hbm,
    gain_hbm,
    points_hbm,
    own_hbm,
    other_hbm,
    out_own_hbm,
    out_other_hbm,
    fc1_own_hbm,
    fc1_other_hbm,
    fc2_own_hbm,
    fc2_other_hbm,
    done_ref,
    whole_hbm,
    rank_ref,
    gain_ref,
    points_ref,
    context_ref,
    out_ref,
    fc1_ref,
    fc2_ref,
    middle_ref,
    normed_ref,
    in_sems,
    sems,
):
    length = context_ref.shape[0]
    half_rows = done_ref.shape[0]
    base = pl.multiple_of(lax.axis_index("mp") * half_rows, half_rows)
    hidden_half = fc2_own_hbm.shape[0]
    half = out_own_hbm.shape[0]
    early = [(rank_hbm, rank_ref), (own_hbm, context_ref.at[:, :half]), (other_hbm, context_ref.at[:, half:])]
    later = [
        (gain_hbm, gain_ref),
        (points_hbm.at[pl.ds(base, half_rows)], points_ref),
        (out_own_hbm, out_ref.at[:half]),
        (out_other_hbm, out_ref.at[half:]),
    ]
    last = [
        (fc1_own_hbm, fc1_ref.at[:, :hidden_half]),
        (fc1_other_hbm, fc1_ref.at[:, hidden_half:]),
        (fc2_own_hbm, fc2_ref.at[:hidden_half]),
        (fc2_other_hbm, fc2_ref.at[hidden_half:]),
    ]
    copies = [pltpu.make_async_copy(*ends, in_sems.at[k]) for k, ends in enumerate(early + later + last)]
    early, later, last = copies[:3], copies[3:7], copies[7:]
    for copy in copies:
        copy.start()

    blocks = blocks_of(half_rows, TALL)
    for copy in early:
        copy.wait()
    for i, rows in enumerate(blocks):
        start = pl.multiple_of(base + i * TALL, TALL)
        context = unorder(rank_ref, start, TALL, length, shards, context_ref)
        if i == 0:
            for copy in later:
                copy.wait()
        attn_out = dot(context, out_ref[...])
        middle = (points_ref[rows, :].astype(f32) + attn_out.astype(bf16).astype(f32)).astype(bf16)
        middle_ref[rows, :] = middle
        normed_ref[rows, :] = normalise(middle.astype(f32), gain_ref[...]) * 0.5
    for copy in last:
        copy.wait()

    def away(i):
        here = pl.ds(pl.multiple_of(i * TALL, TALL), TALL)
        there = pl.ds(pl.multiple_of(base + i * TALL, TALL), TALL)
        return pltpu.make_async_copy(done_ref.at[here], whole_hbm.at[there], sems.at[i])

    chunks = blocks_of(2 * hidden_half, TALL)

    def mlp(i, carry):
        here = pl.ds(pl.multiple_of(i * TALL, TALL), TALL)
        normed = normed_ref[here, :]
        total = middle_ref[here, :].astype(f32)
        half_hidden = dot(normed, fc1_ref[:, chunks[0]])
        for k, chunk in enumerate(chunks):
            ahead = dot(normed, fc1_ref[:, chunks[k + 1]]) if k + 1 < len(chunks) else None
            total = total + dot(gelu_of_half(half_hidden).astype(bf16), fc2_ref[chunk, :])
            half_hidden = ahead
        done_ref[here, :] = total.astype(bf16)
        away(i).start()
        return carry

    lax.fori_loop(0, half_rows // TALL, mlp, 0)
    for i in range(half_rows // TALL):
        away(i).wait()


def finish(shards, rank_row, gain_row, points, *arrays):
    length, features = points.shape
    half_rows = length // 2
    hidden = 2 * arrays[-1].shape[0]
    return pl.pallas_call(
        functools.partial(finish_kernel, shards),
        out_shape=(
            jax.ShapeDtypeStruct((half_rows, features), bf16),
            jax.ShapeDtypeStruct((length, features), bf16),
        ),
        in_specs=[ANYWHERE] * 11,
        out_specs=(pl.BlockSpec(memory_space=pltpu.VMEM), ANYWHERE),
        scratch_shapes=[
            pltpu.VMEM((1, length), jnp.int32),
            pltpu.VMEM((1, features), f32),
            pltpu.VMEM((half_rows, features), bf16),
            pltpu.VMEM((length, features), bf16),
            pltpu.VMEM((features, features), bf16),
            pltpu.VMEM((features, hidden), bf16),
            pltpu.VMEM((hidden, features), bf16),
            pltpu.VMEM((half_rows, features), bf16),
            pltpu.VMEM((half_rows, features), bf16),
            pltpu.SemaphoreType.DMA((11,)),
            pltpu.SemaphoreType.DMA((half_rows // TALL,)),
        ],
        compiler_params=params(),
        cost_estimate=pl.CostEstimate(
            flops=2 * half_rows * features * (length + 9 * features),
            bytes_accessed=16 * length * features,
            transcendentals=half_rows * 4 * features,
        ),
    )(rank_row, gain_row, points, *arrays)


def across(values):
    return lax.ppermute(values, "mp", [(0, 1), (1, 0)])


def exchange(rows, shards):
    length, columns = rows.shape
    cells = rows.reshape(shards, length // shards, columns)
    return lax.all_to_all(cells, "space", split_axis=0, concat_axis=0, tiled=True).reshape(length, columns)


def body(points, curve_rank, patch_counts, norm_gain_attn, w_qkv, w_out, norm_gain_mlp, w_fc1, w_fc2):
    shards = lax.axis_size("space")
    length, features = points.shape
    rank_row = curve_rank.reshape(1, length)
    own = exchange(order_for_owners(shards, rank_row, norm_gain_attn.reshape(1, features), points), shards)
    swapped = across(w_fc1), across(w_fc2), across(w_out)
    other = across(own)
    context = attend(patch_counts, own, other, w_qkv)
    context, (other_fc1, other_fc2, other_out) = lax.optimization_barrier((context, swapped))
    returned = exchange(context, shards)
    done, whole = finish(
        shards,
        rank_row,
        norm_gain_mlp.reshape(1, features),
        points,
        returned,
        across(returned),
        w_out,
        other_out,
        w_fc1,
        other_fc1,
        w_fc2,
        other_fc2,
    )
    start = (1 - lax.axis_index("mp")) * (length // 2)
    return lax.dynamic_update_slice(whole, across(done), (start, 0))


def solution(mesh):
    placed = (
        P("space", None),
        P("space"),
        P("space", None),
        P(),
        P(None, None, "mp"),
        P("mp", None),
        P(),
        P(None, "mp"),
        P("mp", None),
    )
    return jax.shard_map(
        body, mesh=mesh, in_specs=placed, out_specs=P("space", None), check_vma=False
    )
```
